32 devices in a mesh: groups: 1, wide: 16 (over z, y, core), mp: 2 (over x), sub: 1.
Axes of the slice: x: 2, y: 2, z: 4, core: 2. Of those that a mesh axis runs over, the one named last changes fastest.
Arguments:
- gate_activation: bfloat16 [512, 28672], P(('groups', 'wide'), ('mp', 'sub')), may hold values from -6 to 6
- up_activation: bfloat16 [512, 28672], P(('groups', 'wide'), ('mp', 'sub')), may hold values from -6 to 6
- down_base_weight: bfloat16 [28672, 8192], P(('mp', 'sub'), 'wide'), may hold values from -0.03125 to 0.03125
- first_factor_table: bfloat16 [16, 64, 28672], P('wide', None, ('mp', 'sub')), may hold values from -0.03125 to 0.03125
- second_factor_table: bfloat16 [16, 64, 8192], P(None, ('mp', 'sub'), 'wide'), may hold values from -0.75 to 0.75
- row_adapter_index: int32 [512, 1], P('groups'), may hold values from 0 to 15; in each aligned block of 32 rows (0 to 31, 32 to 63, ...) at most 2 rows name the same one
- adapter_storage_slot: int32 [16], replicated, may hold values from 0 to 15, each once
Outputs:
- mixed: bfloat16 [512, 8192], P(('groups', 'mp', 'sub'), 'wide')
The draws below stay inside these ranges and needn't reach their ends.
Inputs may be any that keep to these rules, and one draw needn't show every extreme that they name: `row_adapter_index`: in each aligned block of 32 rows no adapter is named by more than 2 rows; every adapter is named somewhere. `adapter_storage_slot`: each slot once.
All inputs are finite; a program needn't handle non-finite values.
Results may differ from the reference program's by a relative error of at most 0.0055.
Values may be sent and summed in bfloat16 or wider, within the bound.
No kernel may reach another device: no remote copies, remote signals or barrier semaphores. Data moves between devices by JAX's collectives and lax.ppermute only.
A program may use at most 64 MiB of HBM per device.

```python
import math
import jax
import jax.numpy as jnp
import numpy as np
from jax import lax

MODEL_WIDTH = 8192
HIDDEN_UNITS = 28672
ADAPTER_RANK = 64
ROW_DEV = 32
MOST = 2
ROWS = 512
BATCH_ADAPTERS = 16


def block_scale(own_key, dims, split, smallest, top_value):
    factor_of = 1.0
    for position, parts in split:
        steps = jax.random.uniform(jax.random.fold_in(jax.random.fold_in(own_key, 6), position), (parts,), jnp.float32, smallest / len(split), top_value / len(split))
        factor_of = factor_of * jnp.repeat(jnp.exp(steps), dims[position] // parts).reshape((-1,) + (1,) * (len(dims) - 1 - position))
    return factor_of


def shared_out(rng, own, number, rows, amount, top, reach, skew):
    sequence = jax.random.permutation(rng, amount)
    crowded, ordinary = load_shares(amount, rows * top, reach, skew, True), load_shares(amount, rows * top, reach, skew, False)
    places = jnp.arange(amount)

    def named(lengths, rotation):
        used = int((lengths > 0).sum())
        fixed = max(1, used // 4)
        moved = fixed + (places - fixed + rotation * (used - fixed)) % max(1, amount - fixed)
        return jnp.zeros((amount,), jnp.int32).at[sequence[jnp.where(places < fixed, places, moved)]].set(jnp.asarray(lengths, jnp.int32))

    lengths = jnp.where(number % 4 == 0, named(crowded, number // 4), named(ordinary, number - number // 4 - 1))
    mixed = jax.random.permutation(jax.random.fold_in(own, 3), amount)
    donor, receiver = mixed[0:amount // 2 * 2:2], mixed[1:amount // 2 * 2:2]
    room = jnp.minimum(lengths[donor] - 1, reach - lengths[receiver]) // 2
    room = jnp.where((donor == sequence[0]) | (receiver == sequence[0]) | (lengths[receiver] == 0), 0, jnp.maximum(room, 0))
    moved = jax.random.randint(jax.random.fold_in(own, 4), (amount // 2,), 0, 1 << 20) % (room + 1)
    lengths = lengths.at[donor].add(-moved).at[receiver].add(moved)
    members = jnp.searchsorted(jnp.cumsum(lengths), jnp.arange(rows * top), side="right").astype(jnp.int32)
    listing = members.reshape(top, rows).T
    listing = listing[jax.random.permutation(jax.random.fold_in(own, 1), rows)]
    rotation = jax.random.randint(jax.random.fold_in(own, 2), (rows, 1), 0, top)
    return jnp.take_along_axis(listing, (jnp.arange(top)[None, :] + rotation) % top, axis=1)


def load_shares(count, total, bound, slope, full):
    portions = [(1 << 20) // math.isqrt(grade ** slope) + 1 for grade in range(1, count + 1)]
    largest = bound if full else min(bound, max(-(-total // count), total * portions[0] // sum(portions)))
    least = 1 if total - largest >= count - 1 else 0
    given, surplus = [largest] + [least] * (count - 1), total - largest - least * (count - 1)
    while surplus > 0:
        free = [i for i in range(1, count) if given[i] < largest] or [i for i in range(1, count) if given[i] < bound]
        mass, remaining = sum([portions[i] for i in free]), surplus
        for i in free:
            more = min(bound - given[i], max(1, remaining * portions[i] // mass), surplus)
            given[i] = given[i] + more
            surplus = surplus - more
    return np.array(given)


def normal_values(key, extent, width, limit, split=(), held_as=jnp.bfloat16):
    values = width * jax.random.normal(key, extent, jnp.float32)
    if split:
        values = values * block_scale(key, extent, split, -0.22, 0.18)
    return jnp.clip(values, -limit, limit).astype(held_as)


def setup_inputs(seed: int = 0, part: int = 0) -> dict:
    seeds = jax.random.split(jax.random.key(seed), 8)
    part_splits = jax.random.split(jax.random.fold_in(seeds[7], part), 8)
    gate_activation = normal_values(part_splits[0], (ROWS, HIDDEN_UNITS), 1.0, 6.0, ((0, 16), (1, 2)))
    up_activation = normal_values(part_splits[1], (ROWS, HIDDEN_UNITS), 1.0, 6.0, ((0, 16), (1, 2)))
    down_base_weight = normal_values(seeds[2], (HIDDEN_UNITS, MODEL_WIDTH), HIDDEN_UNITS ** -0.5, 0.03125, ((0, 2), (1, 16)))
    first_factor_table = normal_values(seeds[3], (BATCH_ADAPTERS, ADAPTER_RANK, HIDDEN_UNITS), HIDDEN_UNITS ** -0.5, 0.03125, ((0, 16), (2, 2)))
    second_factor_table = normal_values(seeds[4], (BATCH_ADAPTERS, ADAPTER_RANK, MODEL_WIDTH), ADAPTER_RANK ** -0.5, 0.75, ((1, 2), (2, 16)))
    row_adapter_index_keys = jax.random.split(jax.random.fold_in(part_splits[5], 1), ROWS // ROW_DEV)
    row_adapter_index_turns = jax.random.permutation(jax.random.fold_in(part_splits[5], 3), ROWS // ROW_DEV)
    row_adapter_index = jax.vmap(lambda own, number: shared_out(jax.random.fold_in(part_splits[5], 2), own, number, ROW_DEV, BATCH_ADAPTERS, 1, MOST, 2))(row_adapter_index_keys, row_adapter_index_turns).reshape((ROWS, 1))
    adapter_storage_slot = jax.random.permutation(seeds[6], BATCH_ADAPTERS).astype(jnp.int32)
    return {"gate_activation": gate_activation, "up_activation": up_activation, "down_base_weight": down_base_weight, "first_factor_table": first_factor_table, "second_factor_table": second_factor_table, "row_adapter_index": row_adapter_index, "adapter_storage_slot": adapter_storage_slot}


def reference(gate_activation, up_activation, down_base_weight, first_factor_table, second_factor_table, row_adapter_index, adapter_storage_slot):
    hidden = (jax.nn.silu(gate_activation.astype(jnp.float32)) * up_activation.astype(jnp.float32)).astype(jnp.bfloat16)
    base = jnp.dot(hidden, down_base_weight, preferred_element_type=jnp.float32)
    slots = adapter_storage_slot[row_adapter_index[:, 0].astype(jnp.int32)].astype(jnp.int32)

    def one_row(item):
        row, storage_position = item
        first_factor = lax.dynamic_index_in_dim(first_factor_table, storage_position, 0, keepdims=False)
        low = jnp.dot(first_factor, row, preferred_element_type=jnp.float32).astype(jnp.bfloat16)
        second_factor = lax.dynamic_index_in_dim(second_factor_table, storage_position, 0, keepdims=False)
        return jnp.dot(low, second_factor, preferred_element_type=jnp.float32)

    delta = lax.map(one_row, (hidden, slots))
    return (base + delta).astype(jnp.bfloat16)
```

```python
import functools

import jax
import jax.numpy as jnp
from jax import lax
from jax.experimental import pallas as pl
from jax.experimental.pallas import tpu as pltpu
from jax.sharding import PartitionSpec as P

MOST = 2
CHUNKS = 2
INNER = ("mp", "sub")


def tile_of(depth, most=1792):
    parts = 1
    while depth % parts or (depth // parts) % 128 or depth // parts > most:
        parts += 1
    return depth // parts


def rows_kernel(per_chunk, tiles, *refs):
    count = CHUNKS * per_chunk
    pieces, (weight, first, base, low) = refs[:count], refs[count:]
    step = pl.program_id(0)

    @pl.when(step == 0)
    def _():
        base[...] = jnp.zeros_like(base)
        low[...] = jnp.zeros_like(low)

    for chunk in range(CHUNKS):

        @pl.when(step // tiles == chunk)
        def _():
            held = pieces[chunk * per_chunk : (chunk + 1) * per_chunk]
            rows = jnp.concatenate([piece[...] for piece in held], axis=0)
            base[...] += jnp.dot(rows, weight[...], preferred_element_type=jnp.float32)
            low[...] += lax.dot_general(
                rows, first[...], (((1,), (1,)), ((), ())), preferred_element_type=jnp.float32
            )


def rows_product(pieces, weight, first):
    per_chunk = len(pieces[0])
    row_count, depth = pieces[0][0].shape
    tile = tile_of(depth)
    tiles = depth // tile
    total = per_chunk * row_count
    width, rank = weight.shape[1], first.shape[0]
    specs = []
    for chunk in range(CHUNKS):
        for _ in range(per_chunk):
            specs.append(
                pl.BlockSpec(
                    (row_count, tile),
                    lambda i, chunk=chunk: (0, jnp.clip(i - chunk * tiles, 0, tiles - 1)),
                )
            )
    specs.append(pl.BlockSpec((tile, width), lambda i: (i, 0)))
    specs.append(pl.BlockSpec((rank, tile), lambda i: (0, i)))
    return pl.pallas_call(
        functools.partial(rows_kernel, per_chunk, tiles),
        grid=(CHUNKS * tiles,),
        in_specs=specs,
        out_specs=[
            pl.BlockSpec((total, width), lambda i: (0, 0)),
            pl.BlockSpec((total, rank), lambda i: (0, 0)),
        ],
        out_shape=[
            jax.ShapeDtypeStruct((total, width), jnp.float32),
            jax.ShapeDtypeStruct((total, rank), jnp.float32),
        ],
        compiler_params=pltpu.CompilerParams(vmem_limit_bytes=24 * 2**20),
        cost_estimate=pl.CostEstimate(
            flops=2 * total * depth * CHUNKS * (width + rank),
            bytes_accessed=2 * depth * CHUNKS * (width + rank + total),
            transcendentals=0,
        ),
    )(*pieces[0], *pieces[1], weight, first)


def ring_order(nodes, lanes):
    if lanes == 1:
        return list(range(nodes))
    return list(range(0, nodes, 2)) + list(range(nodes - 1, 0, -2))


def on_device(
    gate_activation,
    up_activation,
    down_base_weight,
    first_factor_table,
    second_factor_table,
    row_adapter_index,
    adapter_storage_slot,
):
    f32, bf16 = jnp.float32, jnp.bfloat16
    row_count, width_part = gate_activation.shape
    owners = lax.axis_size("wide")
    inner = lax.axis_size(INNER)
    slots = first_factor_table.shape[0] * owners
    lanes = 2 if lax.axis_size("sub") == 1 and owners % 4 == 0 else 1
    nodes = owners // lanes
    order = ring_order(nodes, lanes)
    place = [order.index(node) for node in range(nodes)]
    steps = (nodes - 1) // 2
    far = nodes // 2

    home = lax.axis_index("wide")
    lane = home % lanes
    my_place = jnp.asarray(place, jnp.int32)[home // lanes]
    part = lax.axis_index(INNER)

    def moved(shift, cross=False):
        return [
            (order[p] * lanes + c, order[(p + shift) % nodes] * lanes + (c ^ int(cross)))
            for p in range(nodes)
            for c in range(lanes)
        ]

    def node_at(shift):
        return jnp.asarray(order, jnp.int32)[(my_place + shift) % nodes]

    def sibling(piece):
        return lax.ppermute(piece, "wide", moved(0, True))

    def both(piece):
        return [piece, sibling(piece)] if lanes == 2 else [piece]

    ids = row_adapter_index[:, 0]
    names = jnp.arange(slots, dtype=jnp.int32)
    slot_all = jnp.sum(
        jnp.where(ids[:, None] == names[None, :], adapter_storage_slot[None, :], 0), axis=1
    ).reshape(owners, row_count)
    ranks = jnp.arange(row_count, dtype=jnp.int32)
    earlier = (slot_all[:, :, None] == slot_all[:, None, :]) & (ranks[None, :] < ranks[:, None])[None]
    position = jnp.sum(earlier.astype(jnp.int32), axis=2)

    depth = width_part // CHUNKS
    hidden = []
    for chunk in range(CHUNKS):
        gate = gate_activation[:, chunk * depth : (chunk + 1) * depth].astype(f32)
        up = up_activation[:, chunk * depth : (chunk + 1) * depth].astype(f32)
        hidden.append((jax.nn.silu(gate) * up).astype(bf16))

    first = first_factor_table[0]

    my_slot = lax.dynamic_index_in_dim(slot_all, home, 0, keepdims=False)
    my_position = lax.dynamic_index_in_dim(position, home, 0, keepdims=False)
    far_rows = []
    for cross in range(lanes):
        target = node_at(far) * lanes + (lane ^ cross)
        pick = (my_slot[None, :] == target) & (my_position[None, :] == jnp.arange(MOST)[:, None])
        sent = jnp.concatenate(
            [
                jnp.dot(pick.astype(bf16), block, preferred_element_type=f32).astype(bf16)
                for block in hidden
            ],
            axis=1,
        )
        far_rows.append(lax.ppermute(sent, "wide", moved(far, bool(cross))))

    right, left = list(hidden), list(hidden)
    groups = [(0, [both(block) for block in hidden])]
    for step in range(1, steps + 1):
        right = [lax.ppermute(block, "wide", moved(1)) for block in right]
        left = [lax.ppermute(block, "wide", moved(-1)) for block in left]
        groups.append((step, [both(r) + both(l) for r, l in zip(right, left)]))
    last = [
        lax.ppermute(right[0], "wide", moved(1)),
        lax.ppermute(left[1], "wide", moved(-1)),
    ]
    groups.append((far, [both(block) for block in last]))

    base, low, where = {}, [], []
    for step, pieces in groups:
        total, lowered = rows_product(pieces, down_base_weight, first)
        total = total.reshape(-1, lanes * row_count, total.shape[1])
        shifts = [step] if step in (0, far) else [-step, step]
        for index, shift in enumerate(shifts):
            base[shift % nodes] = total[index]
        if step != far:
            low.append(lowered)
            for shift in shifts:
                where += [node_at(shift) * lanes + (lane ^ c) for c in range(lanes)]
    far_where = [node_at(far) * lanes + (lane ^ c) for c in range(lanes)]
    low.append(
        lax.dot_general(
            jnp.concatenate(far_rows, axis=0),
            first,
            (((1,), (1,)), ((), ())),
            preferred_element_type=f32,
        )
    )
    low = jnp.concatenate(low, axis=0)

    blocks = jnp.arange(owners, dtype=jnp.int32)
    items = jnp.arange(MOST, dtype=jnp.int32)
    where = jnp.stack(where)
    chosen = (
        (where[None, None, :, None] == blocks[:, None, None, None])
        & (slot_all == home)[:, None, None, :]
        & (position[:, None, None, :] == items[None, :, None, None])
    ).reshape(owners * MOST, -1)
    far_chosen = (
        (jnp.stack(far_where)[None, None, :, None] == blocks[:, None, None, None])
        & (items[:, None] == items[None, :])[None, :, None, :]
    ).reshape(owners * MOST, -1)
    chosen = jnp.concatenate([chosen, far_chosen], axis=1).astype(f32)
    low = jnp.dot(chosen, low, precision=lax.Precision.HIGHEST)

    half = owners * MOST // inner
    if inner == 2:
        kept = jnp.where(part == 0, low[:half], low[half:])
        sent = jnp.where(part == 0, low[half:], low[:half])
        low = kept + lax.ppermute(sent, INNER, [(0, 1), (1, 0)])
    else:
        low = lax.psum_scatter(low, INNER, scatter_dimension=0, tiled=True)
    low = low.astype(bf16)[None]
    if owners & (owners - 1) == 0:
        gap = 1
        while gap < owners:
            other = lax.ppermute(low, "wide", [(w, w ^ gap) for w in range(owners)])
            low = jnp.where(
                home & gap == 0,
                jnp.concatenate([low, other], axis=0),
                jnp.concatenate([other, low], axis=0),
            )
            gap *= 2
    else:
        low = lax.all_gather(low, "wide", axis=0, tiled=True)
    own_blocks = owners // inner
    low = low.reshape(slots, own_blocks, MOST, -1)

    if inner == 2:
        other = lax.ppermute(second_factor_table, INNER, [(0, 1), (1, 0)])
        second = jnp.where(
            part == 0,
            jnp.concatenate([second_factor_table, other], axis=1),
            jnp.concatenate([other, second_factor_table], axis=1),
        )
    else:
        second = lax.all_gather(second_factor_table, INNER, axis=1, tiled=True)
    width = second.shape[2]
    own_slot = lax.dynamic_slice_in_dim(slot_all, part * own_blocks, own_blocks)
    own_position = lax.dynamic_slice_in_dim(position, part * own_blocks, own_blocks)
    spread = 0
    for item in range(MOST):
        mask = (own_slot[:, :, None] == names) & (own_position == item)[:, :, None]
        spread += jnp.where(mask[..., None], jnp.swapaxes(low[:, :, item], 0, 1)[:, None], 0)
    delta = jnp.dot(
        spread.reshape(own_blocks * row_count, -1).astype(bf16),
        second.reshape(-1, width),
        preferred_element_type=f32,
    )

    half_nodes = nodes // inner if nodes % inner == 0 else 0
    opposite = (
        inner == 2
        and nodes % 2 == 0
        and all((order[p] < half_nodes) != (order[(p + far) % nodes] < half_nodes) for p in range(nodes))
    )
    group_rows = lanes * row_count
    if opposite:
        sums, targets = [], []
        for shift in range(far):
            mine = node_at(shift) // half_nodes == part
            kept = jnp.where(mine, base[shift], base[shift + far])
            sent = jnp.where(mine, base[shift + far], base[shift])
            sums.append(kept + lax.ppermute(sent, INNER, [(0, 1), (1, 0)]))
            targets.append(jnp.where(mine, node_at(shift), node_at(shift + far)) % half_nodes)
    else:
        sums = [base[shift] for shift in range(nodes)]
        targets = [node_at(shift) for shift in range(nodes)]
    out = []
    for index in range(len(sums)):
        rows = sums[0]
        for target, value in zip(targets[1:], sums[1:]):
            rows = jnp.where(target == index, value, rows)
        out.append(rows)
    out = jnp.stack(out).reshape(-1, lanes, row_count, width)
    if lanes == 2:
        out = jnp.where(lane == 0, out, out[:, ::-1])
    out = out.reshape(-1, width)
    if not opposite:
        out = lax.psum_scatter(out, INNER, scatter_dimension=0, tiled=True)
    return (out + delta).astype(bf16)


def solution(mesh):
    return jax.shard_map(
        on_device,
        mesh=mesh,
        in_specs=(
            P(("groups", "wide"), ("mp", "sub")),
            P(("groups", "wide"), ("mp", "sub")),
            P(("mp", "sub"), "wide"),
            P("wide", None, ("mp", "sub")),
            P(None, ("mp", "sub"), "wide"),
            P("groups", None),
            P(),
        ),
        out_specs=P(("groups", "mp", "sub"), "wide"),
        check_vma=False,
    )
```

```python
import functools

import jax
import jax.numpy as jnp
import numpy as np
from jax import lax
from jax.experimental import pallas as pl
from jax.experimental.pallas import tpu as pltpu
from jax.sharding import PartitionSpec as P

MOST = 2
INNER = ("mp", "sub")
SWAP = [(0, 1), (1, 0)]


def tile_of(depth, most=1792):
    parts = 1
    while depth % parts or (depth // parts) % 128 or depth // parts > most:
        parts += 1
    return depth // parts


def rows_kernel(count, lane_ref, *refs):
    pieces, rest = refs[:count], refs[count:]
    weight, weight_sib, first, first_sib, mine, sib, low, acc, acc_sib, acc_low = rest
    step = pl.program_id(0)

    @pl.when(step == 0)
    def _():
        acc[...] = jnp.zeros_like(acc)
        acc_sib[...] = jnp.zeros_like(acc_sib)
        acc_low[...] = jnp.zeros_like(acc_low)

    rows = jnp.concatenate([piece[...] for piece in pieces], axis=0)
    factors = jnp.concatenate([first[...], first_sib[...]], axis=0)
    acc[...] += jnp.dot(rows, weight[...], preferred_element_type=jnp.float32)
    acc_sib[...] += jnp.dot(rows, weight_sib[...], preferred_element_type=jnp.float32)
    acc_low[...] += lax.dot_general(
        rows, factors, (((1,), (1,)), ((), ())), preferred_element_type=jnp.float32
    )

    @pl.when(step == pl.num_programs(0) - 1)
    def _():
        height = pieces[0].shape[0]
        for index in range(count):
            lane = jnp.bitwise_xor(lane_ref[0], index % 2)
            block = slice(index * height, (index + 1) * height)
            mine[index // 2, lane] = acc[block, :]
            sib[index // 2, lane] = acc_sib[block, :]
            low[index // 2, lane] = acc_low[block, :]


def rows_product(lane, pieces, weight, weight_sib, first, first_sib):
    count = len(pieces)
    row_count, depth = pieces[0].shape
    tile = tile_of(depth)
    tiles = depth // tile
    width, rank = weight.shape[1], first.shape[0]
    total = count * row_count
    grid_spec = pltpu.PrefetchScalarGridSpec(
        num_scalar_prefetch=1,
        grid=(tiles,),
        in_specs=[pl.BlockSpec((row_count, tile), lambda i, lane: (0, i))] * count
        + [
            pl.BlockSpec((tile, width), lambda i, lane: (lane[0] * tiles + i, 0)),
            pl.BlockSpec((tile, width), lambda i, lane: (i, 0)),
            pl.BlockSpec((rank, tile), lambda i, lane: (0, lane[0] * tiles + i)),
            pl.BlockSpec((rank, tile), lambda i, lane: (0, i)),
        ],
        out_specs=[
            pl.BlockSpec((count // 2, 2, row_count, size), lambda i, lane: (0, 0, 0, 0))
            for size in (width, width, 2 * rank)
        ],
        scratch_shapes=[
            pltpu.VMEM((total, size), jnp.float32) for size in (width, width, 2 * rank)
        ],
    )
    return pl.pallas_call(
        functools.partial(rows_kernel, count),
        grid_spec=grid_spec,
        out_shape=[
            jax.ShapeDtypeStruct((count // 2, 2, row_count, size), jnp.float32)
            for size in (width, width, 2 * rank)
        ],
        compiler_params=pltpu.CompilerParams(vmem_limit_bytes=40 * 2**20),
        cost_estimate=pl.CostEstimate(
            flops=4 * total * depth * (width + rank),
            bytes_accessed=2 * depth * (2 * width + 2 * rank + total),
            transcendentals=0,
        ),
    )(lane, *pieces, weight, weight_sib, first, first_sib)


def hidden_of(gate, up):
    return (jax.nn.silu(gate.astype(jnp.float32)) * up.astype(jnp.float32)).astype(jnp.bfloat16)


def slots_of(row_adapter_index, adapter_storage_slot):
    names = jnp.arange(adapter_storage_slot.shape[0], dtype=jnp.int32)
    same = row_adapter_index == names[None, :]
    return jnp.sum(jnp.where(same, adapter_storage_slot[None, :], 0), axis=1)


def gathered(
    gate_activation,
    up_activation,
    down_base_weight,
    first_factor_table,
    second_factor_table,
    row_adapter_index,
    adapter_storage_slot,
):
    hidden = hidden_of(gate_activation, up_activation)
    row_count = hidden.shape[0]
    owners = lax.axis_size("wide")
    local_adapter = first_factor_table.shape[0]
    slots = local_adapter * owners
    rank_portion = second_factor_table.shape[1]
    home = lax.axis_index("wide")
    slot_all = slots_of(row_adapter_index, adapter_storage_slot)
    blocks = slot_all.reshape(owners, row_count)
    order = jnp.arange(row_count, dtype=jnp.int32)
    earlier = (blocks[:, :, None] == blocks[:, None, :]) & (order[None, :] < order[:, None])
    position = jnp.sum(earlier.astype(jnp.int32), axis=2)
    rows = lax.all_gather(hidden, "wide", axis=0, tiled=True)
    base = jnp.dot(rows, down_base_weight, preferred_element_type=jnp.float32)
    low = jnp.einsum("re,nqe->nrq", rows, first_factor_table, preferred_element_type=jnp.float32)
    low = low.reshape(local_adapter, owners, row_count, low.shape[2])
    own = home * local_adapter + jnp.arange(local_adapter, dtype=jnp.int32)
    kept = []
    for item in range(MOST):
        mask = (blocks[None] == own[:, None, None]) & (position == item)[None]
        kept.append(jnp.sum(jnp.where(mask[..., None], low, 0), axis=2))
    low = lax.psum_scatter(jnp.stack(kept, axis=2), INNER, scatter_dimension=3, tiled=True)
    low = lax.all_gather(low.astype(jnp.bfloat16), "wide", axis=0, tiled=True)
    spread = 0
    for item in range(MOST):
        mask = (blocks[None] == jnp.arange(slots, dtype=jnp.int32)[:, None, None]) & (position == item)
        spread += jnp.where(mask[..., None], low[:, :, item][:, :, None], 0)
    spread = spread.reshape(slots, owners * row_count, rank_portion)
    delta = jnp.einsum("srq,sqw->rw", spread, second_factor_table, preferred_element_type=jnp.float32)
    total = base + delta
    return lax.psum_scatter(total, INNER, scatter_dimension=0, tiled=True).astype(jnp.bfloat16)


def ring_order(nodes):
    return list(range(0, nodes, 2)) + list(range(nodes - 1, 0, -2))


def ringed(
    gate_activation,
    up_activation,
    down_base_weight,
    first_factor_table,
    second_factor_table,
    row_adapter_index,
    adapter_storage_slot,
):
    f32, bf16 = jnp.float32, jnp.bfloat16
    row_count, width_part = gate_activation.shape
    owners = lax.axis_size("wide")
    nodes = owners // 2
    far = nodes // 2
    steps = far - 1
    own_nodes = nodes // 2
    own_blocks = owners // 2
    order = ring_order(nodes)
    depth = width_part // 2

    table = []
    for w in range(owners):
        p, lane = order.index(w // 2), w % 2
        at = lambda shift: order[(p + shift) % nodes]
        arrivals = [at(0)] + [at(s * k) for k in range(1, far) for s in (-1, 1)]
        row = [lane]
        row += [2 * node + side for node in arrivals for side in (0, 1)]
        row += [2 * at(far) + (lane ^ side) for side in (0, 1)]
        row += [int(at(s) < own_nodes) for s in range(far)]
        row += [at(s) % own_nodes for s in range(far)]
        row += [at(s + far) % own_nodes for s in range(far)]
        table.append(row)
    home = lax.axis_index("wide")
    part = lax.axis_index(INNER)
    facts = lax.dynamic_index_in_dim(jnp.asarray(np.array(table, np.int32)), home, 0, keepdims=False)
    edges = np.cumsum([0, 1, 2 * (nodes - 1), 2, far, far, far])
    lane, arrived, far_wide, in_first, near_target, far_target = [
        facts[a:b] for a, b in zip(edges[:-1], edges[1:])
    ]
    side = lane[0]
    mine = (in_first == 1) == (part == 0)
    target = jnp.where(mine, near_target, far_target)

    def moved(shift, cross=0):
        return [
            (order[p] * 2 + c, order[(p + shift) % nodes] * 2 + (c ^ cross))
            for p in range(nodes)
            for c in (0, 1)
        ]

    def send(value, shift, cross=0):
        return lax.ppermute(value, "wide", moved(shift, cross))

    def half_of(value, which, axis):
        return lax.dynamic_slice_in_dim(value, which * depth, depth, axis)

    keep = hidden_of(half_of(gate_activation, side, 1), half_of(up_activation, side, 1))
    right, left = [send(keep, 1)], [send(keep, -1)]
    give = hidden_of(half_of(gate_activation, 1 - side, 1), half_of(up_activation, 1 - side, 1))
    twin = send(give, 0, 1)
    right.append(send(twin, 1))
    left.append(send(twin, -1))

    first = first_factor_table[0]
    weight_sib = send(half_of(down_base_weight, 1 - side, 0), 0, 1)
    first_sib = send(half_of(first, 1 - side, 1), 0, 1)
    product = lambda pieces: rows_product(
        lane, pieces, down_base_weight, weight_sib, first, first_sib
    )

    slot_all = slots_of(row_adapter_index, adapter_storage_slot).reshape(owners, row_count)
    ranks = jnp.arange(row_count, dtype=jnp.int32)
    earlier = (slot_all[:, :, None] == slot_all[:, None, :]) & (ranks[None, :] < ranks[:, None])
    position = jnp.sum(earlier.astype(jnp.int32), axis=2)
    items = jnp.arange(MOST, dtype=jnp.int32)

    sides = jnp.arange(2, dtype=jnp.int32)
    own_wide = jnp.bitwise_xor(home, sides)
    blocks = jnp.arange(owners, dtype=jnp.int32)
    own_is = own_wide[:, None, None] == blocks[None, :, None]
    own_slot = jnp.sum(jnp.where(own_is, slot_all[None], 0), axis=1)
    own_position = jnp.sum(jnp.where(own_is, position[None], 0), axis=1)
    pick = (own_slot[None, :, None, :] == far_wide[:, None, None, None]) & (
        own_position[None, :, None, :] == items[None, None, :, None]
    )
    pick = jnp.where(
        (sides[:, None] == sides[None, :])[None, :, None, :, None], pick[:, :, :, None, :], False
    ).reshape(4 * MOST, 2 * row_count)
    both = jnp.concatenate([keep, twin], axis=0)
    picked = jnp.dot(pick.astype(bf16), both, preferred_element_type=f32).astype(bf16)
    far_rows = send(picked, far)

    mine_sums, sib_sums, lows = [], [], []

    def add(result):
        mine_sums.append(result[0])
        sib_sums.append(send(result[1], 0, 1))
        lows.append(result[2].reshape(-1, result[2].shape[3]))

    pieces = [keep, twin]
    result = None
    for step in range(1, steps + 1):
        pieces += right + left
        if result is not None:
            right[0], left[0], result = lax.optimization_barrier((right[0], left[0], result))
            add(result)
        if step < steps:
            right = [send(block, 1) for block in right]
            left = [send(block, -1) for block in left]
        else:
            last = [send(right[0], 1), send(left[1], -1)]
        result = product(pieces)
        pieces = []
    last[0], last[1], result = lax.optimization_barrier((last[0], last[1], result))
    add(result)

    far_low = lax.dot_general(
        far_rows,
        jnp.concatenate([first_half(first, side, depth), first_sib], axis=0),
        (((1,), (1,)), ((), ())),
        preferred_element_type=f32,
    )
    rank = first.shape[0]
    low = jnp.concatenate(lows, axis=0)

    def chosen(slot, far_part):
        near = (
            (arrived[None, None, :, None] == blocks[:, None, None, None])
            & (slot_all == slot)[:, None, None, :]
            & (position[:, None, None, :] == items[None, :, None, None])
        ).reshape(owners * MOST, -1)
        there = (
            (far_wide[None, None, :, None] == blocks[:, None, None, None])
            & (items[:, None] == items[None, :])[None, :, None, :]
        ).reshape(owners * MOST, -1)
        return jnp.concatenate([near, there], axis=1).astype(f32)

    def compact(slot, values, far_values):
        return jnp.dot(
            chosen(slot, far_values),
            jnp.concatenate([values, far_values], axis=0),
            precision=lax.Precision.HIGHEST,
        )

    count = 2 * MOST
    low_sib = compact(jnp.bitwise_xor(home, 1), low[:, rank:], far_low[count:, rank:])
    low_mine = compact(home, low[:, :rank], far_low[:count, :rank])
    low = low_mine + send(low_sib, 0, 1)

    half = owners * MOST // 2
    kept = jnp.where(part == 0, low[:half], low[half:])
    sent = jnp.where(part == 0, low[half:], low[:half])
    low = (kept + lax.ppermute(sent, INNER, SWAP)).astype(bf16)[None]
    gap = 1
    while gap < owners:
        other = lax.ppermute(low, "wide", [(w, w ^ gap) for w in range(owners)])
        low = jnp.where(
            home & gap == 0,
            jnp.concatenate([low, other], axis=0),
            jnp.concatenate([other, low], axis=0),
        )
        gap *= 2
    low = low.reshape(owners, own_blocks, MOST, rank)

    other = lax.ppermute(second_factor_table, INNER, SWAP)
    second = jnp.where(
        part == 0,
        jnp.concatenate([second_factor_table, other], axis=1),
        jnp.concatenate([other, second_factor_table], axis=1),
    )
    width = second.shape[2]
    slot_here = lax.dynamic_slice_in_dim(slot_all, part * own_blocks, own_blocks)
    position_here = lax.dynamic_slice_in_dim(position, part * own_blocks, own_blocks)
    spread = 0
    for item in range(MOST):
        mask = (slot_here[:, :, None] == blocks) & (position_here == item)[:, :, None]
        spread += jnp.where(mask[..., None], jnp.swapaxes(low[:, :, item], 0, 1)[:, None], 0)
    delta = jnp.dot(
        spread.reshape(own_blocks * row_count, -1).astype(bf16),
        second.reshape(-1, width),
        preferred_element_type=f32,
    )

    result = product(last)
    add(result)
    sums = [a + b for a, b in zip(mine_sums, sib_sums)]
    group_rows = 2 * row_count
    by_shift = {0: sums[0][0], far: sums[-1][0]}
    for step in range(1, far):
        extra = 1 if step == 1 else 0
        by_shift[nodes - step] = sums[step - 1][extra]
        by_shift[step] = sums[step - 1][extra + 1]

    def over_mp(shifts):
        near = jnp.stack([by_shift[s] for s in shifts])
        away = jnp.stack([by_shift[s + far] for s in shifts])
        pred = mine[shifts[0] : shifts[-1] + 1][:, None, None, None]
        kept = jnp.where(pred, near, away)
        sent = jnp.where(pred, away, near).astype(bf16)
        return kept + lax.ppermute(sent, INNER, SWAP).astype(f32)

    values = jnp.concatenate([over_mp([0]), over_mp(list(range(1, far)))], axis=0)
    delta = delta.reshape(own_nodes, group_rows, width)
    out = []
    for index in range(own_nodes):
        rows = delta[index]
        for pair in range(far):
            rows = rows + jnp.where(
                target[pair] == index, values[pair].reshape(group_rows, width), 0
            )
        out.append(rows)
    return jnp.stack(out).reshape(-1, width).astype(bf16)


def first_half(first, side, depth):
    return lax.dynamic_slice_in_dim(first, side * depth, depth, 1)


def solution(mesh):
    shape = dict(mesh.shape)
    wide, inner = shape["wide"], shape["mp"] * shape["sub"]
    paired = shape["sub"] == 1 and inner == 2 and wide % 8 == 0 and wide & (wide - 1) == 0
    if paired:
        nodes = wide // 2
        order = ring_order(nodes)
        paired = all(
            (order[p] < nodes // 2) != (order[(p + nodes // 2) % nodes] < nodes // 2)
            for p in range(nodes)
        )
    return jax.shard_map(
        ringed if paired else gathered,
        mesh=mesh,
        in_specs=(
            P(("groups", "wide"), ("mp", "sub")),
            P(("groups", "wide"), ("mp", "sub")),
            P(("mp", "sub"), "wide"),
            P("wide", None, ("mp", "sub")),
            P(None, ("mp", "sub"), "wide"),
            P("groups", None),
            P(),
        ),
        out_specs=P(("groups", "mp", "sub"), "wide"),
        check_vma=False,
    )
```

```python
import functools

import jax
import jax.numpy as jnp
import numpy as np
from jax import lax
from jax.experimental import pallas as pl
from jax.experimental.pallas import tpu as pltpu
from jax.sharding import PartitionSpec as P

MOST = 2
INNER = ("mp", "sub")
SWAP = [(0, 1), (1, 0)]


def tile_of(depth, most=512):
    parts = 1
    while depth % parts or (depth // parts) % 128 or depth // parts > most:
        parts += 1
    return depth // parts


def rows_kernel(count, extra, with_base, with_low, lane_ref, *refs):
    pieces, refs = refs[:count], refs[count:]
    more, refs = refs[:extra], refs[extra:]
    weights, refs = refs[: 2 * with_base], refs[2 * with_base :]
    factors, refs = refs[: 2 * with_low], refs[2 * with_low :]
    outs = refs[: 2 * with_base + with_low + extra]
    sums = refs[2 * with_base + with_low + extra :]
    step = pl.program_id(0)

    @pl.when(step == 0)
    def _():
        for total in sums:
            total[...] = jnp.zeros_like(total)

    rows = jnp.concatenate([piece[...] for piece in pieces], axis=0)
    for weight, total in zip(weights, sums):
        total[...] += jnp.dot(rows, weight[...], preferred_element_type=jnp.float32)
    if with_low:
        table = jnp.concatenate([factor[...] for factor in factors], axis=0)
        for values, total in zip([rows] + [m[...] for m in more], sums[2 * with_base :]):
            total[...] += lax.dot_general(
                values, table, (((1,), (1,)), ((), ())), preferred_element_type=jnp.float32
            )

    @pl.when(step == pl.num_programs(0) - 1)
    def _():
        height = pieces[0].shape[0]
        for out, total in zip(outs[: 2 * with_base + with_low], sums):
            for index in range(count):
                lane = jnp.bitwise_xor(lane_ref[0], index % 2)
                out[index // 2, lane] = total[index * height : (index + 1) * height, :]
        for out, total in zip(outs[2 * with_base + with_low :], sums[2 * with_base + with_low :]):
            out[...] = total[...]


def rows_product(lane, pieces, weights=(), factors=(), more=()):
    count = len(pieces)
    row_count, depth = pieces[0].shape
    tile = tile_of(depth)
    tiles = depth // tile
    total = count * row_count
    in_specs = [pl.BlockSpec((row_count, tile), lambda i, lane: (0, i))] * count
    in_specs += [pl.BlockSpec((m.shape[0], tile), lambda i, lane: (0, i)) for m in more]
    in_specs += [pl.BlockSpec((tile, w.shape[1]), lambda i, lane: (lane[0] * tiles + i, 0)) for w in weights]
    in_specs += [pl.BlockSpec((f.shape[0], tile), lambda i, lane: (0, lane[0] * tiles + i)) for f in factors]
    sizes = [w.shape[1] for w in weights]
    if factors:
        sizes.append(sum(f.shape[0] for f in factors))
    out_specs = [
        pl.BlockSpec((count // 2, 2, row_count, size), lambda i, lane: (0, 0, 0, 0)) for size in sizes
    ]
    out_shape = [
        jax.ShapeDtypeStruct((count // 2, 2, row_count, size), jnp.float32) for size in sizes
    ]
    scratch = [pltpu.VMEM((total, size), jnp.float32) for size in sizes]
    for m in more:
        out_specs.append(pl.BlockSpec((m.shape[0], sizes[-1]), lambda i, lane: (0, 0)))
        out_shape.append(jax.ShapeDtypeStruct((m.shape[0], sizes[-1]), jnp.float32))
        scratch.append(pltpu.VMEM((m.shape[0], sizes[-1]), jnp.float32))
    return pl.pallas_call(
        functools.partial(rows_kernel, count, len(more), int(bool(weights)), int(bool(factors))),
        grid_spec=pltpu.PrefetchScalarGridSpec(
            num_scalar_prefetch=1,
            grid=(tiles,),
            in_specs=in_specs,
            out_specs=out_specs,
            scratch_shapes=scratch,
        ),
        out_shape=out_shape,
        compiler_params=pltpu.CompilerParams(vmem_limit_bytes=40 * 2**20),
        cost_estimate=pl.CostEstimate(
            flops=total * depth * sum(sizes) // 8,
            bytes_accessed=depth * sum(sizes) // 4,
            transcendentals=0,
        ),
    )(lane, *pieces, *more, *weights, *factors)


def hidden_of(gate, up):
    return (jax.nn.silu(gate.astype(jnp.float32)) * up.astype(jnp.float32)).astype(jnp.bfloat16)


def slots_of(row_adapter_index, adapter_storage_slot):
    names = jnp.arange(adapter_storage_slot.shape[0], dtype=jnp.int32)
    same = row_adapter_index == names[None, :]
    return jnp.sum(jnp.where(same, adapter_storage_slot[None, :], 0), axis=1)


def gathered(
    gate_activation,
    up_activation,
    down_base_weight,
    first_factor_table,
    second_factor_table,
    row_adapter_index,
    adapter_storage_slot,
):
    hidden = hidden_of(gate_activation, up_activation)
    row_count = hidden.shape[0]
    owners = lax.axis_size("wide")
    local_adapter = first_factor_table.shape[0]
    slots = local_adapter * owners
    rank_portion = second_factor_table.shape[1]
    home = lax.axis_index("wide")
    slot_all = slots_of(row_adapter_index, adapter_storage_slot)
    blocks = slot_all.reshape(owners, row_count)
    order = jnp.arange(row_count, dtype=jnp.int32)
    earlier = (blocks[:, :, None] == blocks[:, None, :]) & (order[None, :] < order[:, None])
    position = jnp.sum(earlier.astype(jnp.int32), axis=2)
    rows = lax.all_gather(hidden, "wide", axis=0, tiled=True)
    base = jnp.dot(rows, down_base_weight, preferred_element_type=jnp.float32)
    low = jnp.einsum("re,nqe->nrq", rows, first_factor_table, preferred_element_type=jnp.float32)
    low = low.reshape(local_adapter, owners, row_count, low.shape[2])
    own = home * local_adapter + jnp.arange(local_adapter, dtype=jnp.int32)
    kept = []
    for item in range(MOST):
        mask = (blocks[None] == own[:, None, None]) & (position == item)[None]
        kept.append(jnp.sum(jnp.where(mask[..., None], low, 0), axis=2))
    low = lax.psum_scatter(jnp.stack(kept, axis=2), INNER, scatter_dimension=3, tiled=True)
    low = lax.all_gather(low.astype(jnp.bfloat16), "wide", axis=0, tiled=True)
    spread = 0
    for item in range(MOST):
        mask = (blocks[None] == jnp.arange(slots, dtype=jnp.int32)[:, None, None]) & (position == item)
        spread += jnp.where(mask[..., None], low[:, :, item][:, :, None], 0)
    spread = spread.reshape(slots, owners * row_count, rank_portion)
    delta = jnp.einsum("srq,sqw->rw", spread, second_factor_table, preferred_element_type=jnp.float32)
    total = base + delta
    return lax.psum_scatter(total, INNER, scatter_dimension=0, tiled=True).astype(jnp.bfloat16)


def ring_order(nodes):
    return list(range(0, nodes, 2)) + list(range(nodes - 1, 0, -2))


def combine_kernel(first_pair, pairs, flags, near, near_sib, away, away_sib, kept, sent):
    for pair in range(pairs):
        here = near[pair] + near_sib[pair]
        there = away[pair] + away_sib[pair]
        mine = flags[first_pair + pair] == 1
        kept[pair] = jnp.where(mine, here, there)
        sent[pair] = jnp.where(mine, there, here).astype(jnp.bfloat16)


def combine(first_pair, flags, near, near_sib, away, away_sib):
    pairs = near.shape[0]
    return pl.pallas_call(
        functools.partial(combine_kernel, first_pair, pairs),
        in_specs=[pl.BlockSpec(memory_space=pltpu.SMEM)]
        + [pl.BlockSpec(memory_space=pltpu.VMEM)] * 4,
        out_specs=[pl.BlockSpec(memory_space=pltpu.VMEM)] * 2,
        out_shape=[
            jax.ShapeDtypeStruct(near.shape, jnp.float32),
            jax.ShapeDtypeStruct(near.shape, jnp.bfloat16),
        ],
    )(flags, near, near_sib, away, away_sib)


def delta_kernel(low, choose, mask, second, out):
    own = jnp.dot(choose[...], low[...], preferred_element_type=jnp.float32).astype(jnp.bfloat16)
    copies = mask.shape[1] // own.shape[1]
    spread = jnp.concatenate([own] * copies, axis=1) * mask[...]
    out[...] = jnp.dot(spread, second[...], preferred_element_type=jnp.float32)


def assemble_kernel(target, kept, got, kept_more, got_more, delta, out):
    pairs = out.shape[0]
    for pair in range(pairs):
        place = target[pair]
        if pair == 0:
            value = kept[0] + got[0].astype(jnp.float32)
        else:
            value = kept_more[pair - 1] + got_more[pair - 1].astype(jnp.float32)
        out[place] = (value + delta[place]).astype(jnp.bfloat16)


def whole_call(kernel, out_shape, scalars, *arrays):
    return pl.pallas_call(
        kernel,
        in_specs=[pl.BlockSpec(memory_space=pltpu.SMEM)] * len(scalars)
        + [pl.BlockSpec(memory_space=pltpu.VMEM)] * len(arrays),
        out_specs=pl.BlockSpec(memory_space=pltpu.VMEM),
        out_shape=out_shape,
    )(*scalars, *arrays)


def ringed(
    gate_activation,
    up_activation,
    down_base_weight,
    first_factor_table,
    second_factor_table,
    row_adapter_index,
    adapter_storage_slot,
):
    f32, bf16 = jnp.float32, jnp.bfloat16
    row_count, width_part = gate_activation.shape
    owners = lax.axis_size("wide")
    nodes = owners // 2
    far = nodes // 2
    steps = far - 1
    own_nodes = nodes // 2
    own_blocks = owners // 2
    group_rows = 2 * row_count
    order = ring_order(nodes)
    depth = width_part // 2
    width = down_base_weight.shape[1]
    rank = first_factor_table.shape[1]

    table = []
    for w in range(owners):
        p, lane = order.index(w // 2), w % 2
        at = lambda shift: order[(p + shift) % nodes]
        arrivals = [at(0)] + [at(s * k) for k in range(1, far) for s in (-1, 1)]
        row = [2 * node + side for node in arrivals for side in (0, 1)]
        row += [2 * at(far) + (lane ^ side) for side in (0, 1)]
        for half in (0, 1):
            here = [(at(s) < own_nodes) == (half == 0) for s in range(far)]
            row += [int(h) for h in here]
            row += [at(s if h else s + far) % own_nodes for s, h in enumerate(here)]
        table.append(row)
    home = lax.axis_index("wide")
    part = lax.axis_index(INNER)
    side = jnp.bitwise_and(home, 1)
    lane = side[None]

    def moved(shift, cross=0):
        return [
            (order[p] * 2 + c, order[(p + shift) % nodes] * 2 + (c ^ cross))
            for p in range(nodes)
            for c in (0, 1)
        ]

    def send(value, shift, cross=0):
        return lax.ppermute(value, "wide", moved(shift, cross))

    def half_of(value, which, axis):
        return lax.dynamic_slice_in_dim(value, which * depth, depth, axis)

    keep = hidden_of(half_of(gate_activation, side, 1), half_of(up_activation, side, 1))
    right, left = [send(keep, 1)], [send(keep, -1)]
    other_side, keep = lax.optimization_barrier((1 - side, keep))
    give = hidden_of(half_of(gate_activation, other_side, 1), half_of(up_activation, other_side, 1))
    twin = send(give, 0, 1)
    right.append(send(twin, 1))
    left.append(send(twin, -1))

    first = first_factor_table[0]
    first, twin = lax.optimization_barrier((first, twin))
    weight, first_sib = lax.optimization_barrier((down_base_weight, send(first, 0, 1)))
    weights = (weight, send(weight, 0, 1))
    factors = (first, first_sib)

    facts = lax.dynamic_index_in_dim(
        jnp.asarray(np.array(table, np.int32)), home, 0, keepdims=False
    )
    edges = np.cumsum([0, 2 * (nodes - 1), 2, far, far, far, far])
    arrived, far_wide, *rest = [facts[a:b] for a, b in zip(edges[:-1], edges[1:])]
    flags = jnp.where(part == 0, rest[0], rest[2])
    target = jnp.where(part == 0, rest[1], rest[3])
    slot_all = slots_of(row_adapter_index, adapter_storage_slot).reshape(owners, row_count)
    ranks = jnp.arange(row_count, dtype=jnp.int32)
    earlier = (slot_all[:, :, None] == slot_all[:, None, :]) & (ranks[None, :] < ranks[:, None])
    position = jnp.sum(earlier.astype(jnp.int32), axis=2)
    items = jnp.arange(MOST, dtype=jnp.int32)

    sides = jnp.arange(2, dtype=jnp.int32)
    own_wide = jnp.bitwise_xor(home, sides)
    blocks = jnp.arange(owners, dtype=jnp.int32)
    own_is = own_wide[:, None, None] == blocks[None, :, None]
    own_slot = jnp.sum(jnp.where(own_is, slot_all[None], 0), axis=1)
    own_position = jnp.sum(jnp.where(own_is, position[None], 0), axis=1)
    pick = (own_slot[None, :, None, :] == far_wide[:, None, None, None]) & (
        own_position[None, :, None, :] == items[None, None, :, None]
    )
    pick = jnp.where(
        (sides[:, None] == sides[None, :])[None, :, None, :, None], pick[:, :, :, None, :], False
    ).reshape(4 * MOST, group_rows)
    both = jnp.concatenate([keep, twin], axis=0)
    picked = jnp.dot(pick.astype(bf16), both, preferred_element_type=f32).astype(bf16)
    far_rows = send(picked, far)

    slot_here = lax.dynamic_slice_in_dim(slot_all, part * own_blocks, own_blocks)
    position_here = lax.dynamic_slice_in_dim(position, part * own_blocks, own_blocks)
    came = jnp.bitwise_xor(home, blocks)
    choose = (
        (slot_here[:, :, None, None, None] == came[:, None, None])
        & (position_here[:, :, None, None, None] == items)
        & (jnp.arange(own_blocks)[:, None] == jnp.arange(own_blocks)[None, :])[:, None, None, :, None]
    )
    choose = choose.astype(bf16).reshape(own_blocks * row_count, owners * own_blocks * MOST)
    mask = jnp.repeat(
        (slot_here.reshape(-1)[:, None] == blocks[None, :]).astype(bf16), rank, axis=1
    )

    other = lax.ppermute(second_factor_table, INNER, SWAP)
    second = jnp.where(
        part == 0,
        jnp.concatenate([second_factor_table, other], axis=1),
        jnp.concatenate([other, second_factor_table], axis=1),
    ).reshape(owners * rank, width)

    def chosen(slot):
        near = (
            (arrived[None, None, :, None] == blocks[:, None, None, None])
            & (slot_all == slot)[:, None, None, :]
            & (position[:, None, None, :] == items[None, :, None, None])
        ).reshape(owners * MOST, -1)
        there = (
            (far_wide[None, None, :, None] == blocks[:, None, None, None])
            & (items[:, None] == items[None, :])[None, :, None, :]
        ).reshape(owners * MOST, -1)
        return jnp.concatenate([near, there], axis=1).astype(f32)

    chosen_mine, chosen_sib = chosen(home), chosen(jnp.bitwise_xor(home, 1))

    results, sibs, lows = [], [], []

    def add(result):
        results.append(result)
        sibs.append(send(result[1], 0, 1))

    ready = (far_rows, second, choose, mask, chosen_mine, chosen_sib)
    pieces = [keep, twin]
    for step in range(1, steps + 1):
        if step > 1:
            right, left, ready, result = lax.optimization_barrier((right, left, ready, result))
            add(result[:2])
            lows.append(result[2])
        pieces += right + left
        if step < steps:
            right = [send(block, 1) for block in right]
            left = [send(block, -1) for block in left]
            result = rows_product(lane, pieces, weights, factors)
        else:
            last = [send(right[0], 1), send(left[1], -1)]
            far_rows, second, choose, mask, chosen_mine, chosen_sib = ready
            low, far_low = rows_product(lane, pieces, (), factors, (far_rows,))
            lows.append(low)
            result = rows_product(lane, pieces, weights)
        pieces = []
    result, last = lax.optimization_barrier((result, last))
    add(result)

    low = jnp.concatenate([values.reshape(-1, 2 * rank) for values in lows], axis=0)
    count = 2 * MOST

    def compact(choice, values, far_values):
        return jnp.dot(
            choice,
            jnp.concatenate([values, far_values], axis=0),
            precision=lax.Precision.HIGHEST,
        )

    low = jnp.stack(
        [
            compact(chosen_mine, low[:, :rank], far_low[:count, :rank]),
            compact(chosen_sib, low[:, rank:], far_low[count:, rank:]),
        ]
    )
    half = own_blocks * MOST
    kept = jnp.where(part == 0, low[:, :half], low[:, half:])
    sent = jnp.where(part == 0, low[:, half:], low[:, :half])
    low = kept + lax.ppermute(sent, INNER, SWAP)
    low = (low + send(low, 0, 1)[::-1]).astype(bf16)
    gap = 2
    while gap < owners:
        other = lax.ppermute(low, "wide", [(w, w ^ gap) for w in range(owners)])
        low = jnp.concatenate([low, other], axis=0)
        gap *= 2
    delta = whole_call(
        delta_kernel,
        jax.ShapeDtypeStruct((own_blocks * row_count, width), f32),
        (),
        low.reshape(owners * half, rank),
        choose,
        mask,
        second,
    ).reshape(own_nodes, group_rows, width)

    def node(values, shift):
        if shift == 0:
            return values[0][0]
        if shift == far:
            return values[-1][0]
        step = min(shift, nodes - shift)
        return values[step - 1][(1 if step == 1 else 0) + (0 if shift > far else 1)]

    def over_mp(shifts):
        stacks = []
        for offset in (0, far):
            for values in ([r[0] for r in results], sibs):
                group = jnp.stack([node(values, s + offset) for s in shifts])
                stacks.append(group.reshape(len(shifts), group_rows, width))
        kept, sent = combine(shifts[0], flags, *stacks)
        return kept, lax.ppermute(sent, INNER, SWAP)

    more = over_mp(list(range(1, far)))
    add(rows_product(lane, last, weights))
    out = whole_call(
        assemble_kernel,
        jax.ShapeDtypeStruct((own_nodes, group_rows, width), bf16),
        (target,),
        *over_mp([0]),
        *more,
        delta,
    )
    return out.reshape(-1, width)


def solution(mesh):
    shape = dict(mesh.shape)
    wide, inner = shape["wide"], shape["mp"] * shape["sub"]
    paired = shape["sub"] == 1 and inner == 2 and wide % 8 == 0 and wide & (wide - 1) == 0
    if paired:
        nodes = wide // 2
        order = ring_order(nodes)
        paired = all(
            (order[p] < nodes // 2) != (order[(p + nodes // 2) % nodes] < nodes // 2)
            for p in range(nodes)
        )
    return jax.shard_map(
        ringed if paired else gathered,
        mesh=mesh,
        in_specs=(
            P(("groups", "wide"), ("mp", "sub")),
            P(("groups", "wide"), ("mp", "sub")),
            P(("mp", "sub"), "wide"),
            P("wide", None, ("mp", "sub")),
            P(None, ("mp", "sub"), "wide"),
            P("groups", None),
            P(),
        ),
        out_specs=P(("groups", "mp", "sub"), "wide"),
        check_vma=False,
    )
```

```python
import functools

import jax
import jax.numpy as jnp
import numpy as np
from jax import lax
from jax.experimental import pallas as pl
from jax.experimental.pallas import tpu as pltpu
from jax.sharding import PartitionSpec as P

MOST = 2
INNER = ("mp", "sub")
SWAP = [(0, 1), (1, 0)]


def tile_of(depth, most=1024):
    parts = 1
    while depth % parts or (depth // parts) % 128 or depth // parts > most:
        parts += 1
    return depth // parts


def rows_kernel(count, extra, with_base, with_low, tile, lane_ref, *refs):
    pieces, refs = refs[:count], refs[count:]
    more, refs = refs[:extra], refs[extra:]
    weights, refs = refs[: 2 * with_base], refs[2 * with_base :]
    factors, refs = refs[: 2 * with_low], refs[2 * with_low :]
    made = 2 * with_base + with_low + extra
    outs, sums, refs = refs[:made], refs[made : 2 * made], refs[2 * made :]
    depth = pieces[0].shape[1]
    first_row = pl.multiple_of(lane_ref[0] * depth, 128)
    tiles = depth // tile

    weight_copies, factor_copies = [], []
    if with_base:
        held, arrived = refs[:2]
        for index in range(tiles):
            for which, weight in enumerate(weights):
                copy = pltpu.make_async_copy(
                    weight.at[pl.ds(first_row + index * tile, tile)],
                    held.at[which, index],
                    arrived.at[which, index],
                )
                copy.start()
                weight_copies.append(copy)
    if with_low:
        table, ready = refs[-2:]
        rank = factors[0].shape[0]
        for which, factor in enumerate(factors):
            copy = pltpu.make_async_copy(
                factor.at[:, pl.ds(first_row, depth)],
                table.at[pl.ds(which * rank, rank)],
                ready.at[which],
            )
            copy.start()
            factor_copies.append(copy)

    for total in sums:
        total[...] = jnp.zeros_like(total)
    for index in range(tiles if with_base else 0):
        rows = jnp.concatenate([p[:, index * tile : (index + 1) * tile] for p in pieces], axis=0)
        for which in range(2):
            weight_copies[2 * index + which].wait()
            sums[which][...] += jnp.dot(
                rows, held[which, index], preferred_element_type=jnp.float32
            )
    for copy in factor_copies:
        copy.wait()
    if with_low:

        def step(index, carry):
            columns = pl.ds(pl.multiple_of(index * tile, 128), tile)
            rows = jnp.concatenate([p[:, columns] for p in pieces], axis=0)
            for values, total in zip([rows] + [m[:, columns] for m in more], sums[2 * with_base :]):
                total[...] += lax.dot_general(
                    values,
                    table[:, columns],
                    (((1,), (1,)), ((), ())),
                    preferred_element_type=jnp.float32,
                )
            return carry

        lax.fori_loop(0, tiles, step, 0)
    for out, total in zip(outs[: made - extra], sums):
        height = out.shape[2]
        for index in range(2 * out.shape[0]):
            lane = jnp.bitwise_xor(lane_ref[0], index % 2)
            out[index // 2, lane] = total[index * height : (index + 1) * height, :]
    for out, total in zip(outs[made - extra :], sums[made - extra :]):
        out[...] = total[...]


def rows_product(lane, row_count, pieces, weights=(), factors=(), more=()):
    count = len(pieces)
    depth = pieces[0].shape[1]
    total = sum(piece.shape[0] for piece in pieces)
    nodes = total // (2 * row_count)
    tile = tile_of(depth)
    sizes = [w.shape[1] for w in weights]
    if factors:
        sizes.append(sum(f.shape[0] for f in factors))
    out_shape = [
        jax.ShapeDtypeStruct((nodes, 2, row_count, size), jnp.float32) for size in sizes
    ]
    scratch = [pltpu.VMEM((total, size), jnp.float32) for size in sizes]
    for m in more:
        out_shape.append(jax.ShapeDtypeStruct((m.shape[0], sizes[-1]), jnp.float32))
        scratch.append(pltpu.VMEM((m.shape[0], sizes[-1]), jnp.float32))
    if weights:
        scratch.append(pltpu.VMEM((2, depth // tile, tile, sizes[0]), jnp.bfloat16))
        scratch.append(pltpu.SemaphoreType.DMA((2, depth // tile)))
    if factors:
        scratch.append(pltpu.VMEM((sizes[-1], depth), jnp.bfloat16))
        scratch.append(pltpu.SemaphoreType.DMA((2,)))
    return pl.pallas_call(
        functools.partial(
            rows_kernel, count, len(more), int(bool(weights)), int(bool(factors)), tile
        ),
        in_specs=[pl.BlockSpec(memory_space=pltpu.SMEM)]
        + [pl.BlockSpec(memory_space=pltpu.VMEM)] * (count + len(more))
        + [pl.BlockSpec(memory_space=pl.ANY)] * (len(weights) + len(factors)),
        out_specs=[pl.BlockSpec(memory_space=pltpu.VMEM)] * len(out_shape),
        out_shape=out_shape,
        scratch_shapes=scratch,
        compiler_params=pltpu.CompilerParams(vmem_limit_bytes=40 * 2**20),
        cost_estimate=pl.CostEstimate(
            flops=total * depth * sum(sizes) // 64,
            bytes_accessed=depth * sum(sizes) // 32,
            transcendentals=0,
        ),
    )(lane, *pieces, *more, *weights, *factors)


def hidden_of(gate, up):
    return (jax.nn.silu(gate.astype(jnp.float32)) * up.astype(jnp.float32)).astype(jnp.bfloat16)


def slots_of(row_adapter_index, adapter_storage_slot):
    names = jnp.arange(adapter_storage_slot.shape[0], dtype=jnp.int32)
    same = row_adapter_index == names[None, :]
    return jnp.sum(jnp.where(same, adapter_storage_slot[None, :], 0), axis=1)


def gathered(
    gate_activation,
    up_activation,
    down_base_weight,
    first_factor_table,
    second_factor_table,
    row_adapter_index,
    adapter_storage_slot,
):
    hidden = hidden_of(gate_activation, up_activation)
    row_count = hidden.shape[0]
    owners = lax.axis_size("wide")
    local_adapter = first_factor_table.shape[0]
    slots = local_adapter * owners
    rank_portion = second_factor_table.shape[1]
    home = lax.axis_index("wide")
    slot_all = slots_of(row_adapter_index, adapter_storage_slot)
    blocks = slot_all.reshape(owners, row_count)
    order = jnp.arange(row_count, dtype=jnp.int32)
    earlier = (blocks[:, :, None] == blocks[:, None, :]) & (order[None, :] < order[:, None])
    position = jnp.sum(earlier.astype(jnp.int32), axis=2)
    rows = lax.all_gather(hidden, "wide", axis=0, tiled=True)
    base = jnp.dot(rows, down_base_weight, preferred_element_type=jnp.float32)
    low = jnp.einsum("re,nqe->nrq", rows, first_factor_table, preferred_element_type=jnp.float32)
    low = low.reshape(local_adapter, owners, row_count, low.shape[2])
    own = home * local_adapter + jnp.arange(local_adapter, dtype=jnp.int32)
    kept = []
    for item in range(MOST):
        mask = (blocks[None] == own[:, None, None]) & (position == item)[None]
        kept.append(jnp.sum(jnp.where(mask[..., None], low, 0), axis=2))
    low = lax.psum_scatter(jnp.stack(kept, axis=2), INNER, scatter_dimension=3, tiled=True)
    low = lax.all_gather(low.astype(jnp.bfloat16), "wide", axis=0, tiled=True)
    spread = 0
    for item in range(MOST):
        mask = (blocks[None] == jnp.arange(slots, dtype=jnp.int32)[:, None, None]) & (position == item)
        spread += jnp.where(mask[..., None], low[:, :, item][:, :, None], 0)
    spread = spread.reshape(slots, owners * row_count, rank_portion)
    delta = jnp.einsum("srq,sqw->rw", spread, second_factor_table, preferred_element_type=jnp.float32)
    total = base + delta
    return lax.psum_scatter(total, INNER, scatter_dimension=0, tiled=True).astype(jnp.bfloat16)


def ring_order(nodes):
    return list(range(0, nodes, 2)) + list(range(nodes - 1, 0, -2))


def ringed(
    gate_activation,
    up_activation,
    down_base_weight,
    first_factor_table,
    second_factor_table,
    row_adapter_index,
    adapter_storage_slot,
):
    f32, bf16 = jnp.float32, jnp.bfloat16
    row_count, width_part = gate_activation.shape
    owners = lax.axis_size("wide")
    nodes = owners // 2
    far = nodes // 2
    steps = far - 1
    own_nodes = nodes // 2
    own_blocks = owners // 2
    group_rows = 2 * row_count
    order = ring_order(nodes)
    depth = width_part // 2
    width = down_base_weight.shape[1]
    rank = first_factor_table.shape[1]

    table = []
    for w in range(owners):
        p, lane = order.index(w // 2), w % 2
        at = lambda shift: order[(p + shift) % nodes]
        arrivals = [at(0)] + [at(s * k) for k in range(1, far) for s in (-1, 1)]
        row = [2 * node + side for node in arrivals for side in (0, 1)]
        row += [2 * at(far) + (lane ^ side) for side in (0, 1)]
        for half in (0, 1):
            here = [(at(s) < own_nodes) == (half == 0) for s in range(far)]
            row += [int(h) for h in here]
            row += [at(s if h else s + far) % own_nodes for s, h in enumerate(here)]
        table.append(row)
    home = lax.axis_index("wide")
    part = lax.axis_index(INNER)
    side = jnp.bitwise_and(home, 1)
    lane = side[None]

    def moved(shift, cross=0):
        return [
            (order[p] * 2 + c, order[(p + shift) % nodes] * 2 + (c ^ cross))
            for p in range(nodes)
            for c in (0, 1)
        ]

    def send(value, shift, cross=0):
        return lax.ppermute(value, "wide", moved(shift, cross))

    def half_of(value, which, axis):
        return lax.dynamic_slice_in_dim(value, which * depth, depth, axis)

    facts = lax.dynamic_index_in_dim(
        jnp.asarray(np.array(table, np.int32)), home, 0, keepdims=False
    )
    edges = np.cumsum([0, 2 * (nodes - 1), 2, far, far, far, far])
    arrived, far_wide, *rest = [facts[a:b] for a, b in zip(edges[:-1], edges[1:])]
    flags = jnp.where(part == 0, rest[0], rest[2])
    target = jnp.where(part == 0, rest[1], rest[3])
    slot_all = slots_of(row_adapter_index, adapter_storage_slot).reshape(owners, row_count)
    ranks = jnp.arange(row_count, dtype=jnp.int32)
    earlier = (slot_all[:, :, None] == slot_all[:, None, :]) & (ranks[None, :] < ranks[:, None])
    position = jnp.sum(earlier.astype(jnp.int32), axis=2)
    items = jnp.arange(MOST, dtype=jnp.int32)

    sides = jnp.arange(2, dtype=jnp.int32)
    own_wide = jnp.bitwise_xor(home, sides)
    blocks = jnp.arange(owners, dtype=jnp.int32)
    own_is = own_wide[:, None, None] == blocks[None, :, None]
    own_slot = jnp.sum(jnp.where(own_is, slot_all[None], 0), axis=1)
    own_position = jnp.sum(jnp.where(own_is, position[None], 0), axis=1)
    pick = (own_slot[None, :, None, :] == far_wide[:, None, None, None]) & (
        own_position[None, :, None, :] == items[None, None, :, None]
    )
    pick = jnp.where(
        (sides[:, None] == sides[None, :])[None, :, None, :, None], pick[:, :, :, None, :], False
    ).reshape(4 * MOST, group_rows).astype(bf16)

    keep = hidden_of(half_of(gate_activation, side, 1), half_of(up_activation, side, 1))
    give = hidden_of(half_of(gate_activation, 1 - side, 1), half_of(up_activation, 1 - side, 1))
    twin, slot_all, position, pick = lax.optimization_barrier(
        (send(give, 0, 1), slot_all, position, pick)
    )
    block = jnp.concatenate([keep, twin], axis=0)
    right, left = send(block, 1), send(block, -1)

    weight, first, block = lax.optimization_barrier(
        (down_base_weight, first_factor_table[0], block)
    )
    weights = (weight, send(weight, 0, 1))
    factors = (first, send(first, 0, 1))
    slot_all, position, weights = lax.optimization_barrier((slot_all, position, weights))

    picked = jnp.dot(pick, block, preferred_element_type=f32).astype(bf16)
    far_rows = send(picked, far)

    slot_here = lax.dynamic_slice_in_dim(slot_all, part * own_blocks, own_blocks)
    position_here = lax.dynamic_slice_in_dim(position, part * own_blocks, own_blocks)
    came = jnp.bitwise_xor(home, blocks)
    spots = (
        (slot_here[:, :, None, None, None] == came[:, None, None])
        & (position_here[:, :, None, None, None] == items)
        & (jnp.arange(own_blocks)[:, None] == jnp.arange(own_blocks)[None, :])[:, None, None, :, None]
    )
    spots = spots.astype(bf16).reshape(own_blocks * row_count, owners * own_blocks * MOST)
    mask = jnp.repeat(
        (slot_here.reshape(-1)[:, None] == blocks[None, :]).astype(bf16), rank, axis=1
    )

    other = lax.ppermute(second_factor_table, INNER, SWAP)
    second = jnp.where(
        part == 0,
        jnp.concatenate([second_factor_table, other], axis=1),
        jnp.concatenate([other, second_factor_table], axis=1),
    ).reshape(owners * rank, width)

    def chosen(slot):
        near = (
            (arrived[None, None, :, None] == blocks[:, None, None, None])
            & (slot_all == slot)[:, None, None, :]
            & (position[:, None, None, :] == items[None, :, None, None])
        ).reshape(owners * MOST, -1)
        there = (
            (far_wide[None, None, :, None] == blocks[:, None, None, None])
            & (items[:, None] == items[None, :])[None, :, None, :]
        ).reshape(owners * MOST, -1)
        return jnp.concatenate([near, there], axis=1).astype(f32)

    chosen_mine, chosen_sib = chosen(home), chosen(jnp.bitwise_xor(home, 1))

    results, sibs, lows = [], [], []

    def add(result):
        results.append(result)
        sibs.append(send(result[1], 0, 1))

    ready = (second, spots, mask, chosen_mine, chosen_sib)
    pieces = [block]
    for step in range(1, steps + 1):
        if step > 1:
            right, left, result = lax.optimization_barrier((right, left, result))
            add(result[:2])
            lows.append(result[2])
        pieces += [right, left]
        if step < steps:
            right, left = send(right, 1), send(left, -1)
            result = rows_product(lane, row_count, pieces, weights, factors)
        else:
            right, left, far_rows, ready, sibs[0] = lax.optimization_barrier(
                (right, left, far_rows, ready, sibs[0])
            )
            last = [send(right[:row_count], 1), send(left[row_count:], -1)]
            second, spots, mask, chosen_mine, chosen_sib = ready
            low, far_low = rows_product(lane, row_count, pieces, (), factors, (far_rows,))
            lows.append(low)
            result = rows_product(lane, row_count, pieces, weights)
        pieces = []
    result, last, sibs = lax.optimization_barrier((result, last, sibs))
    add(result)

    def node(values, shift):
        if shift == 0:
            return values[0][0]
        if shift == far:
            return values[-1][0]
        step = min(shift, nodes - shift)
        return values[step - 1][(1 if step == 1 else 0) + (0 if shift > far else 1)]

    def total(shift):
        both = node([r[0] for r in results], shift) + node(sibs, shift)
        return both.reshape(1, group_rows, width)

    def over_mp(shifts):
        pairs = [(flags[s : s + 1, None, None] == 1, total(s), total(s + far)) for s in shifts]
        sent = jnp.concatenate([jnp.where(f, b, a).astype(bf16) for f, a, b in pairs], axis=0)
        got = lax.ppermute(sent, INNER, SWAP)
        return [jnp.where(f, a, b) for f, a, b in pairs], got


    low = jnp.concatenate([values.reshape(-1, 2 * rank) for values in lows], axis=0)
    count = 2 * MOST

    def compact(choice, values, far_values):
        return jnp.dot(
            choice,
            jnp.concatenate([values, far_values], axis=0),
            precision=lax.Precision.HIGHEST,
        )

    low = jnp.stack(
        [
            compact(chosen_mine, low[:, :rank], far_low[:count, :rank]),
            compact(chosen_sib, low[:, rank:], far_low[count:, rank:]),
        ]
    )
    half = own_blocks * MOST
    kept = jnp.where(part == 0, low[:, :half], low[:, half:])
    sent = jnp.where(part == 0, low[:, half:], low[:, :half])
    low = kept + lax.ppermute(sent, INNER, SWAP)
    low, last = lax.optimization_barrier((low, last))
    low = (low + send(low, 0, 1)[::-1]).astype(bf16)
    kept, got = over_mp(list(range(1, far)))
    add(rows_product(lane, row_count, last, weights))
    gap = 2
    while gap < owners:
        if gap * 2 == owners:
            low, results[-1], got = lax.optimization_barrier((low, results[-1], got))
        other = lax.ppermute(low, "wide", [(w, w ^ gap) for w in range(owners)])
        low = jnp.concatenate([low, other], axis=0)
        gap *= 2
    own_low = jnp.dot(spots, low.reshape(owners * half, rank), preferred_element_type=f32)
    copies = jnp.tile(jnp.eye(rank, dtype=bf16), (1, owners))
    spread = jnp.dot(own_low.astype(bf16), copies, preferred_element_type=f32).astype(bf16) * mask
    delta = jnp.dot(spread, second, preferred_element_type=f32)
    delta = delta.reshape(own_nodes, group_rows, width)

    places = jnp.arange(own_nodes, dtype=jnp.int32)[:, None, None]
    out = delta
    for pair, value in enumerate(kept, 1):
        value = value + got[pair - 1 : pair].astype(f32)
        out = out + jnp.where(places == target[pair : pair + 1, None, None], value, 0)
    kept, got = over_mp([0])
    out = out + jnp.where(places == target[:1, None, None], kept[0] + got.astype(f32), 0)
    return out.astype(bf16).reshape(-1, width)


def solution(mesh):
    shape = dict(mesh.shape)
    wide, inner = shape["wide"], shape["mp"] * shape["sub"]
    paired = shape["sub"] == 1 and inner == 2 and wide % 8 == 0 and wide & (wide - 1) == 0
    if paired:
        nodes = wide // 2
        order = ring_order(nodes)
        paired = all(
            (order[p] < nodes // 2) != (order[(p + nodes // 2) % nodes] < nodes // 2)
            for p in range(nodes)
        )
    return jax.shard_map(
        ringed if paired else gathered,
        mesh=mesh,
        in_specs=(
            P(("groups", "wide"), ("mp", "sub")),
            P(("groups", "wide"), ("mp", "sub")),
            P(("mp", "sub"), "wide"),
            P("wide", None, ("mp", "sub")),
            P(None, ("mp", "sub"), "wide"),
            P("groups", None),
            P(),
        ),
        out_specs=P(("groups", "mp", "sub"), "wide"),
        check_vma=False,
    )
```

```python
import functools

import jax
import jax.numpy as jnp
import numpy as np
from jax import lax
from jax.experimental import pallas as pl
from jax.experimental.pallas import tpu as pltpu
from jax.sharding import PartitionSpec as P

MOST = 2
INNER = ("mp", "sub")
SWAP = [(0, 1), (1, 0)]


def tile_of(depth, most=1024):
    parts = 1
    while depth % parts or (depth // parts) % 128 or depth // parts > most:
        parts += 1
    return depth // parts


def rows_kernel(count, extra, with_base, with_low, tile, lane_ref, *refs):
    pieces, refs = refs[:count], refs[count:]
    more, refs = refs[:extra], refs[extra:]
    weights, refs = refs[: 2 * with_base], refs[2 * with_base :]
    factors, refs = refs[: 2 * with_low], refs[2 * with_low :]
    made = 2 * with_base + with_low + extra
    outs, sums, refs = refs[:made], refs[made : 2 * made], refs[2 * made :]
    depth = pieces[0].shape[1]
    first_row = pl.multiple_of(lane_ref[0] * depth, 128)
    tiles = depth // tile

    weight_copies, factor_copies = [], []
    if with_base:
        held, arrived = refs[:2]
        for index in range(tiles):
            for which, weight in enumerate(weights):
                copy = pltpu.make_async_copy(
                    weight.at[pl.ds(first_row + index * tile, tile)],
                    held.at[which, index],
                    arrived.at[which, index],
                )
                copy.start()
                weight_copies.append(copy)
    if with_low:
        table, ready = refs[-2:]
        rank = factors[0].shape[0]
        for which, factor in enumerate(factors):
            copy = pltpu.make_async_copy(
                factor.at[:, pl.ds(first_row, depth)],
                table.at[pl.ds(which * rank, rank)],
                ready.at[which],
            )
            copy.start()
            factor_copies.append(copy)

    for total in sums:
        total[...] = jnp.zeros_like(total)
    for index in range(tiles if with_base else 0):
        rows = jnp.concatenate([p[:, index * tile : (index + 1) * tile] for p in pieces], axis=0)
        for which in range(2):
            weight_copies[2 * index + which].wait()
            sums[which][...] += jnp.dot(
                rows, held[which, index], preferred_element_type=jnp.float32
            )
    for copy in factor_copies:
        copy.wait()
    if with_low:

        def step(index, carry):
            columns = pl.ds(pl.multiple_of(index * tile, 128), tile)
            rows = jnp.concatenate([p[:, columns] for p in pieces], axis=0)
            for values, total in zip([rows] + [m[:, columns] for m in more], sums[2 * with_base :]):
                total[...] += lax.dot_general(
                    values,
                    table[:, columns],
                    (((1,), (1,)), ((), ())),
                    preferred_element_type=jnp.float32,
                )
            return carry

        lax.fori_loop(0, tiles, step, 0)
    for out, total in zip(outs[: made - extra], sums):
        height = out.shape[2]
        for index in range(2 * out.shape[0]):
            lane = jnp.bitwise_xor(lane_ref[0], index % 2)
            out[index // 2, lane] = total[index * height : (index + 1) * height, :]
    for out, total in zip(outs[made - extra :], sums[made - extra :]):
        out[...] = total[...]


def rows_product(lane, row_count, pieces, weights=(), factors=(), more=()):
    count = len(pieces)
    depth = pieces[0].shape[1]
    total = sum(piece.shape[0] for piece in pieces)
    nodes = total // (2 * row_count)
    tile = tile_of(depth)
    sizes = [w.shape[1] for w in weights]
    if factors:
        sizes.append(sum(f.shape[0] for f in factors))
    out_shape = [
        jax.ShapeDtypeStruct((nodes, 2, row_count, size), jnp.float32) for size in sizes
    ]
    scratch = [pltpu.VMEM((total, size), jnp.float32) for size in sizes]
    for m in more:
        out_shape.append(jax.ShapeDtypeStruct((m.shape[0], sizes[-1]), jnp.float32))
        scratch.append(pltpu.VMEM((m.shape[0], sizes[-1]), jnp.float32))
    if weights:
        scratch.append(pltpu.VMEM((2, depth // tile, tile, sizes[0]), jnp.bfloat16))
        scratch.append(pltpu.SemaphoreType.DMA((2, depth // tile)))
    if factors:
        scratch.append(pltpu.VMEM((sizes[-1], depth), jnp.bfloat16))
        scratch.append(pltpu.SemaphoreType.DMA((2,)))
    return pl.pallas_call(
        functools.partial(
            rows_kernel, count, len(more), int(bool(weights)), int(bool(factors)), tile
        ),
        in_specs=[pl.BlockSpec(memory_space=pltpu.SMEM)]
        + [pl.BlockSpec(memory_space=pltpu.VMEM)] * (count + len(more))
        + [pl.BlockSpec(memory_space=pl.ANY)] * (len(weights) + len(factors)),
        out_specs=[pl.BlockSpec(memory_space=pltpu.VMEM)] * len(out_shape),
        out_shape=out_shape,
        scratch_shapes=scratch,
        compiler_params=pltpu.CompilerParams(vmem_limit_bytes=40 * 2**20),
        cost_estimate=pl.CostEstimate(
            flops=total * depth * sum(sizes) // 64,
            bytes_accessed=depth * sum(sizes) // 32,
            transcendentals=0,
        ),
    )(lane, *pieces, *more, *weights, *factors)


def hidden_of(gate, up):
    return (jax.nn.silu(gate.astype(jnp.float32)) * up.astype(jnp.float32)).astype(jnp.bfloat16)


def slots_of(row_adapter_index, adapter_storage_slot):
    names = jnp.arange(adapter_storage_slot.shape[0], dtype=jnp.int32)
    same = row_adapter_index == names[None, :]
    return jnp.sum(jnp.where(same, adapter_storage_slot[None, :], 0), axis=1)


def gathered(
    gate_activation,
    up_activation,
    down_base_weight,
    first_factor_table,
    second_factor_table,
    row_adapter_index,
    adapter_storage_slot,
):
    hidden = hidden_of(gate_activation, up_activation)
    row_count = hidden.shape[0]
    owners = lax.axis_size("wide")
    local_adapter = first_factor_table.shape[0]
    slots = local_adapter * owners
    rank_portion = second_factor_table.shape[1]
    home = lax.axis_index("wide")
    slot_all = slots_of(row_adapter_index, adapter_storage_slot)
    blocks = slot_all.reshape(owners, row_count)
    order = jnp.arange(row_count, dtype=jnp.int32)
    earlier = (blocks[:, :, None] == blocks[:, None, :]) & (order[None, :] < order[:, None])
    position = jnp.sum(earlier.astype(jnp.int32), axis=2)
    rows = lax.all_gather(hidden, "wide", axis=0, tiled=True)
    base = jnp.dot(rows, down_base_weight, preferred_element_type=jnp.float32)
    low = jnp.einsum("re,nqe->nrq", rows, first_factor_table, preferred_element_type=jnp.float32)
    low = low.reshape(local_adapter, owners, row_count, low.shape[2])
    own = home * local_adapter + jnp.arange(local_adapter, dtype=jnp.int32)
    kept = []
    for item in range(MOST):
        mask = (blocks[None] == own[:, None, None]) & (position == item)[None]
        kept.append(jnp.sum(jnp.where(mask[..., None], low, 0), axis=2))
    low = lax.psum_scatter(jnp.stack(kept, axis=2), INNER, scatter_dimension=3, tiled=True)
    low = lax.all_gather(low.astype(jnp.bfloat16), "wide", axis=0, tiled=True)
    spread = 0
    for item in range(MOST):
        mask = (blocks[None] == jnp.arange(slots, dtype=jnp.int32)[:, None, None]) & (position == item)
        spread += jnp.where(mask[..., None], low[:, :, item][:, :, None], 0)
    spread = spread.reshape(slots, owners * row_count, rank_portion)
    delta = jnp.einsum("srq,sqw->rw", spread, second_factor_table, preferred_element_type=jnp.float32)
    total = base + delta
    return lax.psum_scatter(total, INNER, scatter_dimension=0, tiled=True).astype(jnp.bfloat16)


def ring_order(nodes):
    return list(range(0, nodes, 2)) + list(range(nodes - 1, 0, -2))


def ringed(
    gate_activation,
    up_activation,
    down_base_weight,
    first_factor_table,
    second_factor_table,
    row_adapter_index,
    adapter_storage_slot,
):
    f32, bf16 = jnp.float32, jnp.bfloat16
    row_count, width_part = gate_activation.shape
    owners = lax.axis_size("wide")
    nodes = owners // 2
    far = nodes // 2
    steps = far - 1
    own_nodes = nodes // 2
    own_blocks = owners // 2
    group_rows = 2 * row_count
    order = ring_order(nodes)
    depth = width_part // 2
    width = down_base_weight.shape[1]
    rank = first_factor_table.shape[1]

    table = []
    for w in range(owners):
        p = order.index(w // 2)
        at = lambda shift: order[(p + shift) % nodes]
        arrivals = [at(0)] + [at(s * k) for k in range(1, far) for s in (-1, 1)] + [at(far)]
        row = [2 * node + side for node in arrivals for side in (0, 1)]
        for half in (0, 1):
            here = [(at(s) < own_nodes) == (half == 0) for s in range(far)]
            row += [int(h) for h in here]
            row += [at(s if h else s + far) % own_nodes for s, h in enumerate(here)]
        table.append(row)
    home = lax.axis_index("wide")
    part = lax.axis_index(INNER)
    side = jnp.bitwise_and(home, 1)
    lane = side[None]

    def moved(shift, cross=0):
        return [
            (order[p] * 2 + c, order[(p + shift) % nodes] * 2 + (c ^ cross))
            for p in range(nodes)
            for c in (0, 1)
        ]

    def send(value, shift, cross=0):
        return lax.ppermute(value, "wide", moved(shift, cross))

    def half_of(value, which, axis):
        return lax.dynamic_slice_in_dim(value, which * depth, depth, axis)

    keep = hidden_of(half_of(gate_activation, side, 1), half_of(up_activation, side, 1))
    give = hidden_of(half_of(gate_activation, 1 - side, 1), half_of(up_activation, 1 - side, 1))
    right = [send(keep, 1), send(give, 1, 1)]
    left = [send(keep, -1), send(give, -1, 1)]

    first, twin = lax.optimization_barrier((first_factor_table[0], send(give, 0, 1)))
    factors = (first, send(first, 0, 1))
    weight, factors, twin, right, left = lax.optimization_barrier(
        (down_base_weight, factors, twin, right, left)
    )
    weights = (weight, send(weight, 0, 1))
    home_late, row_adapter_index, second_factor_table, weights = lax.optimization_barrier(
        (home, row_adapter_index, second_factor_table, weights)
    )

    pieces = [keep, twin] + right + left
    for step in range(2, steps + 1):
        right = [send(block, 1) for block in right]
        left = [send(block, -1) for block in left]
        if step < steps:
            right, left = lax.optimization_barrier((right, left))
            pieces += right + left

    facts = lax.dynamic_index_in_dim(
        jnp.asarray(np.array(table, np.int32)), home_late, 0, keepdims=False
    )
    edges = np.cumsum([0, 2 * nodes, far, far, far, far])
    arrived, *rest = [facts[a:b] for a, b in zip(edges[:-1], edges[1:])]
    flags = jnp.where(part == 0, rest[0], rest[2])[:, None, None] == 1
    target = jnp.where(part == 0, rest[1], rest[3])
    places = target[:, None] == jnp.arange(own_nodes, dtype=jnp.int32)[None, :]
    slot_all = slots_of(row_adapter_index, adapter_storage_slot).reshape(owners, row_count)
    ranks = jnp.arange(row_count, dtype=jnp.int32)
    earlier = (slot_all[:, :, None] == slot_all[:, None, :]) & (ranks[None, :] < ranks[:, None])
    position = jnp.sum(earlier.astype(jnp.int32), axis=2)
    items = jnp.arange(MOST, dtype=jnp.int32)
    blocks = jnp.arange(owners, dtype=jnp.int32)

    def chosen(slot):
        picks = (
            (arrived[None, None, :, None] == blocks[:, None, None, None])
            & (slot_all == slot)[:, None, None, :]
            & (position[:, None, None, :] == items[None, :, None, None])
        )
        return picks.reshape(owners * MOST, -1).astype(f32)

    chosen_mine, chosen_sib = chosen(home_late), chosen(jnp.bitwise_xor(home_late, 1))

    half = own_blocks * MOST
    here = own_blocks * row_count
    slot_here = lax.dynamic_slice_in_dim(slot_all, part * own_blocks, own_blocks).reshape(here, 1)
    position_here = lax.dynamic_slice_in_dim(position, part * own_blocks, own_blocks)
    block_here = jnp.arange(here, dtype=jnp.int32)[:, None] // row_count
    spot = (
        jnp.bitwise_xor(slot_here, home_late) * half + block_here * MOST + position_here.reshape(here, 1)
    )
    spots = (spot == jnp.arange(owners * half, dtype=jnp.int32)[None, :]).astype(bf16)
    column = jnp.arange(owners * rank, dtype=jnp.int32)[None, :]
    piece = rank // 2
    own_rank = jnp.bitwise_xor(part, column // (owners * piece)) * piece + column % piece
    mask = (slot_here == column // piece % owners).astype(bf16)
    copies = (jnp.arange(rank, dtype=jnp.int32)[:, None] == own_rank).astype(bf16)
    ready = (spots, mask, copies, chosen_mine, chosen_sib, flags, places)

    other = lax.ppermute(second_factor_table, INNER, SWAP)
    second = jnp.concatenate(
        [table.reshape(owners * piece, width) for table in (second_factor_table, other)], axis=0
    )

    results = [rows_product(lane, row_count, pieces, weights, factors)]
    sibs = []
    right, left, results, ready = lax.optimization_barrier((right, left, results, ready))
    spots, mask, copies, chosen_mine, chosen_sib, flags, places = ready
    last = [send(right[0], 1), send(left[1], -1)]
    sibs.append(send(results[0][1], 0, 1))
    results.append(rows_product(lane, row_count, right + left, weights, factors))
    results, sibs, last, second = lax.optimization_barrier((results, sibs, last, second))
    sibs.append(send(results[1][1], 0, 1))

    low_last = rows_product(lane, row_count, last, (), factors)[0]
    lows = [values[2] for values in results] + [low_last]
    low = jnp.concatenate([values.reshape(-1, 2 * rank) for values in lows], axis=0)
    low = jnp.stack(
        [
            jnp.dot(chosen_mine, low[:, :rank], precision=lax.Precision.HIGHEST),
            jnp.dot(chosen_sib, low[:, rank:], precision=lax.Precision.HIGHEST),
        ]
    )
    kept = jnp.where(part == 0, low[:, :half], low[:, half:])
    sent = jnp.where(part == 0, low[:, half:], low[:, :half])
    crossed = [(2 * w + m, 2 * (w ^ 1) + (1 - m)) for w in range(owners) for m in (0, 1)]
    low_mp = lax.ppermute(sent, INNER, SWAP)
    low_sib = send(kept, 0, 1)
    low_both = lax.ppermute(sent, ("wide",) + INNER, crossed)

    low_mp, low_sib, low_both, last = lax.optimization_barrier((low_mp, low_sib, low_both, last))
    results.append(rows_product(lane, row_count, last, weights))
    sibs.append(send(results[2][1], 0, 1))

    low = (kept + low_mp + (low_sib + low_both)[::-1]).astype(bf16)

    def from_node(value, gap):
        return lax.ppermute(value, "wide", [(w, w ^ (2 * gap)) for w in range(owners)])

    gap = 1
    while gap < nodes:
        reach = min(4, nodes // gap)
        low = jnp.concatenate([low] + [from_node(low, gap * k) for k in range(1, reach)], axis=0)
        gap *= reach

    order_of = [0] + [s * k for k in range(1, far) for s in (-1, 1)] + [far]
    of_result = [nodes - 3, 2, 1]

    def total(shift):
        index = [s % nodes for s in order_of].index(shift)
        for values, sib, size in zip(results, sibs, of_result):
            if index < size:
                return (values[0][index] + sib[index]).reshape(1, group_rows, width)
            index -= size

    def over_mp(shifts):
        pairs = [(flags[s : s + 1], total(s), total(s + far)) for s in shifts]
        sent = jnp.concatenate([jnp.where(f, b, a).astype(bf16) for f, a, b in pairs], axis=0)
        got = lax.ppermute(sent, INNER, SWAP)
        return [jnp.where(f, a, b) for f, a, b in pairs], got

    kept_more, got_more = over_mp(list(range(1, far)))
    low, got_more, results[2] = lax.optimization_barrier((low, got_more, results[2]))
    kept_one, got_one = over_mp([0])

    own_low = jnp.dot(spots, low.reshape(owners * half, rank), preferred_element_type=f32)
    spread = jnp.dot(own_low.astype(bf16), copies, preferred_element_type=f32).astype(bf16) * mask
    out = jnp.dot(spread, second, preferred_element_type=f32).reshape(own_nodes, group_rows, width)
    for pair, value in enumerate(kept_more, 1):
        value = value + got_more[pair - 1 : pair].astype(f32)
        out = out + jnp.where(places[pair][:, None, None], value, 0)
    value = kept_one[0] + got_one.astype(f32)
    out = out + jnp.where(places[0][:, None, None], value, 0)
    return out.astype(bf16).reshape(-1, width)


def solution(mesh):
    shape = dict(mesh.shape)
    wide, inner = shape["wide"], shape["mp"] * shape["sub"]
    paired = shape["sub"] == 1 and inner == 2 and wide % 8 == 0 and wide & (wide - 1) == 0
    if paired:
        nodes = wide // 2
        order = ring_order(nodes)
        paired = all(
            (order[p] < nodes // 2) != (order[(p + nodes // 2) % nodes] < nodes // 2)
            for p in range(nodes)
        )
    return jax.shard_map(
        ringed if paired else gathered,
        mesh=mesh,
        in_specs=(
            P(("groups", "wide"), ("mp", "sub")),
            P(("groups", "wide"), ("mp", "sub")),
            P(("mp", "sub"), "wide"),
            P("wide", None, ("mp", "sub")),
            P(None, ("mp", "sub"), "wide"),
            P("groups", None),
            P(),
        ),
        out_specs=P(("groups", "mp", "sub"), "wide"),
        check_vma=False,
    )
```

```python
import functools

import jax
import jax.numpy as jnp
import numpy as np
from jax import lax
from jax.experimental import pallas as pl
from jax.experimental.pallas import tpu as pltpu
from jax.sharding import PartitionSpec as P

MOST = 2
INNER = ("mp", "sub")
SWAP = [(0, 1), (1, 0)]


def accumulate(pieces, tables, sums=(), lows=()):
    depth, width = pieces[0].shape[1], tables[0].shape[1]
    rank = (tables[0].shape[0] - depth) * width // depth
    for total in (*sums, *lows):
        total[...] = jnp.zeros_like(total)
    for index in range(depth // width):
        here = slice(index * width, (index + 1) * width)
        rows = jnp.concatenate([piece[:, here] for piece in pieces], axis=0)
        for table, total in zip(tables, sums):
            total[...] += jnp.dot(rows, table[here, :], preferred_element_type=jnp.float32)
        for table, total in zip(tables, lows):
            block = table[depth + index * rank : depth + (index + 1) * rank, :]
            total[...] += lax.dot_general(
                rows, block, (((1,), (1,)), ((), ())), preferred_element_type=jnp.float32
            )


def in_lanes(lane, total, index, height):
    first = total[2 * index * height : (2 * index + 1) * height]
    other = total[(2 * index + 1) * height : (2 * index + 2) * height]
    whole = jnp.concatenate([first, other], axis=0)
    turned = jnp.concatenate([other, first], axis=0)
    return jnp.where(lane == 0, whole, turned)


def compacted(choice, low):
    return jnp.dot(choice, low, precision=lax.Precision.HIGHEST, preferred_element_type=jnp.float32)


def early_kernel(count, facts, *refs):
    pieces, tables, choices = refs[:count], refs[count : count + 2], refs[count + 2]
    base, base_sib, compact = refs[count + 3 : count + 6]
    sums, lows = refs[count + 6 : count + 8], refs[count + 8 :]
    accumulate(pieces, tables, sums, lows)
    height = pieces[0].shape[0]
    for which, (out, total) in enumerate(zip((base, base_sib), sums)):
        for index in range(count // 2):
            out[index] = in_lanes(facts[0], total, index, height)
        compact[which] = compacted(choices[which], lows[which][...])


def share(flag, near, away, outs, pair):
    (near_own, near_sib), (away_own, away_sib) = near, away
    kept, to_sib, to_mp, to_both = outs
    kept[pair] = jnp.where(flag == 1, near_own, away_own)
    to_sib[pair] = jnp.where(flag == 1, near_sib, away_sib)
    to_mp[pair] = jnp.where(flag == 1, away_own, near_own).astype(to_mp.dtype)
    to_both[pair] = jnp.where(flag == 1, away_sib, near_sib).astype(to_both.dtype)


def middle_kernel(count, facts, *refs):
    pieces, tables = refs[:count], refs[count : count + 2]
    choices, compact_in, base, base_sib = refs[count + 2 : count + 6]
    outs, compact = refs[count + 6 : count + 10], refs[count + 10]
    sums, lows = refs[count + 11 : count + 13], refs[count + 13 :]
    accumulate(pieces, tables, sums, lows)
    height = pieces[0].shape[0]
    fresh = [[in_lanes(facts[0], total, index, height) for total in sums] for index in (0, 1)]
    pairs = outs[0].shape[0]
    for pair in range(pairs):
        step = pair + 1
        near = fresh[1] if step == pairs else (base[2 * step], base_sib[2 * step])
        back = pairs + 1 - step
        away = fresh[0] if back == pairs else (base[2 * back - 1], base_sib[2 * back - 1])
        share(facts[2 + step], near, away, outs, pair)
    for which, total in enumerate(lows):
        compact[which] = compact_in[which] + compacted(choices[which], total[...])


def low_kernel(facts, piece, other, table, table_sib, choices, compact_in, kept, sent, *lows):
    accumulate((piece, other), (table, table_sib), (), lows)
    half = kept.shape[1]
    for which, total in enumerate(lows):
        compact = compact_in[which] + compacted(choices[which], total[...])
        kept[which] = jnp.where(facts[1] == 0, compact[:half], compact[half:])
        sent[which] = jnp.where(facts[1] == 0, compact[half:], compact[:half])


def last_kernel(facts, piece, other, table, table_sib, base, base_sib, *refs):
    outs, sums = refs[:4], refs[4:]
    accumulate((piece, other), (table, table_sib), sums)
    away = [in_lanes(facts[0], total, 0, piece.shape[0]) for total in sums]
    share(facts[2], (base[0], base_sib[0]), away, outs, 0)


def kernel_call(kernel, facts, arrays, shapes, scratch, flops):
    in_vmem = pl.BlockSpec(memory_space=pltpu.VMEM)
    return pl.pallas_call(
        kernel,
        in_specs=[pl.BlockSpec(memory_space=pltpu.SMEM)] + [in_vmem] * len(arrays),
        out_specs=[in_vmem] * len(shapes),
        out_shape=[jax.ShapeDtypeStruct(shape, kind) for shape, kind in shapes],
        scratch_shapes=[pltpu.VMEM(shape, jnp.float32) for shape in scratch for _ in (0, 1)],
        compiler_params=pltpu.CompilerParams(vmem_limit_bytes=16 * 2**20),
        cost_estimate=pl.CostEstimate(flops=flops, bytes_accessed=flops // 64, transcendentals=0),
    )(facts, *arrays)


def hidden_of(gate, up):
    return (jax.nn.silu(gate.astype(jnp.float32)) * up.astype(jnp.float32)).astype(jnp.bfloat16)


def slots_of(row_adapter_index, adapter_storage_slot):
    names = jnp.arange(adapter_storage_slot.shape[0], dtype=jnp.int32)
    same = row_adapter_index == names[None, :]
    return jnp.sum(jnp.where(same, adapter_storage_slot[None, :], 0), axis=1)


def gathered(
    gate_activation,
    up_activation,
    down_base_weight,
    first_factor_table,
    second_factor_table,
    row_adapter_index,
    adapter_storage_slot,
):
    hidden = hidden_of(gate_activation, up_activation)
    row_count = hidden.shape[0]
    owners = lax.axis_size("wide")
    local_adapter = first_factor_table.shape[0]
    slots = local_adapter * owners
    rank_portion = second_factor_table.shape[1]
    home = lax.axis_index("wide")
    slot_all = slots_of(row_adapter_index, adapter_storage_slot)
    blocks = slot_all.reshape(owners, row_count)
    order = jnp.arange(row_count, dtype=jnp.int32)
    earlier = (blocks[:, :, None] == blocks[:, None, :]) & (order[None, :] < order[:, None])
    position = jnp.sum(earlier.astype(jnp.int32), axis=2)
    rows = lax.all_gather(hidden, "wide", axis=0, tiled=True)
    base = jnp.dot(rows, down_base_weight, preferred_element_type=jnp.float32)
    low = jnp.einsum("re,nqe->nrq", rows, first_factor_table, preferred_element_type=jnp.float32)
    low = low.reshape(local_adapter, owners, row_count, low.shape[2])
    own = home * local_adapter + jnp.arange(local_adapter, dtype=jnp.int32)
    kept = []
    for item in range(MOST):
        mask = (blocks[None] == own[:, None, None]) & (position == item)[None]
        kept.append(jnp.sum(jnp.where(mask[..., None], low, 0), axis=2))
    low = lax.psum_scatter(jnp.stack(kept, axis=2), INNER, scatter_dimension=3, tiled=True)
    low = lax.all_gather(low.astype(jnp.bfloat16), "wide", axis=0, tiled=True)
    spread = 0
    for item in range(MOST):
        mask = (blocks[None] == jnp.arange(slots, dtype=jnp.int32)[:, None, None]) & (position == item)
        spread += jnp.where(mask[..., None], low[:, :, item][:, :, None], 0)
    spread = spread.reshape(slots, owners * row_count, rank_portion)
    delta = jnp.einsum("srq,sqw->rw", spread, second_factor_table, preferred_element_type=jnp.float32)
    total = base + delta
    return lax.psum_scatter(total, INNER, scatter_dimension=0, tiled=True).astype(jnp.bfloat16)


def ring_order(nodes):
    return list(range(0, nodes, 2)) + list(range(nodes - 1, 0, -2))


def ringed(
    gate_activation,
    up_activation,
    down_base_weight,
    first_factor_table,
    second_factor_table,
    row_adapter_index,
    adapter_storage_slot,
):
    f32, bf16 = jnp.float32, jnp.bfloat16
    row_count, width_part = gate_activation.shape
    owners = lax.axis_size("wide")
    nodes = owners // 2
    far = nodes // 2
    steps = far - 1
    own_nodes = nodes // 2
    own_blocks = owners // 2
    group_rows = 2 * row_count
    order = ring_order(nodes)
    depth = width_part // 2
    width = down_base_weight.shape[1]
    rank = first_factor_table.shape[1]

    table = []
    for w in range(owners):
        p = order.index(w // 2)
        at = lambda shift: order[(p + shift) % nodes]
        arrivals = [at(0)] + [at(s * k) for k in range(1, far) for s in (-1, 1)] + [at(far)]
        row = [2 * node + (w % 2 ^ side) for node in arrivals for side in (0, 1)]
        for half in (0, 1):
            here = [(at(s) < own_nodes) == (half == 0) for s in range(far)]
            row += [int(h) for h in here]
            row += [at(s if h else s + far) % own_nodes for s, h in enumerate(here)]
        table.append(row)
    home = lax.axis_index("wide")
    part = lax.axis_index(INNER)
    side = jnp.bitwise_and(home, 1)

    def moved(shift, cross=0):
        return [
            (order[p] * 2 + c, order[(p + shift) % nodes] * 2 + (c ^ cross))
            for p in range(nodes)
            for c in (0, 1)
        ]

    def send(value, shift, cross=0):
        return lax.ppermute(value, "wide", moved(shift, cross))

    def half_of(value, which, axis):
        return lax.dynamic_slice_in_dim(value, which * depth, depth, axis)

    crossed = [(2 * w + m, 2 * (w ^ 1) + (1 - m)) for w in range(owners) for m in (0, 1)]

    def to_three(to_sib, to_mp, to_both):
        return (
            send(to_sib, 0, 1),
            lax.ppermute(to_mp, INNER, SWAP),
            lax.ppermute(to_both, ("wide",) + INNER, crossed),
        )

    keep = hidden_of(half_of(gate_activation, side, 1), half_of(up_activation, side, 1))
    give = hidden_of(half_of(gate_activation, 1 - side, 1), half_of(up_activation, 1 - side, 1))
    right = [send(keep, 1), send(give, 1, 1)]
    left = [send(keep, -1), send(give, -1, 1)]
    twin = send(give, 0, 1)

    def joined(which):
        first = half_of(first_factor_table[0], which, 1).reshape(rank, depth // width, width)
        first = jnp.swapaxes(first, 0, 1).reshape(-1, width)
        return jnp.concatenate([half_of(down_base_weight, which, 0), first], axis=0)

    own_table, sib_table = joined(side), joined(1 - side)
    own_table, sib_table, twin, right, left = lax.optimization_barrier(
        (own_table, sib_table, twin, right, left)
    )
    sib_table = send(sib_table, 0, 1)
    home_late, row_adapter_index, second_factor_table, sib_table = lax.optimization_barrier(
        (home, row_adapter_index, second_factor_table, sib_table)
    )
    tables = [own_table, sib_table]

    pieces = [keep, twin] + right + left
    for step in range(2, steps + 1):
        right = [send(block, 1) for block in right]
        left = [send(block, -1) for block in left]
        if step < steps:
            right, left = lax.optimization_barrier((right, left))
            pieces += right + left

    row = lax.dynamic_index_in_dim(
        jnp.asarray(np.array(table, np.int32)), home_late, 0, keepdims=False
    )
    edges = np.cumsum([0, 2 * nodes, far, far, far, far])
    arrived, *rest = [row[a:b] for a, b in zip(edges[:-1], edges[1:])]
    flags = jnp.where(part == 0, rest[0], rest[2])
    facts = jnp.concatenate([side[None], part[None].astype(jnp.int32), flags])
    target = jnp.where(part == 0, rest[1], rest[3])
    places = target[:, None] == jnp.arange(own_nodes, dtype=jnp.int32)[None, :]
    slot_all = slots_of(row_adapter_index, adapter_storage_slot).reshape(owners, row_count)
    ranks = jnp.arange(row_count, dtype=jnp.int32)
    earlier = (slot_all[:, :, None] == slot_all[:, None, :]) & (ranks[None, :] < ranks[:, None])
    position = jnp.sum(earlier.astype(jnp.int32), axis=2)
    blocks = jnp.arange(owners, dtype=jnp.int32)

    items = jnp.arange(owners * MOST, dtype=jnp.int32)
    came = arrived[:, None] == blocks[None, :]
    slot_came = jnp.sum(jnp.where(came[:, :, None], slot_all[None], 0), axis=1).reshape(1, -1)
    place_came = jnp.sum(
        jnp.where(came[:, :, None], position[None] + MOST * blocks[None, :, None], 0), axis=1
    ).reshape(1, -1)
    chosen = jnp.stack(
        [
            ((place_came == items[:, None]) & (slot_came == slot)).astype(f32)
            for slot in (home_late, jnp.bitwise_xor(home_late, 1))
        ]
    )
    early_rows = len(pieces) * row_count
    middle_rows = early_rows + 4 * row_count
    choices = [
        chosen[:, :, :early_rows],
        chosen[:, :, early_rows:middle_rows],
        chosen[:, :, middle_rows:],
    ]

    half = own_blocks * MOST
    here = own_blocks * row_count
    slot_here = lax.dynamic_slice_in_dim(slot_all, part * own_blocks, own_blocks).reshape(here, 1)
    position_here = lax.dynamic_slice_in_dim(position, part * own_blocks, own_blocks)
    block_here = jnp.arange(here, dtype=jnp.int32)[:, None] // row_count
    spot = (
        jnp.bitwise_xor(slot_here, home_late) * half
        + block_here * MOST
        + position_here.reshape(here, 1)
    )
    spots = (spot == jnp.arange(owners * half, dtype=jnp.int32)[None, :]).astype(bf16)
    column = jnp.arange(owners * rank, dtype=jnp.int32)[None, :]
    piece = rank // 2
    own_rank = jnp.bitwise_xor(part, column // (owners * piece)) * piece + column % piece
    mask = (slot_here == column // piece % owners).astype(bf16)
    copies = (jnp.arange(rank, dtype=jnp.int32)[:, None] == own_rank).astype(bf16)

    other = lax.ppermute(second_factor_table, INNER, SWAP)
    second = jnp.concatenate(
        [values.reshape(owners * piece, width) for values in (second_factor_table, other)], axis=0
    )

    def flops(rows, columns):
        return rows * depth * columns // 16

    count = len(pieces)
    early = kernel_call(
        functools.partial(early_kernel, count),
        facts,
        (*pieces, *tables, choices[0]),
        [((count // 2, group_rows, width), f32)] * 2 + [((2, owners * MOST, rank), f32)],
        [(early_rows, width), (early_rows, rank)],
        flops(early_rows, width + rank),
    )
    ready = (facts, spots, mask, copies, choices, places)
    right, left, early, ready = lax.optimization_barrier((right, left, early, ready))
    facts, spots, mask, copies, choices, places = ready

    last = [send(right[0], 1), send(left[1], -1)]

    def shares(pairs):
        shape = (pairs, group_rows, width)
        return [(shape, f32)] * 2 + [(shape, bf16)] * 2

    *middle, compact = kernel_call(
        functools.partial(middle_kernel, 4),
        facts,
        (*right, *left, *tables, choices[1], early[2], early[0], early[1]),
        shares(far - 1) + [((2, owners * MOST, rank), f32)],
        [(4 * row_count, width), (4 * row_count, rank)],
        flops(4 * row_count, width + rank),
    )
    kept_more = middle[0]
    got_more = to_three(*middle[1:])
    last, compact, second = lax.optimization_barrier((last, compact, second))

    kept, sent = kernel_call(
        low_kernel,
        facts,
        (*last, *tables, choices[2], compact),
        [((2, half, rank), f32)] * 2,
        [(group_rows, rank)],
        flops(group_rows, rank),
    )
    got = to_three(kept, sent, sent)
    got, last = lax.optimization_barrier((got, last))

    kept_one, *one = kernel_call(
        last_kernel,
        facts,
        (*last, *tables, early[0], early[1]),
        shares(1),
        [(group_rows, width)],
        flops(group_rows, width),
    )
    got_one = to_three(*one)

    low = (kept + got[1] + (got[0] + got[2])[::-1]).astype(bf16)

    def from_node(value, gap):
        return lax.ppermute(value, "wide", [(w, w ^ (2 * gap)) for w in range(owners)])

    gap = 1
    while gap < nodes:
        reach = min(4, nodes // gap)
        low = jnp.concatenate([low] + [from_node(low, gap * k) for k in range(1, reach)], axis=0)
        gap *= reach

    more = kept_more + got_more[0] + got_more[1].astype(f32) + got_more[2].astype(f32)
    rows = 0
    for pair in range(1, far):
        rows = rows + jnp.where(places[pair][:, None, None], more[pair - 1 : pair], 0)
    own_low = jnp.dot(spots, low.reshape(owners * half, rank), preferred_element_type=f32)
    spread = jnp.dot(own_low.astype(bf16), copies, preferred_element_type=f32).astype(bf16) * mask
    delta = jnp.dot(spread, second, preferred_element_type=f32)
    one = kept_one + got_one[0] + got_one[1].astype(f32) + got_one[2].astype(f32)
    rows = rows + jnp.where(places[0][:, None, None], one, 0)
    return (delta + rows.reshape(-1, width)).astype(bf16)


def solution(mesh):
    shape = dict(mesh.shape)
    wide, inner = shape["wide"], shape["mp"] * shape["sub"]
    paired = shape["sub"] == 1 and inner == 2 and wide % 8 == 0 and wide & (wide - 1) == 0
    if paired:
        nodes = wide // 2
        order = ring_order(nodes)
        paired = all(
            (order[p] < nodes // 2) != (order[(p + nodes // 2) % nodes] < nodes // 2)
            for p in range(nodes)
        )
    return jax.shard_map(
        ringed if paired else gathered,
        mesh=mesh,
        in_specs=(
            P(("groups", "wide"), ("mp", "sub")),
            P(("groups", "wide"), ("mp", "sub")),
            P(("mp", "sub"), "wide"),
            P("wide", None, ("mp", "sub")),
            P(None, ("mp", "sub"), "wide"),
            P("groups", None),
            P(),
        ),
        out_specs=P(("groups", "mp", "sub"), "wide"),
        check_vma=False,
    )
```

```python
import functools

import jax
import jax.numpy as jnp
import numpy as np
from jax import lax
from jax.experimental import pallas as pl
from jax.experimental.pallas import tpu as pltpu
from jax.sharding import PartitionSpec as P

MOST = 2
INNER = ("mp", "sub")
SWAP = [(0, 1), (1, 0)]


def tile_of(depth, most=1024):
    parts = 1
    while depth % parts or (depth // parts) % 128 or depth // parts > most:
        parts += 1
    return depth // parts


def started(sources, places, ready):
    copies = []
    for index, (source, place) in enumerate(zip(sources, places)):
        copies.append(pltpu.make_async_copy(source, place, ready.at[index]))
        copies[-1].start()
    return copies


def weight_copies(lane, weights, held, ready):
    tiles, tile = held.shape[1:3]
    first = pl.multiple_of(lane * tiles * tile, 128)
    sources = [w.at[pl.ds(first + i * tile, tile)] for i in range(tiles) for w in weights]
    places = [held.at[which, i] for i in range(tiles) for which in (0, 1)]
    return started(sources, places, ready)


def factor_copies(lane, factors, held, ready):
    rank, depth = held.shape[1:]
    first = pl.multiple_of(lane * depth, 128)
    sources = [f.at[:, pl.ds(first, depth)] for f in factors]
    return started(sources, [held.at[which] for which in (0, 1)], ready)


def weight_products(pieces, copies, held, sums):
    tiles, tile = held.shape[1:3]
    for total in sums:
        total[...] = jnp.zeros_like(total)
    for index in range(tiles):
        here = slice(index * tile, (index + 1) * tile)
        rows = jnp.concatenate([piece[:, here] for piece in pieces], axis=0)
        for which, total in enumerate(sums):
            copies[2 * index + which].wait()
            total[...] += jnp.dot(rows, held[which, index], preferred_element_type=jnp.float32)


def factor_products(pieces, copies, held, low):
    rank, depth = held.shape[1:]
    tile = tile_of(depth)
    low[...] = jnp.zeros_like(low)
    for copy in copies:
        copy.wait()

    def step(index, carry):
        here = pl.ds(pl.multiple_of(index * tile, 128), tile)
        rows = jnp.concatenate([piece[:, here] for piece in pieces], axis=0)
        both = jnp.concatenate([held[which, :, here] for which in (0, 1)], axis=0)
        low[...] += lax.dot_general(
            rows, both, (((1,), (1,)), ((), ())), preferred_element_type=jnp.float32
        )
        return carry

    lax.fori_loop(0, depth // tile, step, 0)


def in_lanes(lane, total, index, height):
    first = total[2 * index * height : (2 * index + 1) * height]
    other = total[(2 * index + 1) * height : (2 * index + 2) * height]
    whole = jnp.concatenate([first, other], axis=0)
    turned = jnp.concatenate([other, first], axis=0)
    return jnp.where(lane == 0, whole, turned)


def compacted(choice, low):
    return jnp.dot(choice, low, precision=lax.Precision.HIGHEST, preferred_element_type=jnp.float32)


def early_kernel(count, facts, *refs):
    pieces, refs = refs[:count], refs[count:]
    weights, factors, choices = refs[:2], refs[2:4], refs[4]
    (base, base_sib, compact), refs = refs[5:8], refs[8:]
    sums, low, held, ready, held_low, ready_low = refs[:2], *refs[2:]
    rank = held_low.shape[1]
    in_flight = weight_copies(facts[0], weights, held, ready)
    in_flight_low = factor_copies(facts[0], factors, held_low, ready_low)
    weight_products(pieces, in_flight, held, sums)
    factor_products(pieces, in_flight_low, held_low, low)
    height = base.shape[1] // 2
    for which, (out, total) in enumerate(zip((base, base_sib), sums)):
        for index in range(out.shape[0]):
            out[index] = in_lanes(facts[0], total, index, height)
        compact[which] = compacted(choices[which], low[:, which * rank : (which + 1) * rank])


def share(flag, near, away, outs, pair):
    (near_own, near_sib), (away_own, away_sib) = near, away
    kept, to_sib, to_mp, to_both = outs
    kept[pair] = jnp.where(flag == 1, near_own, away_own)
    to_sib[pair] = jnp.where(flag == 1, near_sib, away_sib)
    to_mp[pair] = jnp.where(flag == 1, away_own, near_own).astype(to_mp.dtype)
    to_both[pair] = jnp.where(flag == 1, away_sib, near_sib).astype(to_both.dtype)


def middle_kernel(facts, piece, other, *refs):
    weights, factors = refs[:2], refs[2:4]
    (choices, compact_in, base, base_sib), refs = refs[4:8], refs[8:]
    outs, compact, refs = refs[:4], refs[4], refs[5:]
    sums, low, held, ready, held_low, ready_low = refs[:2], *refs[2:]
    rank = held_low.shape[1]
    in_flight = weight_copies(facts[0], weights, held, ready)
    in_flight_low = factor_copies(facts[0], factors, held_low, ready_low)
    weight_products((piece, other), in_flight, held, sums)
    factor_products((piece, other), in_flight_low, held_low, low)
    pairs, group = outs[0].shape[:2]
    fresh = [[in_lanes(facts[0], total, index, group // 2) for total in sums] for index in (0, 1)]
    for pair in range(pairs):
        step, back = pair + 1, pairs - pair
        near = fresh[1] if step == pairs else (base[2 * step], base_sib[2 * step])
        away = fresh[0] if back == pairs else (base[2 * back - 1], base_sib[2 * back - 1])
        share(facts[2 + step], near, away, outs, pair)
    for which in (0, 1):
        compact[which] = compact_in[which] + compacted(
            choices[which], low[:, which * rank : (which + 1) * rank]
        )


def low_kernel(facts, piece, other, *refs):
    factors, (choices, compact_in, kept, sent, low, held, ready) = refs[:2], refs[2:]
    rank, half = held.shape[1], kept.shape[1]
    factor_products((piece, other), factor_copies(facts[0], factors, held, ready), held, low)
    for which in (0, 1):
        compact = compact_in[which] + compacted(
            choices[which], low[:, which * rank : (which + 1) * rank]
        )
        kept[which] = jnp.where(facts[1] == 0, compact[:half], compact[half:])
        sent[which] = jnp.where(facts[1] == 0, compact[half:], compact[:half])


def last_kernel(facts, piece, other, *refs):
    weights, (base, base_sib), refs = refs[:2], refs[2:4], refs[4:]
    outs, sums, (held, ready) = refs[:4], refs[4:6], refs[6:]
    weight_products((piece, other), weight_copies(facts[0], weights, held, ready), held, sums)
    away = [in_lanes(facts[0], total, 0, piece.shape[0]) for total in sums]
    share(facts[2], (base[0], base_sib[0]), away, outs, 0)


def kernel_call(kernel, facts, rows, weights, factors, others, shapes):
    in_vmem, anywhere = pl.BlockSpec(memory_space=pltpu.VMEM), pl.BlockSpec(memory_space=pl.ANY)
    depth, total = rows[0].shape[1], sum(values.shape[0] for values in rows)
    tile = tile_of(depth)
    scratch, columns = [], 0
    if weights:
        width = weights[0].shape[1]
        columns += 2 * width
        scratch += [pltpu.VMEM((total, width), jnp.float32)] * 2
    if factors:
        rank = factors[0].shape[0]
        columns += 2 * rank
        scratch += [pltpu.VMEM((total, 2 * rank), jnp.float32)]
    if weights:
        scratch += [pltpu.VMEM((2, depth // tile, tile, width), jnp.bfloat16)]
        scratch += [pltpu.SemaphoreType.DMA((2 * depth // tile,))]
    if factors:
        scratch += [pltpu.VMEM((2, rank, depth), jnp.bfloat16), pltpu.SemaphoreType.DMA((2,))]
    return pl.pallas_call(
        kernel,
        in_specs=[pl.BlockSpec(memory_space=pltpu.SMEM)]
        + [in_vmem] * len(rows)
        + [anywhere] * (len(weights) + len(factors))
        + [in_vmem] * len(others),
        out_specs=[in_vmem] * len(shapes),
        out_shape=[jax.ShapeDtypeStruct(shape, kind) for shape, kind in shapes],
        scratch_shapes=scratch,
        compiler_params=pltpu.CompilerParams(vmem_limit_bytes=40 * 2**20),
        cost_estimate=pl.CostEstimate(
            flops=total * depth * columns // 32,
            bytes_accessed=depth * columns // 16,
            transcendentals=0,
        ),
    )(facts, *rows, *weights, *factors, *others)


def hidden_of(gate, up):
    return (jax.nn.silu(gate.astype(jnp.float32)) * up.astype(jnp.float32)).astype(jnp.bfloat16)


def slots_of(row_adapter_index, adapter_storage_slot):
    names = jnp.arange(adapter_storage_slot.shape[0], dtype=jnp.int32)
    same = row_adapter_index == names[None, :]
    return jnp.sum(jnp.where(same, adapter_storage_slot[None, :], 0), axis=1)


def gathered(
    gate_activation,
    up_activation,
    down_base_weight,
    first_factor_table,
    second_factor_table,
    row_adapter_index,
    adapter_storage_slot,
):
    hidden = hidden_of(gate_activation, up_activation)
    row_count = hidden.shape[0]
    owners = lax.axis_size("wide")
    local_adapter = first_factor_table.shape[0]
    slots = local_adapter * owners
    rank_portion = second_factor_table.shape[1]
    home = lax.axis_index("wide")
    slot_all = slots_of(row_adapter_index, adapter_storage_slot)
    blocks = slot_all.reshape(owners, row_count)
    order = jnp.arange(row_count, dtype=jnp.int32)
    earlier = (blocks[:, :, None] == blocks[:, None, :]) & (order[None, :] < order[:, None])
    position = jnp.sum(earlier.astype(jnp.int32), axis=2)
    rows = lax.all_gather(hidden, "wide", axis=0, tiled=True)
    base = jnp.dot(rows, down_base_weight, preferred_element_type=jnp.float32)
    low = jnp.einsum("re,nqe->nrq", rows, first_factor_table, preferred_element_type=jnp.float32)
    low = low.reshape(local_adapter, owners, row_count, low.shape[2])
    own = home * local_adapter + jnp.arange(local_adapter, dtype=jnp.int32)
    kept = []
    for item in range(MOST):
        mask = (blocks[None] == own[:, None, None]) & (position == item)[None]
        kept.append(jnp.sum(jnp.where(mask[..., None], low, 0), axis=2))
    low = lax.psum_scatter(jnp.stack(kept, axis=2), INNER, scatter_dimension=3, tiled=True)
    low = lax.all_gather(low.astype(jnp.bfloat16), "wide", axis=0, tiled=True)
    spread = 0
    for item in range(MOST):
        mask = (blocks[None] == jnp.arange(slots, dtype=jnp.int32)[:, None, None]) & (position == item)
        spread += jnp.where(mask[..., None], low[:, :, item][:, :, None], 0)
    spread = spread.reshape(slots, owners * row_count, rank_portion)
    delta = jnp.einsum("srq,sqw->rw", spread, second_factor_table, preferred_element_type=jnp.float32)
    total = base + delta
    return lax.psum_scatter(total, INNER, scatter_dimension=0, tiled=True).astype(jnp.bfloat16)


def ring_order(nodes):
    return list(range(0, nodes, 2)) + list(range(nodes - 1, 0, -2))


def ringed(
    gate_activation,
    up_activation,
    down_base_weight,
    first_factor_table,
    second_factor_table,
    row_adapter_index,
    adapter_storage_slot,
):
    f32, bf16 = jnp.float32, jnp.bfloat16
    row_count, width_part = gate_activation.shape
    owners = lax.axis_size("wide")
    nodes = owners // 2
    far = nodes // 2
    steps = far - 1
    own_nodes = nodes // 2
    own_blocks = owners // 2
    group_rows = 2 * row_count
    order = ring_order(nodes)
    depth = width_part // 2
    width = down_base_weight.shape[1]
    rank = first_factor_table.shape[1]

    table = []
    for w in range(owners):
        p = order.index(w // 2)
        at = lambda shift: order[(p + shift) % nodes]
        arrivals = [at(0)] + [at(s * k) for k in range(1, far) for s in (-1, 1)] + [at(far)]
        row = [2 * node + (w % 2 ^ side) for node in arrivals for side in (0, 1)]
        for half in (0, 1):
            here = [(at(s) < own_nodes) == (half == 0) for s in range(far)]
            row += [int(h) for h in here]
            row += [at(s if h else s + far) % own_nodes for s, h in enumerate(here)]
        table.append(row)
    home = lax.axis_index("wide")
    part = lax.axis_index(INNER)
    side = jnp.bitwise_and(home, 1)

    def moved(shift, cross=0):
        return [
            (order[p] * 2 + c, order[(p + shift) % nodes] * 2 + (c ^ cross))
            for p in range(nodes)
            for c in (0, 1)
        ]

    def send(value, shift, cross=0):
        return lax.ppermute(value, "wide", moved(shift, cross))

    def half_of(value, which, axis):
        return lax.dynamic_slice_in_dim(value, which * depth, depth, axis)

    crossed = [(2 * w + m, 2 * (w ^ 1) + (1 - m)) for w in range(owners) for m in (0, 1)]

    def to_three(to_sib, to_mp, to_both):
        return (
            send(to_sib, 0, 1),
            lax.ppermute(to_mp, INNER, SWAP),
            lax.ppermute(to_both, ("wide",) + INNER, crossed),
        )

    keep = hidden_of(half_of(gate_activation, side, 1), half_of(up_activation, side, 1))
    give = hidden_of(half_of(gate_activation, 1 - side, 1), half_of(up_activation, 1 - side, 1))
    block = jnp.concatenate([keep, send(give, 0, 1)], axis=0)
    right, left = send(block, 1), send(block, -1)

    weight, first, block = lax.optimization_barrier(
        (down_base_weight, first_factor_table[0], block)
    )
    weights = (weight, send(weight, 0, 1))
    factors = (first, send(first, 0, 1))
    home_late, row_adapter_index, second_factor_table, weights = lax.optimization_barrier(
        (home, row_adapter_index, second_factor_table, weights)
    )

    pieces = [block, right, left]
    for step in range(2, steps + 1):
        right, left = send(right, 1), send(left, -1)
        if step < steps:
            right, left = lax.optimization_barrier((right, left))
            pieces += [right, left]

    row = lax.dynamic_index_in_dim(
        jnp.asarray(np.array(table, np.int32)), home_late, 0, keepdims=False
    )
    edges = np.cumsum([0, 2 * nodes, far, far, far, far])
    arrived, *rest = [row[a:b] for a, b in zip(edges[:-1], edges[1:])]
    flags = jnp.where(part == 0, rest[0], rest[2])
    facts = jnp.concatenate([side[None], part[None].astype(jnp.int32), flags])
    target = jnp.where(part == 0, rest[1], rest[3])
    places = target[:, None] == jnp.arange(own_nodes, dtype=jnp.int32)[None, :]
    slot_all = slots_of(row_adapter_index, adapter_storage_slot).reshape(owners, row_count)
    ranks = jnp.arange(row_count, dtype=jnp.int32)
    earlier = (slot_all[:, :, None] == slot_all[:, None, :]) & (ranks[None, :] < ranks[:, None])
    position = jnp.sum(earlier.astype(jnp.int32), axis=2)
    blocks = jnp.arange(owners, dtype=jnp.int32)

    items = jnp.arange(owners * MOST, dtype=jnp.int32)
    came = arrived[:, None] == blocks[None, :]
    slot_came = jnp.sum(jnp.where(came[:, :, None], slot_all[None], 0), axis=1).reshape(1, -1)
    place_came = jnp.sum(
        jnp.where(came[:, :, None], position[None] + MOST * blocks[None, :, None], 0), axis=1
    ).reshape(1, -1)
    chosen = jnp.stack(
        [
            ((place_came == items[:, None]) & (slot_came == slot)).astype(f32)
            for slot in (home_late, jnp.bitwise_xor(home_late, 1))
        ]
    )
    early_rows = len(pieces) * group_rows
    middle_rows = early_rows + 4 * row_count
    choices = [
        chosen[:, :, :early_rows],
        chosen[:, :, early_rows:middle_rows],
        chosen[:, :, middle_rows:],
    ]

    half = own_blocks * MOST
    here = own_blocks * row_count
    slot_here = lax.dynamic_slice_in_dim(slot_all, part * own_blocks, own_blocks).reshape(here, 1)
    position_here = lax.dynamic_slice_in_dim(position, part * own_blocks, own_blocks)
    block_here = jnp.arange(here, dtype=jnp.int32)[:, None] // row_count
    spot = (
        jnp.bitwise_xor(slot_here, home_late) * half
        + block_here * MOST
        + position_here.reshape(here, 1)
    )
    spots = (spot == jnp.arange(owners * half, dtype=jnp.int32)[None, :]).astype(bf16)
    column = jnp.arange(owners * rank, dtype=jnp.int32)[None, :]
    piece = rank // 2
    own_rank = jnp.bitwise_xor(part, column // (owners * piece)) * piece + column % piece
    mask = (slot_here == column // piece % owners).astype(bf16)
    copies = (jnp.arange(rank, dtype=jnp.int32)[:, None] == own_rank).astype(bf16)

    other = lax.ppermute(second_factor_table, INNER, SWAP)
    second = jnp.concatenate(
        [values.reshape(owners * piece, width) for values in (second_factor_table, other)], axis=0
    )

    compact_shape = ((2, owners * MOST, rank), f32)
    early = kernel_call(
        functools.partial(early_kernel, len(pieces)),
        facts,
        pieces,
        weights,
        factors,
        (choices[0],),
        [((len(pieces), group_rows, width), f32)] * 2 + [compact_shape],
    )
    ready = (facts, spots, mask, copies, choices, places)
    right, left, early, ready = lax.optimization_barrier((right, left, early, ready))
    facts, spots, mask, copies, choices, places = ready

    last = [send(right[:row_count], 1), send(left[row_count:], -1)]

    def shares(pairs):
        shape = (pairs, group_rows, width)
        return [(shape, f32)] * 2 + [(shape, bf16)] * 2

    kept_more, *more, compact = kernel_call(
        middle_kernel,
        facts,
        (right, left),
        weights,
        factors,
        (choices[1], early[2], early[0], early[1]),
        shares(far - 1) + [compact_shape],
    )
    got_more = to_three(*more)
    last, compact, second = lax.optimization_barrier((last, compact, second))

    kept, sent = kernel_call(
        low_kernel, facts, last, (), factors, (choices[2], compact), [((2, half, rank), f32)] * 2
    )
    got = to_three(kept, sent, sent)
    got, last = lax.optimization_barrier((got, last))

    kept_one, *one = kernel_call(
        last_kernel, facts, last, weights, (), (early[0], early[1]), shares(1)
    )
    got_one = to_three(*one)

    low = (kept + got[1] + (got[0] + got[2])[::-1]).astype(bf16)

    def from_node(value, gap):
        return lax.ppermute(value, "wide", [(w, w ^ (2 * gap)) for w in range(owners)])

    gap = 1
    while gap < nodes:
        reach = min(4, nodes // gap)
        low = jnp.concatenate([low] + [from_node(low, gap * k) for k in range(1, reach)], axis=0)
        gap *= reach

    more = kept_more + got_more[0] + got_more[1].astype(f32) + got_more[2].astype(f32)
    rows = 0
    for pair in range(1, far):
        rows = rows + jnp.where(places[pair][:, None, None], more[pair - 1 : pair], 0)
    own_low = jnp.dot(spots, low.reshape(owners * half, rank), preferred_element_type=f32)
    spread = jnp.dot(own_low.astype(bf16), copies, preferred_element_type=f32).astype(bf16) * mask
    delta = jnp.dot(spread, second, preferred_element_type=f32)
    one = kept_one + got_one[0] + got_one[1].astype(f32) + got_one[2].astype(f32)
    rows = rows + jnp.where(places[0][:, None, None], one, 0)
    return (delta + rows.reshape(-1, width)).astype(bf16)


def solution(mesh):
    shape = dict(mesh.shape)
    wide, inner = shape["wide"], shape["mp"] * shape["sub"]
    paired = shape["sub"] == 1 and inner == 2 and wide % 8 == 0 and wide & (wide - 1) == 0
    if paired:
        nodes = wide // 2
        order = ring_order(nodes)
        paired = all(
            (order[p] < nodes // 2) != (order[(p + nodes // 2) % nodes] < nodes // 2)
            for p in range(nodes)
        )
    return jax.shard_map(
        ringed if paired else gathered,
        mesh=mesh,
        in_specs=(
            P(("groups", "wide"), ("mp", "sub")),
            P(("groups", "wide"), ("mp", "sub")),
            P(("mp", "sub"), "wide"),
            P("wide", None, ("mp", "sub")),
            P(None, ("mp", "sub"), "wide"),
            P("groups", None),
            P(),
        ),
        out_specs=P(("groups", "mp", "sub"), "wide"),
        check_vma=False,
    )
```

```python
import functools

import jax
import jax.numpy as jnp
import numpy as np
from jax import lax
from jax.experimental import pallas as pl
from jax.experimental.pallas import tpu as pltpu
from jax.sharding import PartitionSpec as P

MOST = 2
INNER = ("mp", "sub")
SWAP = [(0, 1), (1, 0)]


def tile_of(depth, most=1024):
    parts = 1
    while depth % parts or (depth // parts) % 128 or depth // parts > most:
        parts += 1
    return depth // parts


def started(sources, places, ready):
    copies = []
    for index, (source, place) in enumerate(zip(sources, places)):
        copies.append(pltpu.make_async_copy(source, place, ready.at[index]))
        copies[-1].start()
    return copies


def weight_copies(lane, weights, held, ready):
    tiles, tile = held.shape[1:3]
    first = pl.multiple_of(lane * tiles * tile, 128)
    sources = [w.at[pl.ds(first + i * tile, tile)] for i in range(tiles) for w in weights]
    places = [held.at[which, i] for i in range(tiles) for which in (0, 1)]
    return started(sources, places, ready)


def factor_copies(lane, factors, held, ready):
    rank, depth = held.shape[1:]
    first = pl.multiple_of(lane * depth, 128)
    sources = [f.at[:, pl.ds(first, depth)] for f in factors]
    return started(sources, [held.at[which] for which in (0, 1)], ready)


def weight_products(rows_of, copies, held, sums):
    tiles, tile = held.shape[1:3]
    for total in sums:
        total[...] = jnp.zeros_like(total)
    for index in range(tiles):
        rows = rows_of(slice(index * tile, (index + 1) * tile))
        for which, total in enumerate(sums):
            copies[2 * index + which].wait()
            total[...] += jnp.dot(rows, held[which, index], preferred_element_type=jnp.float32)


def factor_products(rows_of, copies, held, low):
    rank, depth = held.shape[1:]
    tile = tile_of(depth)
    low[...] = jnp.zeros_like(low)
    for copy in copies:
        copy.wait()

    def step(index, carry):
        here = pl.ds(pl.multiple_of(index * tile, 128), tile)
        both = jnp.concatenate([held[which, :, here] for which in (0, 1)], axis=0)
        low[...] += lax.dot_general(
            rows_of(here), both, (((1,), (1,)), ((), ())), preferred_element_type=jnp.float32
        )
        return carry

    lax.fori_loop(0, depth // tile, step, 0)


def in_lanes(lane, total, index, height):
    first = total[2 * index * height : (2 * index + 1) * height]
    other = total[(2 * index + 1) * height : (2 * index + 2) * height]
    whole = jnp.concatenate([first, other], axis=0)
    turned = jnp.concatenate([other, first], axis=0)
    return jnp.where(lane == 0, whole, turned)


def compacted(choice, low):
    high = low.astype(jnp.bfloat16)
    rest = low - high.astype(jnp.float32)
    middle = rest.astype(jnp.bfloat16)
    tail = (rest - middle.astype(jnp.float32)).astype(jnp.bfloat16)
    picked = jnp.dot(
        choice,
        jnp.concatenate([high, middle, tail], axis=1),
        preferred_element_type=jnp.float32,
    )
    size = low.shape[1]
    total = picked[:, :size] + (picked[:, size : 2 * size] + picked[:, 2 * size :])
    count, rank = choice.shape[0] // 2, size // 2
    return total[:count, :rank], total[count:, rank:]


def last_rows(lane, piece, other, here):
    return jnp.where(lane == 0, piece[:, here], other[:, here])


def early_kernel(count, facts, *refs):
    pieces, refs = refs[:count], refs[count:]
    weights, factors, choices = refs[:2], refs[2:4], refs[4]
    (base, base_sib, compact), refs = refs[5:8], refs[8:]
    sums, low, held, ready, held_low, ready_low = refs[:2], *refs[2:]
    rows_of = lambda here: jnp.concatenate([piece[:, here] for piece in pieces], axis=0)
    in_flight = weight_copies(facts[0], weights, held, ready)
    in_flight_low = factor_copies(facts[0], factors, held_low, ready_low)
    weight_products(rows_of, in_flight, held, sums)
    factor_products(rows_of, in_flight_low, held_low, low)
    height = base.shape[1] // 2
    for out, total in zip((base, base_sib), sums):
        for index in range(out.shape[0]):
            out[index] = in_lanes(facts[0], total, index, height)
    compact[0], compact[1] = compacted(choices[...], low[...])


def share(flag, near, away, outs, pair):
    (near_own, near_sib), (away_own, away_sib) = near, away
    kept, to_sib, to_mp, to_both = outs
    kept[pair] = jnp.where(flag == 1, near_own, away_own)
    to_sib[pair] = jnp.where(flag == 1, near_sib, away_sib)
    to_mp[pair] = jnp.where(flag == 1, away_own, near_own).astype(to_mp.dtype)
    to_both[pair] = jnp.where(flag == 1, away_sib, near_sib).astype(to_both.dtype)


def middle_kernel(facts, piece, other, *refs):
    weights, factors = refs[:2], refs[2:4]
    (choices, compact_in, base, base_sib), refs = refs[4:8], refs[8:]
    outs, compact, refs = refs[:4], refs[4], refs[5:]
    sums, low, held, ready, held_low, ready_low = refs[:2], *refs[2:]
    rows_of = lambda here: jnp.concatenate([piece[:, here], other[:, here]], axis=0)
    in_flight = weight_copies(facts[0], weights, held, ready)
    in_flight_low = factor_copies(facts[0], factors, held_low, ready_low)
    weight_products(rows_of, in_flight, held, sums)
    factor_products(rows_of, in_flight_low, held_low, low)
    pairs, group = outs[0].shape[:2]
    fresh = [[in_lanes(facts[0], total, index, group // 2) for total in sums] for index in (0, 1)]
    for pair in range(pairs):
        step, back = pair + 1, pairs - pair
        near = fresh[1] if step == pairs else (base[2 * step], base_sib[2 * step])
        away = fresh[0] if back == pairs else (base[2 * back - 1], base_sib[2 * back - 1])
        share(facts[2 + step], near, away, outs, pair)
    for which, fresh_low in enumerate(compacted(choices[...], low[...])):
        compact[which] = compact_in[which] + fresh_low


def low_kernel(facts, piece, other, *refs):
    factors, (choices, compact_in, kept, sent, low, held, ready) = refs[:2], refs[2:]
    half = kept.shape[1]
    rows_of = functools.partial(last_rows, facts[0], piece, other)
    factor_products(rows_of, factor_copies(facts[0], factors, held, ready), held, low)
    for which, fresh_low in enumerate(compacted(choices[...], low[...])):
        total = compact_in[which] + fresh_low
        kept[which] = jnp.where(facts[1] == 0, total[:half], total[half:])
        sent[which] = jnp.where(facts[1] == 0, total[half:], total[:half])


def last_kernel(facts, piece, other, *refs):
    weights, (base, base_sib), refs = refs[:2], refs[2:4], refs[4:]
    outs, sums, (held, ready) = refs[:4], refs[4:6], refs[6:]
    rows_of = functools.partial(last_rows, facts[0], piece, other)
    weight_products(rows_of, weight_copies(facts[0], weights, held, ready), held, sums)
    away = [in_lanes(facts[0], total, 0, piece.shape[0] // 2) for total in sums]
    share(facts[2], (base[0], base_sib[0]), away, outs, 0)


def kernel_call(kernel, facts, rows, total, weights, factors, others, shapes):
    in_vmem, anywhere = pl.BlockSpec(memory_space=pltpu.VMEM), pl.BlockSpec(memory_space=pl.ANY)
    depth = rows[0].shape[1]
    tile = tile_of(depth)
    scratch, columns = [], 0
    if weights:
        width = weights[0].shape[1]
        columns += 2 * width
        scratch += [pltpu.VMEM((total, width), jnp.float32)] * 2
    if factors:
        rank = factors[0].shape[0]
        columns += 2 * rank
        scratch += [pltpu.VMEM((total, 2 * rank), jnp.float32)]
    if weights:
        scratch += [pltpu.VMEM((2, depth // tile, tile, width), jnp.bfloat16)]
        scratch += [pltpu.SemaphoreType.DMA((2 * depth // tile,))]
    if factors:
        scratch += [pltpu.VMEM((2, rank, depth), jnp.bfloat16), pltpu.SemaphoreType.DMA((2,))]
    return pl.pallas_call(
        kernel,
        in_specs=[pl.BlockSpec(memory_space=pltpu.SMEM)]
        + [in_vmem] * len(rows)
        + [anywhere] * (len(weights) + len(factors))
        + [in_vmem] * len(others),
        out_specs=[in_vmem] * len(shapes),
        out_shape=[jax.ShapeDtypeStruct(shape, kind) for shape, kind in shapes],
        scratch_shapes=scratch,
        compiler_params=pltpu.CompilerParams(vmem_limit_bytes=40 * 2**20),
        cost_estimate=pl.CostEstimate(
            flops=total * depth * columns // 32,
            bytes_accessed=depth * columns // 16,
            transcendentals=0,
        ),
    )(facts, *rows, *weights, *factors, *others)


def hidden_of(gate, up):
    return (jax.nn.silu(gate.astype(jnp.float32)) * up.astype(jnp.float32)).astype(jnp.bfloat16)


def slots_of(row_adapter_index, adapter_storage_slot):
    names = jnp.arange(adapter_storage_slot.shape[0], dtype=jnp.int32)
    same = row_adapter_index == names[None, :]
    return jnp.sum(jnp.where(same, adapter_storage_slot[None, :], 0), axis=1)


def gathered(
    gate_activation,
    up_activation,
    down_base_weight,
    first_factor_table,
    second_factor_table,
    row_adapter_index,
    adapter_storage_slot,
):
    hidden = hidden_of(gate_activation, up_activation)
    row_count = hidden.shape[0]
    owners = lax.axis_size("wide")
    local_adapter = first_factor_table.shape[0]
    slots = local_adapter * owners
    rank_portion = second_factor_table.shape[1]
    home = lax.axis_index("wide")
    slot_all = slots_of(row_adapter_index, adapter_storage_slot)
    blocks = slot_all.reshape(owners, row_count)
    order = jnp.arange(row_count, dtype=jnp.int32)
    earlier = (blocks[:, :, None] == blocks[:, None, :]) & (order[None, :] < order[:, None])
    position = jnp.sum(earlier.astype(jnp.int32), axis=2)
    rows = lax.all_gather(hidden, "wide", axis=0, tiled=True)
    base = jnp.dot(rows, down_base_weight, preferred_element_type=jnp.float32)
    low = jnp.einsum("re,nqe->nrq", rows, first_factor_table, preferred_element_type=jnp.float32)
    low = low.reshape(local_adapter, owners, row_count, low.shape[2])
    own = home * local_adapter + jnp.arange(local_adapter, dtype=jnp.int32)
    kept = []
    for item in range(MOST):
        mask = (blocks[None] == own[:, None, None]) & (position == item)[None]
        kept.append(jnp.sum(jnp.where(mask[..., None], low, 0), axis=2))
    low = lax.psum_scatter(jnp.stack(kept, axis=2), INNER, scatter_dimension=3, tiled=True)
    low = lax.all_gather(low.astype(jnp.bfloat16), "wide", axis=0, tiled=True)
    spread = 0
    for item in range(MOST):
        mask = (blocks[None] == jnp.arange(slots, dtype=jnp.int32)[:, None, None]) & (position == item)
        spread += jnp.where(mask[..., None], low[:, :, item][:, :, None], 0)
    spread = spread.reshape(slots, owners * row_count, rank_portion)
    delta = jnp.einsum("srq,sqw->rw", spread, second_factor_table, preferred_element_type=jnp.float32)
    total = base + delta
    return lax.psum_scatter(total, INNER, scatter_dimension=0, tiled=True).astype(jnp.bfloat16)


def ring_order(nodes):
    return list(range(0, nodes, 2)) + list(range(nodes - 1, 0, -2))


def ringed(
    gate_activation,
    up_activation,
    down_base_weight,
    first_factor_table,
    second_factor_table,
    row_adapter_index,
    adapter_storage_slot,
):
    f32, bf16 = jnp.float32, jnp.bfloat16
    row_count, width_part = gate_activation.shape
    owners = lax.axis_size("wide")
    nodes = owners // 2
    far = nodes // 2
    steps = far - 1
    own_nodes = nodes // 2
    own_blocks = owners // 2
    group_rows = 2 * row_count
    order = ring_order(nodes)
    depth = width_part // 2
    width = down_base_weight.shape[1]
    rank = first_factor_table.shape[1]

    table = []
    for w in range(owners):
        p = order.index(w // 2)
        at = lambda shift: order[(p + shift) % nodes]
        arrivals = [at(0)] + [at(s * k) for k in range(1, far) for s in (-1, 1)] + [at(far)]
        row = [2 * node + (w % 2 ^ side) for node in arrivals for side in (0, 1)]
        for half in (0, 1):
            here = [(at(s) < own_nodes) == (half == 0) for s in range(far)]
            row += [int(h) for h in here]
            row += [at(s if h else s + far) % own_nodes for s, h in enumerate(here)]
        table.append(row)
    home = lax.axis_index("wide")
    part = lax.axis_index(INNER)
    side = jnp.bitwise_and(home, 1)

    def moved(shift, cross=0):
        return [
            (order[p] * 2 + c, order[(p + shift) % nodes] * 2 + (c ^ cross))
            for p in range(nodes)
            for c in (0, 1)
        ]

    def send(value, shift, cross=0):
        return lax.ppermute(value, "wide", moved(shift, cross))

    def half_of(value, which, axis):
        return lax.dynamic_slice_in_dim(value, which * depth, depth, axis)

    crossed = [(2 * w + m, 2 * (w ^ 1) + (1 - m)) for w in range(owners) for m in (0, 1)]

    def to_three(to_sib, to_mp, to_both):
        return (
            send(to_sib, 0, 1),
            lax.ppermute(to_mp, INNER, SWAP),
            lax.ppermute(to_both, ("wide",) + INNER, crossed),
        )

    keep = hidden_of(half_of(gate_activation, side, 1), half_of(up_activation, side, 1))
    give = hidden_of(half_of(gate_activation, 1 - side, 1), half_of(up_activation, 1 - side, 1))
    block = jnp.concatenate([keep, send(give, 0, 1)], axis=0)
    right, left = send(block, 1), send(block, -1)

    weight, first, block = lax.optimization_barrier(
        (down_base_weight, first_factor_table[0], block)
    )
    weights = (weight, send(weight, 0, 1))
    factors = (first, send(first, 0, 1))
    home_late, row_adapter_index, second_factor_table, weights = lax.optimization_barrier(
        (home, row_adapter_index, second_factor_table, weights)
    )

    pieces = [block, right, left]
    for step in range(2, steps + 1):
        right, left = send(right, 1), send(left, -1)
        if step < steps:
            right, left = lax.optimization_barrier((right, left))
            pieces += [right, left]

    row = lax.dynamic_index_in_dim(
        jnp.asarray(np.array(table, np.int32)), home_late, 0, keepdims=False
    )
    edges = np.cumsum([0, 2 * nodes, far, far, far, far])
    arrived, *rest = [row[a:b] for a, b in zip(edges[:-1], edges[1:])]
    flags = jnp.where(part == 0, rest[0], rest[2])
    facts = jnp.concatenate([side[None], part[None].astype(jnp.int32), flags])
    target = jnp.where(part == 0, rest[1], rest[3])
    places = target[:, None] == jnp.arange(own_nodes, dtype=jnp.int32)[None, :]
    slot_all = slots_of(row_adapter_index, adapter_storage_slot).reshape(owners, row_count)
    ranks = jnp.arange(row_count, dtype=jnp.int32)
    earlier = (slot_all[:, :, None] == slot_all[:, None, :]) & (ranks[None, :] < ranks[:, None])
    position = jnp.sum(earlier.astype(jnp.int32), axis=2)
    blocks = jnp.arange(owners, dtype=jnp.int32)

    items = jnp.arange(owners * MOST, dtype=jnp.int32)
    came = arrived[:, None] == blocks[None, :]
    slot_came = jnp.sum(jnp.where(came[:, :, None], slot_all[None], 0), axis=1).reshape(1, -1)
    place_came = jnp.sum(
        jnp.where(came[:, :, None], position[None] + MOST * blocks[None, :, None], 0), axis=1
    ).reshape(1, -1)
    chosen = jnp.concatenate(
        [
            ((place_came == items[:, None]) & (slot_came == slot)).astype(bf16)
            for slot in (home_late, jnp.bitwise_xor(home_late, 1))
        ],
        axis=0,
    )
    early_rows = len(pieces) * group_rows
    middle_rows = early_rows + 2 * group_rows
    choices = [
        chosen[:, :early_rows],
        chosen[:, early_rows:middle_rows],
        chosen[:, middle_rows:],
    ]

    half = own_blocks * MOST
    here = own_blocks * row_count
    slot_here = lax.dynamic_slice_in_dim(slot_all, part * own_blocks, own_blocks).reshape(here, 1)
    position_here = lax.dynamic_slice_in_dim(position, part * own_blocks, own_blocks)
    block_here = jnp.arange(here, dtype=jnp.int32)[:, None] // row_count
    spot = (
        jnp.bitwise_xor(slot_here, home_late) * half
        + block_here * MOST
        + position_here.reshape(here, 1)
    )
    spots = (spot == jnp.arange(owners * half, dtype=jnp.int32)[None, :]).astype(bf16)
    piece = rank // 2
    column = jnp.arange(owners * piece, dtype=jnp.int32)[None, :]
    mask = (slot_here == column // piece).astype(bf16)
    copies = [
        (jnp.arange(rank, dtype=jnp.int32)[:, None] == which * piece + column % piece).astype(bf16)
        for which in (part, 1 - part)
    ]

    seconds = [
        values.reshape(owners * piece, width)
        for values in (second_factor_table, lax.ppermute(second_factor_table, INNER, SWAP))
    ]

    compact_shape = ((2, owners * MOST, rank), f32)
    early = kernel_call(
        functools.partial(early_kernel, len(pieces)),
        facts,
        pieces,
        early_rows,
        weights,
        factors,
        (choices[0],),
        [((len(pieces), group_rows, width), f32)] * 2 + [compact_shape],
    )
    ready = (facts, spots, mask, copies, choices, places, seconds)
    right, left, early, ready = lax.optimization_barrier((right, left, early, ready))
    facts, spots, mask, copies, choices, places, seconds = ready

    last = [
        lax.ppermute(right, "wide", [(a, b) for a, b in moved(1) if a % 2 == 0]),
        lax.ppermute(left, "wide", [(a, b) for a, b in moved(-1) if a % 2 == 1]),
    ]

    def shares(pairs):
        shape = (pairs, group_rows, width)
        return [(shape, f32)] * 2 + [(shape, bf16)] * 2

    kept_more, *more, compact = kernel_call(
        middle_kernel,
        facts,
        (right, left),
        2 * group_rows,
        weights,
        factors,
        (choices[1], early[2], early[0], early[1]),
        shares(far - 1) + [compact_shape],
    )
    got_more = to_three(*more)
    last, compact = lax.optimization_barrier((last, compact))

    kept, sent = kernel_call(
        low_kernel,
        facts,
        last,
        group_rows,
        (),
        factors,
        (choices[2], compact),
        [((2, half, rank), f32)] * 2,
    )
    got = to_three(kept, sent, sent)

    kept_one, *one = kernel_call(
        last_kernel, facts, last, group_rows, weights, (), (early[0], early[1]), shares(1)
    )
    got, got_more, one = lax.optimization_barrier((got, got_more, one))
    got_one = to_three(*one)

    low = (kept + got[1] + (got[0] + got[2])[::-1]).astype(bf16)

    def from_node(value, gap):
        return lax.ppermute(value, "wide", [(w, w ^ (2 * gap)) for w in range(owners)])

    gap = 1
    while gap < nodes:
        reach = min(4, nodes // gap)
        low = jnp.concatenate([low] + [from_node(low, gap * k) for k in range(1, reach)], axis=0)
        gap *= reach

    more = kept_more + got_more[0] + got_more[1].astype(f32) + got_more[2].astype(f32)
    rows = 0
    for pair in range(1, far):
        rows = rows + jnp.where(places[pair][:, None, None], more[pair - 1 : pair], 0)
    own_low = jnp.dot(spots, low.reshape(owners * half, rank), preferred_element_type=f32)
    own_low = own_low.astype(bf16)
    delta = 0
    for copy, second in zip(copies, seconds):
        spread = jnp.dot(own_low, copy, preferred_element_type=f32).astype(bf16) * mask
        delta = delta + jnp.dot(spread, second, preferred_element_type=f32)
    one = kept_one + got_one[0] + got_one[1].astype(f32) + got_one[2].astype(f32)
    rows = rows + jnp.where(places[0][:, None, None], one, 0)
    return (delta + rows.reshape(-1, width)).astype(bf16)


def solution(mesh):
    shape = dict(mesh.shape)
    wide, inner = shape["wide"], shape["mp"] * shape["sub"]
    paired = shape["sub"] == 1 and inner == 2 and wide % 8 == 0 and wide & (wide - 1) == 0
    if paired:
        nodes = wide // 2
        order = ring_order(nodes)
        paired = all(
            (order[p] < nodes // 2) != (order[(p + nodes // 2) % nodes] < nodes // 2)
            for p in range(nodes)
        )
    return jax.shard_map(
        ringed if paired else gathered,
        mesh=mesh,
        in_specs=(
            P(("groups", "wide"), ("mp", "sub")),
            P(("groups", "wide"), ("mp", "sub")),
            P(("mp", "sub"), "wide"),
            P("wide", None, ("mp", "sub")),
            P(None, ("mp", "sub"), "wide"),
            P("groups", None),
            P(),
        ),
        out_specs=P(("groups", "mp", "sub"), "wide"),
        check_vma=False,
    )
```

```python
import functools

import jax
import jax.numpy as jnp
import numpy as np
from jax import lax
from jax.experimental import pallas as pl
from jax.experimental.pallas import tpu as pltpu
from jax.sharding import PartitionSpec as P

MOST = 2
INNER = ("mp", "sub")
SWAP = [(0, 1), (1, 0)]


def tile_of(depth, most=1024):
    parts = 1
    while depth % parts or (depth // parts) % 128 or depth // parts > most:
        parts += 1
    return depth // parts


def started(sources, places, ready):
    copies = []
    for index, (source, place) in enumerate(zip(sources, places)):
        copies.append(pltpu.make_async_copy(source, place, ready.at[index]))
        copies[-1].start()
    return copies


def weight_copies(lane, weights, held, ready):
    tiles, tile = held.shape[1:3]
    first = pl.multiple_of(lane * tiles * tile, 128)
    sources = [w.at[pl.ds(first + i * tile, tile)] for i in range(tiles) for w in weights]
    places = [held.at[which, i] for i in range(tiles) for which in (0, 1)]
    return started(sources, places, ready)


def factor_copies(lane, factors, held, ready):
    rank, depth = held.shape[1:]
    first = pl.multiple_of(lane * depth, 128)
    sources = [f.at[:, pl.ds(first, depth)] for f in factors]
    return started(sources, [held.at[which] for which in (0, 1)], ready)


def weight_products(rows_of, copies, held, sums):
    tiles, tile = held.shape[1:3]
    for total in sums:
        total[...] = jnp.zeros_like(total)
    for index in range(tiles):
        rows = rows_of(slice(index * tile, (index + 1) * tile))
        for which, total in enumerate(sums):
            copies[2 * index + which].wait()
            total[...] += jnp.dot(rows, held[which, index], preferred_element_type=jnp.float32)


def factor_products(rows_of, copies, held, low):
    rank, depth = held.shape[1:]
    tile = tile_of(depth)
    low[...] = jnp.zeros_like(low)
    for copy in copies:
        copy.wait()

    def step(index, carry):
        here = pl.ds(pl.multiple_of(index * tile, 128), tile)
        both = jnp.concatenate([held[which, :, here] for which in (0, 1)], axis=0)
        low[...] += lax.dot_general(
            rows_of(here), both, (((1,), (1,)), ((), ())), preferred_element_type=jnp.float32
        )
        return carry

    lax.fori_loop(0, depth // tile, step, 0)


def in_lanes(lane, total, index, height):
    first = total[2 * index * height : (2 * index + 1) * height]
    other = total[(2 * index + 1) * height : (2 * index + 2) * height]
    whole = jnp.concatenate([first, other], axis=0)
    turned = jnp.concatenate([other, first], axis=0)
    return jnp.where(lane == 0, whole, turned)


def compacted(choice, low):
    high = low.astype(jnp.bfloat16)
    rest = low - high.astype(jnp.float32)
    middle = rest.astype(jnp.bfloat16)
    tail = (rest - middle.astype(jnp.float32)).astype(jnp.bfloat16)
    picked = jnp.dot(
        choice,
        jnp.concatenate([high, middle, tail], axis=1),
        preferred_element_type=jnp.float32,
    )
    size = low.shape[1]
    total = picked[:, :size] + (picked[:, size : 2 * size] + picked[:, 2 * size :])
    count, rank = choice.shape[0] // 2, size // 2
    return total[:count, :rank], total[count:, rank:]


def last_rows(lane, piece, other, here):
    return jnp.where(lane == 0, piece[:, here], other[:, here])


def early_kernel(count, facts, *refs):
    pieces, refs = refs[:count], refs[count:]
    weights, factors, choices = refs[:2], refs[2:4], refs[4]
    (base, base_sib, compact), refs = refs[5:8], refs[8:]
    sums, low, held, ready, held_low, ready_low = refs[:2], *refs[2:]
    rows_of = lambda here: jnp.concatenate([piece[:, here] for piece in pieces], axis=0)
    in_flight = weight_copies(facts[0], weights, held, ready)
    in_flight_low = factor_copies(facts[0], factors, held_low, ready_low)
    weight_products(rows_of, in_flight, held, sums)
    factor_products(rows_of, in_flight_low, held_low, low)
    height = base.shape[1] // 2
    for out, total in zip((base, base_sib), sums):
        for index in range(out.shape[0]):
            out[index] = in_lanes(facts[0], total, index, height)
    compact[0], compact[1] = compacted(choices[...], low[...])


def share(flag, near, away, outs, pair):
    (near_own, near_sib), (away_own, away_sib) = near, away
    kept, to_sib, to_mp, to_both = outs
    kept[pair] = jnp.where(flag == 1, near_own, away_own)
    to_sib[pair] = jnp.where(flag == 1, near_sib, away_sib)
    to_mp[pair] = jnp.where(flag == 1, away_own, near_own).astype(to_mp.dtype)
    to_both[pair] = jnp.where(flag == 1, away_sib, near_sib).astype(to_both.dtype)


def middle_kernel(facts, piece, other, *refs):
    weights, factors = refs[:2], refs[2:4]
    (choices, compact_in, base, base_sib), refs = refs[4:8], refs[8:]
    (own, sib, compact), refs = refs[:3], refs[3:]
    sums, low, held, ready, held_low, ready_low = refs[:2], *refs[2:]
    outs = own.at[0], sib.at[0], own.at[1], sib.at[1]
    rows_of = lambda here: jnp.concatenate([piece[:, here], other[:, here]], axis=0)
    in_flight = weight_copies(facts[0], weights, held, ready)
    in_flight_low = factor_copies(facts[0], factors, held_low, ready_low)
    weight_products(rows_of, in_flight, held, sums)
    factor_products(rows_of, in_flight_low, held_low, low)
    pairs, group = own.shape[1:3]
    fresh = [[in_lanes(facts[0], total, index, group // 2) for total in sums] for index in (0, 1)]
    for pair in range(pairs):
        step, back = pair + 1, pairs - pair
        near = fresh[1] if step == pairs else (base[2 * step], base_sib[2 * step])
        away = fresh[0] if back == pairs else (base[2 * back - 1], base_sib[2 * back - 1])
        share(facts[2 + step], near, away, outs, pair)
    for which, fresh_low in enumerate(compacted(choices[...], low[...])):
        compact[which] = compact_in[which] + fresh_low


def low_kernel(facts, piece, other, *refs):
    factors, (choices, compact_in, kept, sent, low, held, ready) = refs[:2], refs[2:]
    half = kept.shape[1]
    rows_of = functools.partial(last_rows, facts[0], piece, other)
    factor_products(rows_of, factor_copies(facts[0], factors, held, ready), held, low)
    for which, fresh_low in enumerate(compacted(choices[...], low[...])):
        total = compact_in[which] + fresh_low
        kept[which] = jnp.where(facts[1] == 0, total[:half], total[half:])
        sent[which] = jnp.where(facts[1] == 0, total[half:], total[:half])


def last_kernel(facts, piece, other, *refs):
    weights, (base, base_sib), refs = refs[:2], refs[2:4], refs[4:]
    outs, sums, (held, ready) = refs[:4], refs[4:6], refs[6:]
    rows_of = functools.partial(last_rows, facts[0], piece, other)
    weight_products(rows_of, weight_copies(facts[0], weights, held, ready), held, sums)
    away = [in_lanes(facts[0], total, 0, piece.shape[0] // 2) for total in sums]
    share(facts[2], (base[0], base_sib[0]), away, outs, 0)


def kernel_call(kernel, facts, rows, total, weights, factors, others, shapes):
    in_vmem, anywhere = pl.BlockSpec(memory_space=pltpu.VMEM), pl.BlockSpec(memory_space=pl.ANY)
    depth = rows[0].shape[1]
    tile = tile_of(depth)
    scratch, columns = [], 0
    if weights:
        width = weights[0].shape[1]
        columns += 2 * width
        scratch += [pltpu.VMEM((total, width), jnp.float32)] * 2
    if factors:
        rank = factors[0].shape[0]
        columns += 2 * rank
        scratch += [pltpu.VMEM((total, 2 * rank), jnp.float32)]
    if weights:
        scratch += [pltpu.VMEM((2, depth // tile, tile, width), jnp.bfloat16)]
        scratch += [pltpu.SemaphoreType.DMA((2 * depth // tile,))]
    if factors:
        scratch += [pltpu.VMEM((2, rank, depth), jnp.bfloat16), pltpu.SemaphoreType.DMA((2,))]
    return pl.pallas_call(
        kernel,
        in_specs=[pl.BlockSpec(memory_space=pltpu.SMEM)]
        + [in_vmem] * len(rows)
        + [anywhere] * (len(weights) + len(factors))
        + [in_vmem] * len(others),
        out_specs=[in_vmem] * len(shapes),
        out_shape=[jax.ShapeDtypeStruct(shape, kind) for shape, kind in shapes],
        scratch_shapes=scratch,
        compiler_params=pltpu.CompilerParams(vmem_limit_bytes=(28 if weights else 8) * 2**20),
        cost_estimate=pl.CostEstimate(
            flops=total * depth * columns // 32,
            bytes_accessed=depth * columns // 16,
            transcendentals=0,
        ),
    )(facts, *rows, *weights, *factors, *others)


def hidden_of(gate, up):
    return (jax.nn.silu(gate.astype(jnp.float32)) * up.astype(jnp.float32)).astype(jnp.bfloat16)


def slots_of(row_adapter_index, adapter_storage_slot):
    names = jnp.arange(adapter_storage_slot.shape[0], dtype=jnp.int32)
    same = row_adapter_index == names[None, :]
    return jnp.sum(jnp.where(same, adapter_storage_slot[None, :], 0), axis=1)


def gathered(
    gate_activation,
    up_activation,
    down_base_weight,
    first_factor_table,
    second_factor_table,
    row_adapter_index,
    adapter_storage_slot,
):
    hidden = hidden_of(gate_activation, up_activation)
    row_count = hidden.shape[0]
    owners = lax.axis_size("wide")
    local_adapter = first_factor_table.shape[0]
    slots = local_adapter * owners
    rank_portion = second_factor_table.shape[1]
    home = lax.axis_index("wide")
    slot_all = slots_of(row_adapter_index, adapter_storage_slot)
    blocks = slot_all.reshape(owners, row_count)
    order = jnp.arange(row_count, dtype=jnp.int32)
    earlier = (blocks[:, :, None] == blocks[:, None, :]) & (order[None, :] < order[:, None])
    position = jnp.sum(earlier.astype(jnp.int32), axis=2)
    rows = lax.all_gather(hidden, "wide", axis=0, tiled=True)
    base = jnp.dot(rows, down_base_weight, preferred_element_type=jnp.float32)
    low = jnp.einsum("re,nqe->nrq", rows, first_factor_table, preferred_element_type=jnp.float32)
    low = low.reshape(local_adapter, owners, row_count, low.shape[2])
    own = home * local_adapter + jnp.arange(local_adapter, dtype=jnp.int32)
    kept = []
    for item in range(MOST):
        mask = (blocks[None] == own[:, None, None]) & (position == item)[None]
        kept.append(jnp.sum(jnp.where(mask[..., None], low, 0), axis=2))
    low = lax.psum_scatter(jnp.stack(kept, axis=2), INNER, scatter_dimension=3, tiled=True)
    low = lax.all_gather(low.astype(jnp.bfloat16), "wide", axis=0, tiled=True)
    spread = 0
    for item in range(MOST):
        mask = (blocks[None] == jnp.arange(slots, dtype=jnp.int32)[:, None, None]) & (position == item)
        spread += jnp.where(mask[..., None], low[:, :, item][:, :, None], 0)
    spread = spread.reshape(slots, owners * row_count, rank_portion)
    delta = jnp.einsum("srq,sqw->rw", spread, second_factor_table, preferred_element_type=jnp.float32)
    total = base + delta
    return lax.psum_scatter(total, INNER, scatter_dimension=0, tiled=True).astype(jnp.bfloat16)


def ring_order(nodes):
    return list(range(0, nodes, 2)) + list(range(nodes - 1, 0, -2))


def ringed(
    gate_activation,
    up_activation,
    down_base_weight,
    first_factor_table,
    second_factor_table,
    row_adapter_index,
    adapter_storage_slot,
):
    f32, bf16 = jnp.float32, jnp.bfloat16
    row_count, width_part = gate_activation.shape
    owners = lax.axis_size("wide")
    nodes = owners // 2
    far = nodes // 2
    steps = far - 1
    own_nodes = nodes // 2
    own_blocks = owners // 2
    group_rows = 2 * row_count
    order = ring_order(nodes)
    depth = width_part // 2
    width = down_base_weight.shape[1]
    rank = first_factor_table.shape[1]

    table = []
    for w in range(owners):
        p = order.index(w // 2)
        at = lambda shift: order[(p + shift) % nodes]
        arrivals = [at(0)] + [at(s * k) for k in range(1, far) for s in (-1, 1)] + [at(far)]
        row = [2 * node + (w % 2 ^ side) for node in arrivals for side in (0, 1)]
        for half in (0, 1):
            here = [(at(s) < own_nodes) == (half == 0) for s in range(far)]
            row += [int(h) for h in here]
            row += [at(s if h else s + far) % own_nodes for s, h in enumerate(here)]
        table.append(row)
    home = lax.axis_index("wide")
    part = lax.axis_index(INNER)
    side = jnp.bitwise_and(home, 1)

    def moved(shift, cross=0):
        return [
            (order[p] * 2 + c, order[(p + shift) % nodes] * 2 + (c ^ cross))
            for p in range(nodes)
            for c in (0, 1)
        ]

    def send(value, shift, cross=0):
        return lax.ppermute(value, "wide", moved(shift, cross))

    def half_of(value, which, axis):
        return lax.dynamic_slice_in_dim(value, which * depth, depth, axis)

    crossed = [(2 * w + m, 2 * (w ^ 1) + (1 - m)) for w in range(owners) for m in (0, 1)]

    def to_three(to_sib, to_mp, to_both):
        return (
            send(to_sib, 0, 1),
            lax.ppermute(to_mp, INNER, SWAP),
            lax.ppermute(to_both, ("wide",) + INNER, crossed),
        )

    keep = hidden_of(half_of(gate_activation, side, 1), half_of(up_activation, side, 1))
    give = hidden_of(half_of(gate_activation, 1 - side, 1), half_of(up_activation, 1 - side, 1))
    block = jnp.concatenate([keep, send(give, 0, 1)], axis=0)
    right, left = send(block, 1), send(block, -1)

    weight, first, second_factor_table, block = lax.optimization_barrier(
        (down_base_weight, first_factor_table[0], second_factor_table, block)
    )
    other_second = lax.ppermute(second_factor_table, INNER, SWAP)
    weights = (weight, send(weight, 0, 1))
    factors = (first, send(first, 0, 1))
    home_late, row_adapter_index, weights = lax.optimization_barrier(
        (home, row_adapter_index, weights)
    )

    pieces = [block, right, left]
    for step in range(2, steps + 1):
        right, left = send(right, 1), send(left, -1)
        if step < steps:
            right, left = lax.optimization_barrier((right, left))
            pieces += [right, left]

    row = lax.dynamic_index_in_dim(
        jnp.asarray(np.array(table, np.int32)), home_late, 0, keepdims=False
    )
    edges = np.cumsum([0, 2 * nodes, far, far, far, far])
    arrived, *rest = [row[a:b] for a, b in zip(edges[:-1], edges[1:])]
    flags = jnp.where(part == 0, rest[0], rest[2])
    facts = jnp.concatenate([side[None], part[None].astype(jnp.int32), flags])
    target = jnp.where(part == 0, rest[1], rest[3])
    places = target[:, None] == jnp.arange(own_nodes, dtype=jnp.int32)[None, :]
    slot_all = slots_of(row_adapter_index, adapter_storage_slot).reshape(owners, row_count)
    ranks = jnp.arange(row_count, dtype=jnp.int32)
    earlier = (slot_all[:, :, None] == slot_all[:, None, :]) & (ranks[None, :] < ranks[:, None])
    position = jnp.sum(earlier.astype(jnp.int32), axis=2)
    blocks = jnp.arange(owners, dtype=jnp.int32)

    items = jnp.arange(owners * MOST, dtype=jnp.int32)
    came = arrived[:, None] == blocks[None, :]
    slot_came = jnp.sum(jnp.where(came[:, :, None], slot_all[None], 0), axis=1).reshape(1, -1)
    place_came = jnp.sum(
        jnp.where(came[:, :, None], position[None] + MOST * blocks[None, :, None], 0), axis=1
    ).reshape(1, -1)
    chosen = jnp.concatenate(
        [
            ((place_came == items[:, None]) & (slot_came == slot)).astype(bf16)
            for slot in (home_late, jnp.bitwise_xor(home_late, 1))
        ],
        axis=0,
    )
    early_rows = len(pieces) * group_rows
    middle_rows = early_rows + 2 * group_rows
    choices = [
        chosen[:, :early_rows],
        chosen[:, early_rows:middle_rows],
        chosen[:, middle_rows:],
    ]

    half = own_blocks * MOST
    here = own_blocks * row_count
    slot_here = lax.dynamic_slice_in_dim(slot_all, part * own_blocks, own_blocks).reshape(here, 1)
    position_here = lax.dynamic_slice_in_dim(position, part * own_blocks, own_blocks)
    block_here = jnp.arange(here, dtype=jnp.int32)[:, None] // row_count
    spot = (
        jnp.bitwise_xor(slot_here, home_late) * half
        + block_here * MOST
        + position_here.reshape(here, 1)
    )
    spots = (spot == jnp.arange(owners * half, dtype=jnp.int32)[None, :]).astype(bf16)
    piece = rank // 2
    column = jnp.arange(owners * rank, dtype=jnp.int32)[None, :]
    own_rank = jnp.bitwise_xor(part, column // (owners * piece)) * piece + column % piece
    mask = (slot_here == column // piece % owners).astype(bf16)
    copies = (jnp.arange(rank, dtype=jnp.int32)[:, None] == own_rank).astype(bf16)

    second = jnp.concatenate(
        [values.reshape(owners * piece, width) for values in (second_factor_table, other_second)],
        axis=0,
    )

    compact_shape = ((2, owners * MOST, rank), f32)
    early = kernel_call(
        functools.partial(early_kernel, len(pieces)),
        facts,
        pieces,
        early_rows,
        weights,
        factors,
        (choices[0],),
        [((len(pieces), group_rows, width), f32)] * 2 + [compact_shape],
    )
    ready = (facts, spots, mask, copies, choices, places, second)
    right, left, early, ready = lax.optimization_barrier((right, left, early, ready))
    facts, spots, mask, copies, choices, places, second = ready

    last = [
        lax.ppermute(right, "wide", [(a, b) for a, b in moved(1) if a % 2 == 0]),
        lax.ppermute(left, "wide", [(a, b) for a, b in moved(-1) if a % 2 == 1]),
    ]

    def shares(pairs):
        shape = (pairs, group_rows, width)
        return [(shape, f32)] * 2 + [(shape, bf16)] * 2

    own_more, sib_more, compact = kernel_call(
        middle_kernel,
        facts,
        (right, left),
        2 * group_rows,
        weights,
        factors,
        (choices[1], early[2], early[0], early[1]),
        [((2, far - 1, group_rows, width), f32)] * 2 + [compact_shape],
    )
    last, compact = lax.optimization_barrier((last, compact))

    kept, sent = kernel_call(
        low_kernel,
        facts,
        last,
        group_rows,
        (),
        factors,
        (choices[2], compact),
        [((2, half, rank), f32)] * 2,
    )
    kept, sent, sib_more = lax.optimization_barrier((kept, sent, sib_more))
    got = to_three(kept, sent, sent)
    low = (kept + got[1] + (got[0] + got[2])[::-1]).astype(bf16)

    kept_more, out_more = [
        a + b for a, b in zip(own_more, send(sib_more, 0, 1))
    ]
    out_more = out_more.astype(bf16)

    def from_node(value, gap):
        return lax.ppermute(value, "wide", [(w, w ^ (2 * gap)) for w in range(owners)])

    def gather(value, gap, reach):
        parts = [from_node(value, gap * k) for k in range(1, reach)]
        return jnp.concatenate([value] + parts, axis=0)

    low, out_more, last = lax.optimization_barrier((low, out_more, last))
    got_more = lax.ppermute(out_more, INNER, SWAP)
    reach = min(4, nodes)
    low = gather(low, 1, reach)

    kept_one, *one = kernel_call(
        last_kernel, facts, last, group_rows, weights, (), (early[0], early[1]), shares(1)
    )
    low, one, got_more = lax.optimization_barrier((low, one, got_more))
    gap = reach
    while gap < nodes:
        low = gather(low, gap, 2)
        gap *= 2
    got_one = to_three(*one)

    more = kept_more + got_more.astype(f32)
    rows = 0
    for pair in range(1, far):
        rows = rows + jnp.where(places[pair][:, None, None], more[pair - 1 : pair], 0)
    own_low = jnp.dot(spots, low.reshape(owners * half, rank), preferred_element_type=f32)
    spread = jnp.dot(own_low.astype(bf16), copies, preferred_element_type=f32).astype(bf16) * mask
    delta = jnp.dot(spread, second, preferred_element_type=f32)
    one = kept_one + got_one[0] + got_one[1].astype(f32) + got_one[2].astype(f32)
    rows = rows + jnp.where(places[0][:, None, None], one, 0)
    return (delta + rows.reshape(-1, width)).astype(bf16)


def solution(mesh):
    shape = dict(mesh.shape)
    wide, inner = shape["wide"], shape["mp"] * shape["sub"]
    paired = shape["sub"] == 1 and inner == 2 and wide % 8 == 0 and wide & (wide - 1) == 0
    if paired:
        nodes = wide // 2
        order = ring_order(nodes)
        paired = all(
            (order[p] < nodes // 2) != (order[(p + nodes // 2) % nodes] < nodes // 2)
            for p in range(nodes)
        )
    return jax.shard_map(
        ringed if paired else gathered,
        mesh=mesh,
        in_specs=(
            P(("groups", "wide"), ("mp", "sub")),
            P(("groups", "wide"), ("mp", "sub")),
            P(("mp", "sub"), "wide"),
            P("wide", None, ("mp", "sub")),
            P(None, ("mp", "sub"), "wide"),
            P("groups", None),
            P(),
        ),
        out_specs=P(("groups", "mp", "sub"), "wide"),
        check_vma=False,
    )
```

```python
import functools

import jax
import jax.numpy as jnp
import numpy as np
from jax import lax
from jax.experimental import pallas as pl
from jax.experimental.pallas import tpu as pltpu
from jax.sharding import PartitionSpec as P

MOST = 2
INNER = ("mp", "sub")
SWAP = [(0, 1), (1, 0)]


def tile_of(depth, most=1024):
    parts = 1
    while depth % parts or (depth // parts) % 128 or depth // parts > most:
        parts += 1
    return depth // parts


def started(sources, places, ready):
    copies = []
    for index, (source, place) in enumerate(zip(sources, places)):
        copies.append(pltpu.make_async_copy(source, place, ready.at[index]))
        copies[-1].start()
    return copies


def weight_copies(lane, weights, held, ready):
    tiles, tile = held.shape[1:3]
    first = pl.multiple_of(lane * tiles * tile, 128)
    sources = [w.at[pl.ds(first + i * tile, tile)] for i in range(tiles) for w in weights]
    places = [held.at[which, i] for i in range(tiles) for which in (0, 1)]
    return started(sources, places, ready)


def factor_copies(lane, factors, held, ready):
    rank, depth = held.shape[0] // 2, held.shape[1]
    first = pl.multiple_of(lane * depth, 128)
    sources = [f.at[:, pl.ds(first, depth)] for f in factors]
    return started(sources, [held.at[pl.ds(which * rank, rank)] for which in (0, 1)], ready)


def weight_products(rows_of, copies, held, sums):
    tiles, tile = held.shape[1:3]
    for total in sums:
        total[...] = jnp.zeros_like(total)
    for index in range(tiles):
        rows = rows_of(slice(index * tile, (index + 1) * tile))
        for which, total in enumerate(sums):
            copies[2 * index + which].wait()
            total[...] += jnp.dot(rows, held[which, index], preferred_element_type=jnp.float32)


def factor_products(rows_of, copies, held, low):
    depth = held.shape[1]
    tile = tile_of(depth)
    low[...] = jnp.zeros_like(low)
    for copy in copies:
        copy.wait()

    def step(index, carry):
        here = pl.ds(pl.multiple_of(index * tile, 128), tile)
        low[...] += lax.dot_general(
            rows_of(here), held[:, here], (((1,), (1,)), ((), ())), preferred_element_type=jnp.float32
        )
        return carry

    lax.fori_loop(0, depth // tile, step, 0)


def in_lanes(lane, total, index, height):
    first = total[2 * index * height : (2 * index + 1) * height]
    other = total[(2 * index + 1) * height : (2 * index + 2) * height]
    whole = jnp.concatenate([first, other], axis=0)
    turned = jnp.concatenate([other, first], axis=0)
    return jnp.where(lane == 0, whole, turned)


def compacted(choice, low):
    high = low.astype(jnp.bfloat16)
    rest = low - high.astype(jnp.float32)
    middle = rest.astype(jnp.bfloat16)
    tail = (rest - middle.astype(jnp.float32)).astype(jnp.bfloat16)
    picked = jnp.dot(
        choice,
        jnp.concatenate([high, middle, tail], axis=1),
        preferred_element_type=jnp.float32,
    )
    size = low.shape[1]
    total = picked[:, :size] + (picked[:, size : 2 * size] + picked[:, 2 * size :])
    count, rank = choice.shape[0] // 2, size // 2
    return total[:count, :rank], total[count:, rank:]


def early_kernel(count, facts, *refs):
    pieces, refs = refs[:count], refs[count:]
    weights, factors, choices = refs[:2], refs[2:4], refs[4]
    (base, base_sib, compact), refs = refs[5:8], refs[8:]
    sums, low, held, ready, held_low, ready_low = refs[:2], *refs[2:]
    rows_of = lambda here: jnp.concatenate([piece[:, here] for piece in pieces], axis=0)
    in_flight = weight_copies(facts[0], weights, held, ready)
    in_flight_low = factor_copies(facts[0], factors, held_low, ready_low)
    weight_products(rows_of, in_flight, held, sums)
    factor_products(rows_of, in_flight_low, held_low, low)
    height = base.shape[1] // 2
    for out, total in zip((base, base_sib), sums):
        for index in range(out.shape[0]):
            out[index] = in_lanes(facts[0], total, index, height)
    compact[0], compact[1] = compacted(choices[...], low[...])


def share(flag, near, away, outs, pair):
    (near_own, near_sib), (away_own, away_sib) = near, away
    kept, to_sib, to_mp, to_both = outs
    kept[pair] = jnp.where(flag == 1, near_own, away_own)
    to_sib[pair] = jnp.where(flag == 1, near_sib, away_sib)
    to_mp[pair] = jnp.where(flag == 1, away_own, near_own).astype(to_mp.dtype)
    to_both[pair] = jnp.where(flag == 1, away_sib, near_sib).astype(to_both.dtype)


def middle_kernel(facts, piece, other, *refs):
    weights, factors = refs[:2], refs[2:4]
    (choices, compact_in, base, base_sib), refs = refs[4:8], refs[8:]
    (own, sib, compact), refs = refs[:3], refs[3:]
    sums, low, held, ready, held_low, ready_low = refs[:2], *refs[2:]
    outs = own.at[0], sib.at[0], own.at[1], sib.at[1]
    rows_of = lambda here: jnp.concatenate([piece[:, here], other[:, here]], axis=0)
    in_flight = weight_copies(facts[0], weights, held, ready)
    in_flight_low = factor_copies(facts[0], factors, held_low, ready_low)
    weight_products(rows_of, in_flight, held, sums)
    factor_products(rows_of, in_flight_low, held_low, low)
    pairs, group = own.shape[1:3]
    fresh = [[in_lanes(facts[0], total, index, group // 2) for total in sums] for index in (0, 1)]
    lane = facts[0]
    ahead = [jnp.where(lane == 0, b, a) for a, b in zip(*fresh)]
    behind = [jnp.where(lane == 0, a, b) for a, b in zip(*fresh)]
    for pair in range(pairs):
        step, back = pair + 1, pairs - pair
        near, away = 2 * step - lane, 2 * back - 1 + lane
        near = ahead if step == pairs else (base[near], base_sib[near])
        away = behind if back == pairs else (base[away], base_sib[away])
        share(facts[2 + step], near, away, outs, pair)
    for which, fresh_low in enumerate(compacted(choices[...], low[...])):
        compact[which] = compact_in[which] + fresh_low


def low_kernel(facts, piece, *refs):
    factors, (choices, compact_in, kept, sent, low, held, ready) = refs[:2], refs[2:]
    half = kept.shape[1]
    rows_of = lambda here: piece[:, here]
    factor_products(rows_of, factor_copies(facts[0], factors, held, ready), held, low)
    for which, fresh_low in enumerate(compacted(choices[...], low[...])):
        total = compact_in[which] + fresh_low
        kept[which] = jnp.where(facts[1] == 0, total[:half], total[half:])
        sent[which] = jnp.where(facts[1] == 0, total[half:], total[:half])


def last_kernel(facts, piece, *refs):
    weights, (base, base_sib), refs = refs[:2], refs[2:4], refs[4:]
    outs, sums, (held, ready) = refs[:4], refs[4:6], refs[6:]
    rows_of = lambda here: piece[:, here]
    weight_products(rows_of, weight_copies(facts[0], weights, held, ready), held, sums)
    away = [in_lanes(facts[0], total, 0, piece.shape[0] // 2) for total in sums]
    share(facts[2], (base[0], base_sib[0]), away, outs, 0)


def kernel_call(kernel, facts, rows, total, weights, factors, others, shapes):
    in_vmem, anywhere = pl.BlockSpec(memory_space=pltpu.VMEM), pl.BlockSpec(memory_space=pl.ANY)
    depth = rows[0].shape[1]
    tile = tile_of(depth)
    scratch, columns = [], 0
    if weights:
        width = weights[0].shape[1]
        columns += 2 * width
        scratch += [pltpu.VMEM((total, width), jnp.float32)] * 2
    if factors:
        rank = factors[0].shape[0]
        columns += 2 * rank
        scratch += [pltpu.VMEM((total, 2 * rank), jnp.float32)]
    if weights:
        scratch += [pltpu.VMEM((2, depth // tile, tile, width), jnp.bfloat16)]
        scratch += [pltpu.SemaphoreType.DMA((2 * depth // tile,))]
    if factors:
        scratch += [pltpu.VMEM((2 * rank, depth), jnp.bfloat16), pltpu.SemaphoreType.DMA((2,))]
    return pl.pallas_call(
        kernel,
        in_specs=[pl.BlockSpec(memory_space=pltpu.SMEM)]
        + [in_vmem] * len(rows)
        + [anywhere] * (len(weights) + len(factors))
        + [in_vmem] * len(others),
        out_specs=[in_vmem] * len(shapes),
        out_shape=[jax.ShapeDtypeStruct(shape, kind) for shape, kind in shapes],
        scratch_shapes=scratch,
        compiler_params=pltpu.CompilerParams(vmem_limit_bytes=(40 if weights else 8) * 2**20),
        cost_estimate=pl.CostEstimate(
            flops=total * depth * columns // 32,
            bytes_accessed=depth * columns // 16,
            transcendentals=0,
        ),
    )(facts, *rows, *weights, *factors, *others)


def hidden_of(gate, up):
    return (jax.nn.silu(gate.astype(jnp.float32)) * up.astype(jnp.float32)).astype(jnp.bfloat16)


def slots_of(row_adapter_index, adapter_storage_slot):
    names = jnp.arange(adapter_storage_slot.shape[0], dtype=jnp.int32)
    same = row_adapter_index == names[None, :]
    return jnp.sum(jnp.where(same, adapter_storage_slot[None, :], 0), axis=1)


def gathered(
    gate_activation,
    up_activation,
    down_base_weight,
    first_factor_table,
    second_factor_table,
    row_adapter_index,
    adapter_storage_slot,
):
    hidden = hidden_of(gate_activation, up_activation)
    row_count = hidden.shape[0]
    owners = lax.axis_size("wide")
    local_adapter = first_factor_table.shape[0]
    slots = local_adapter * owners
    rank_portion = second_factor_table.shape[1]
    home = lax.axis_index("wide")
    slot_all = slots_of(row_adapter_index, adapter_storage_slot)
    blocks = slot_all.reshape(owners, row_count)
    order = jnp.arange(row_count, dtype=jnp.int32)
    earlier = (blocks[:, :, None] == blocks[:, None, :]) & (order[None, :] < order[:, None])
    position = jnp.sum(earlier.astype(jnp.int32), axis=2)
    rows = lax.all_gather(hidden, "wide", axis=0, tiled=True)
    base = jnp.dot(rows, down_base_weight, preferred_element_type=jnp.float32)
    low = jnp.einsum("re,nqe->nrq", rows, first_factor_table, preferred_element_type=jnp.float32)
    low = low.reshape(local_adapter, owners, row_count, low.shape[2])
    own = home * local_adapter + jnp.arange(local_adapter, dtype=jnp.int32)
    kept = []
    for item in range(MOST):
        mask = (blocks[None] == own[:, None, None]) & (position == item)[None]
        kept.append(jnp.sum(jnp.where(mask[..., None], low, 0), axis=2))
    low = lax.psum_scatter(jnp.stack(kept, axis=2), INNER, scatter_dimension=3, tiled=True)
    low = lax.all_gather(low.astype(jnp.bfloat16), "wide", axis=0, tiled=True)
    spread = 0
    for item in range(MOST):
        mask = (blocks[None] == jnp.arange(slots, dtype=jnp.int32)[:, None, None]) & (position == item)
        spread += jnp.where(mask[..., None], low[:, :, item][:, :, None], 0)
    spread = spread.reshape(slots, owners * row_count, rank_portion)
    delta = jnp.einsum("srq,sqw->rw", spread, second_factor_table, preferred_element_type=jnp.float32)
    total = base + delta
    return lax.psum_scatter(total, INNER, scatter_dimension=0, tiled=True).astype(jnp.bfloat16)


def ring_order(nodes):
    return list(range(0, nodes, 2)) + list(range(nodes - 1, 0, -2))


def ringed(
    gate_activation,
    up_activation,
    down_base_weight,
    first_factor_table,
    second_factor_table,
    row_adapter_index,
    adapter_storage_slot,
):
    f32, bf16 = jnp.float32, jnp.bfloat16
    row_count, width_part = gate_activation.shape
    owners = lax.axis_size("wide")
    nodes = owners // 2
    far = nodes // 2
    steps = far - 1
    own_nodes = nodes // 2
    own_blocks = owners // 2
    group_rows = 2 * row_count
    order = ring_order(nodes)
    depth = width_part // 2
    width = down_base_weight.shape[1]
    rank = first_factor_table.shape[1]

    table = []
    for w in range(owners):
        p = order.index(w // 2)
        at = lambda shift: order[(p + shift) % nodes]
        ways = (-1, 1) if w % 2 == 0 else (1, -1)
        arrivals = [at(0)] + [at(s * k) for k in range(1, far) for s in ways] + [at(far)]
        row = [2 * node + (w % 2 ^ side) for node in arrivals for side in (0, 1)]
        for half in (0, 1):
            here = [(at(s) < own_nodes) == (half == 0) for s in range(far)]
            row += [int(h) for h in here]
            row += [at(s if h else s + far) % own_nodes for s, h in enumerate(here)]
        table.append(row)
    home = lax.axis_index("wide")
    part = lax.axis_index(INNER)
    side = jnp.bitwise_and(home, 1)

    def moved(shift, cross=0):
        return [
            (order[p] * 2 + c, order[(p + shift) % nodes] * 2 + (c ^ cross))
            for p in range(nodes)
            for c in (0, 1)
        ]

    def send(value, shift, cross=0):
        return lax.ppermute(value, "wide", moved(shift, cross))

    def turn(value, way):
        to_right, to_left = moved(way), moved(-way)
        pairs = [pair for pair in to_right if pair[0] % 2 == 0]
        pairs += [pair for pair in to_left if pair[0] % 2 == 1]
        return lax.ppermute(value, "wide", pairs)

    def half_of(value, which, axis):
        return lax.dynamic_slice_in_dim(value, which * depth, depth, axis)

    crossed = [(2 * w + m, 2 * (w ^ 1) + (1 - m)) for w in range(owners) for m in (0, 1)]

    def to_three(to_sib, to_mp, to_both):
        return (
            send(to_sib, 0, 1),
            lax.ppermute(to_mp, INNER, SWAP),
            lax.ppermute(to_both, ("wide",) + INNER, crossed),
        )

    keep = hidden_of(half_of(gate_activation, side, 1), half_of(up_activation, side, 1))
    give = hidden_of(half_of(gate_activation, 1 - side, 1), half_of(up_activation, 1 - side, 1))
    block = jnp.concatenate([keep, send(give, 0, 1)], axis=0)
    one_way, other_way = turn(block, 1), turn(block, -1)

    weight, first, second_factor_table, block = lax.optimization_barrier(
        (down_base_weight, first_factor_table[0], second_factor_table, block)
    )
    other_second = lax.ppermute(second_factor_table, INNER, SWAP)
    weights = (weight, send(weight, 0, 1))
    factors = (first, send(first, 0, 1))
    home_late, row_adapter_index, weights = lax.optimization_barrier(
        (home, row_adapter_index, weights)
    )

    pieces = [block, one_way, other_way]
    for step in range(2, steps + 1):
        one_way, other_way = turn(one_way, 1), turn(other_way, -1)
        if step < steps:
            one_way, other_way = lax.optimization_barrier((one_way, other_way))
            pieces += [one_way, other_way]

    row = lax.dynamic_index_in_dim(
        jnp.asarray(np.array(table, np.int32)), home_late, 0, keepdims=False
    )
    edges = np.cumsum([0, 2 * nodes, far, far, far, far])
    arrived, *rest = [row[a:b] for a, b in zip(edges[:-1], edges[1:])]
    flags = jnp.where(part == 0, rest[0], rest[2])
    facts = jnp.concatenate([side[None], part[None].astype(jnp.int32), flags])
    target = jnp.where(part == 0, rest[1], rest[3])
    places = target[:, None] == jnp.arange(own_nodes, dtype=jnp.int32)[None, :]
    slot_all = slots_of(row_adapter_index, adapter_storage_slot).reshape(owners, row_count)
    ranks = jnp.arange(row_count, dtype=jnp.int32)
    earlier = (slot_all[:, :, None] == slot_all[:, None, :]) & (ranks[None, :] < ranks[:, None])
    position = jnp.sum(earlier.astype(jnp.int32), axis=2)
    blocks = jnp.arange(owners, dtype=jnp.int32)

    items = jnp.arange(owners * MOST, dtype=jnp.int32)
    came = arrived[:, None] == blocks[None, :]
    slot_came = jnp.sum(jnp.where(came[:, :, None], slot_all[None], 0), axis=1).reshape(1, -1)
    place_came = jnp.sum(
        jnp.where(came[:, :, None], position[None] + MOST * blocks[None, :, None], 0), axis=1
    ).reshape(1, -1)
    chosen = jnp.concatenate(
        [
            ((place_came == items[:, None]) & (slot_came == slot)).astype(bf16)
            for slot in (home_late, jnp.bitwise_xor(home_late, 1))
        ],
        axis=0,
    )
    early_rows = len(pieces) * group_rows
    middle_rows = early_rows + 2 * group_rows
    choices = [
        chosen[:, :early_rows],
        chosen[:, early_rows:middle_rows],
        chosen[:, middle_rows:],
    ]

    half = own_blocks * MOST
    here = own_blocks * row_count
    slot_here = lax.dynamic_slice_in_dim(slot_all, part * own_blocks, own_blocks).reshape(here, 1)
    position_here = lax.dynamic_slice_in_dim(position, part * own_blocks, own_blocks)
    block_here = jnp.arange(here, dtype=jnp.int32)[:, None] // row_count
    spot = (
        jnp.bitwise_xor(slot_here, home_late) * half
        + block_here * MOST
        + position_here.reshape(here, 1)
    )
    spots = (spot == jnp.arange(owners * half, dtype=jnp.int32)[None, :]).astype(bf16)
    piece = rank // 2
    column = jnp.arange(owners * rank, dtype=jnp.int32)[None, :]
    own_rank = jnp.bitwise_xor(part, column // (owners * piece)) * piece + column % piece
    mask = (slot_here == column // piece % owners).astype(bf16)
    copies = (jnp.arange(rank, dtype=jnp.int32)[:, None] == own_rank).astype(bf16)

    second = jnp.concatenate(
        [values.reshape(owners * piece, width) for values in (second_factor_table, other_second)],
        axis=0,
    )

    compact_shape = ((2, owners * MOST, rank), f32)
    early = kernel_call(
        functools.partial(early_kernel, len(pieces)),
        facts,
        pieces,
        early_rows,
        weights,
        factors,
        (choices[0],),
        [((len(pieces), group_rows, width), f32)] * 2 + [compact_shape],
    )
    ready = (facts, spots, mask, copies, choices, places, second)
    one_way, other_way, early, ready = lax.optimization_barrier(
        (one_way, other_way, early, ready)
    )
    facts, spots, mask, copies, choices, places, second = ready

    last = turn(one_way, 1)

    def shares(pairs):
        shape = (pairs, group_rows, width)
        return [(shape, f32)] * 2 + [(shape, bf16)] * 2

    own_more, sib_more, compact = kernel_call(
        middle_kernel,
        facts,
        (one_way, other_way),
        2 * group_rows,
        weights,
        factors,
        (choices[1], early[2], early[0], early[1]),
        [((2, far - 1, group_rows, width), f32)] * 2 + [compact_shape],
    )
    last, compact = lax.optimization_barrier((last, compact))

    kept, sent = kernel_call(
        low_kernel,
        facts,
        (last,),
        group_rows,
        (),
        factors,
        (choices[2], compact),
        [((2, half, rank), f32)] * 2,
    )
    kept, sent, sib_more = lax.optimization_barrier((kept, sent, sib_more))
    got = to_three(kept, sent, sent)
    low = (kept + got[1] + (got[0] + got[2])[::-1]).astype(bf16)

    kept_more, out_more = [
        a + b for a, b in zip(own_more, send(sib_more, 0, 1))
    ]
    out_more = out_more.astype(bf16)

    def from_node(value, gap):
        return lax.ppermute(value, "wide", [(w, w ^ (2 * gap)) for w in range(owners)])

    def gather(value, gap, reach):
        parts = [from_node(value, gap * k) for k in range(1, reach)]
        return jnp.concatenate([value] + parts, axis=0)

    low, out_more, last = lax.optimization_barrier((low, out_more, last))
    got_more = lax.ppermute(out_more, INNER, SWAP)
    reach = min(4, nodes)
    low = gather(low, 1, reach)

    kept_one, *one = kernel_call(
        last_kernel, facts, (last,), group_rows, weights, (), (early[0], early[1]), shares(1)
    )
    low, one, got_more = lax.optimization_barrier((low, one, got_more))
    gap = reach
    while gap < nodes:
        low = gather(low, gap, 2)
        gap *= 2
    got_one = to_three(*one)

    more = kept_more + got_more.astype(f32)
    rows = 0
    for pair in range(1, far):
        rows = rows + jnp.where(places[pair][:, None, None], more[pair - 1 : pair], 0)
    own_low = jnp.dot(spots, low.reshape(owners * half, rank), preferred_element_type=f32)
    spread = jnp.dot(own_low.astype(bf16), copies, preferred_element_type=f32).astype(bf16) * mask
    delta = jnp.dot(spread, second, preferred_element_type=f32)
    one = kept_one + got_one[0] + got_one[1].astype(f32) + got_one[2].astype(f32)
    rows = rows + jnp.where(places[0][:, None, None], one, 0)
    return (delta + rows.reshape(-1, width)).astype(bf16)


def solution(mesh):
    shape = dict(mesh.shape)
    wide, inner = shape["wide"], shape["mp"] * shape["sub"]
    paired = shape["sub"] == 1 and inner == 2 and wide % 8 == 0 and wide & (wide - 1) == 0
    if paired:
        nodes = wide // 2
        order = ring_order(nodes)
        paired = all(
            (order[p] < nodes // 2) != (order[(p + nodes // 2) % nodes] < nodes // 2)
            for p in range(nodes)
        )
    return jax.shard_map(
        ringed if paired else gathered,
        mesh=mesh,
        in_specs=(
            P(("groups", "wide"), ("mp", "sub")),
            P(("groups", "wide"), ("mp", "sub")),
            P(("mp", "sub"), "wide"),
            P("wide", None, ("mp", "sub")),
            P(None, ("mp", "sub"), "wide"),
            P("groups", None),
            P(),
        ),
        out_specs=P(("groups", "mp", "sub"), "wide"),
        check_vma=False,
    )
```

```python
import functools

import jax
import jax.numpy as jnp
import numpy as np
from jax import lax
from jax.experimental import pallas as pl
from jax.experimental.pallas import tpu as pltpu
from jax.sharding import PartitionSpec as P

MOST = 2
INNER = ("mp", "sub")
SWAP = [(0, 1), (1, 0)]


def tile_of(depth, most=1024):
    parts = 1
    while depth % parts or (depth // parts) % 128 or depth // parts > most:
        parts += 1
    return depth // parts


def started(sources, places, ready):
    copies = []
    for index, (source, place) in enumerate(zip(sources, places)):
        copies.append(pltpu.make_async_copy(source, place, ready.at[index]))
        copies[-1].start()
    return copies


def weight_copies(lane, weights, held, ready):
    tiles, tile = held.shape[1:3]
    first = pl.multiple_of(lane * tiles * tile, 128)
    sources = [w.at[pl.ds(first + i * tile, tile)] for i in range(tiles) for w in weights]
    places = [held.at[which, i] for i in range(tiles) for which in (0, 1)]
    return started(sources, places, ready)


def weight_products(rows_of, copies, held, sums):
    tiles, tile = held.shape[1:3]
    for total in sums:
        total[...] = jnp.zeros_like(total)
    for index in range(tiles):
        rows = rows_of(slice(index * tile, (index + 1) * tile))
        for which, total in enumerate(sums):
            copies[2 * index + which].wait()
            total[...] += jnp.dot(rows, held[which, index], preferred_element_type=jnp.float32)


def factor_products(rows_of, table, low):
    depth = table.shape[1]
    tile = tile_of(depth)
    low[...] = jnp.zeros_like(low)

    def step(index, carry):
        here = pl.ds(pl.multiple_of(index * tile, 128), tile)
        low[...] += lax.dot_general(
            rows_of(here), table[:, here], (((1,), (1,)), ((), ())), preferred_element_type=jnp.float32
        )
        return carry

    lax.fori_loop(0, depth // tile, step, 0)


def in_lanes(lane, total, index, height):
    first = total[2 * index * height : (2 * index + 1) * height]
    other = total[(2 * index + 1) * height : (2 * index + 2) * height]
    whole = jnp.concatenate([first, other], axis=0)
    turned = jnp.concatenate([other, first], axis=0)
    return jnp.where(lane == 0, whole, turned)


def compacted(choice, low):
    high = low.astype(jnp.bfloat16)
    rest = low - high.astype(jnp.float32)
    middle = rest.astype(jnp.bfloat16)
    tail = (rest - middle.astype(jnp.float32)).astype(jnp.bfloat16)
    picked = jnp.dot(
        choice,
        jnp.concatenate([high, middle, tail], axis=1),
        preferred_element_type=jnp.float32,
    )
    size = low.shape[1]
    total = picked[:, :size] + (picked[:, size : 2 * size] + picked[:, 2 * size :])
    count, rank = choice.shape[0] // 2, size // 2
    return total[:count, :rank], total[count:, rank:]


def early_kernel(count, facts, *refs):
    pieces, refs = refs[:count], refs[count:]
    weights, (factors, choices), refs = refs[:2], refs[2:4], refs[4:]
    owns, rests, compact, refs = refs[:2], refs[2:4], refs[4], refs[5:]
    sums, (held, ready, low) = refs[:2], refs[2:]
    rows_of = lambda here: jnp.concatenate([piece[:, here] for piece in pieces], axis=0)
    in_flight = weight_copies(facts[0], weights, held, ready)
    factor_products(rows_of, factors, low)
    weight_products(rows_of, in_flight, held, sums)
    height = owns[0].shape[1] // 2
    for own, rest, total in zip(owns, rests, sums):
        own[0] = in_lanes(facts[0], total, 0, height)
        for index in range(1, count):
            rest[index - 1] = in_lanes(facts[0], total, index, height)
    compact[0], compact[1] = compacted(choices[...], low[...])


def share(flag, near, away, outs, pair):
    (near_own, near_sib), (away_own, away_sib) = near, away
    kept, to_sib, to_mp, to_both = outs
    kept[pair] = jnp.where(flag == 1, near_own, away_own)
    to_sib[pair] = jnp.where(flag == 1, near_sib, away_sib)
    to_mp[pair] = jnp.where(flag == 1, away_own, near_own).astype(to_mp.dtype)
    to_both[pair] = jnp.where(flag == 1, away_sib, near_sib).astype(to_both.dtype)


def middle_kernel(facts, piece, other, *refs):
    weights, (factors, choices, compact_in, base, base_sib), refs = refs[:2], refs[2:7], refs[7:]
    (own, sib, compact), sums, (held, ready, low) = refs[:3], refs[3:5], refs[5:]
    outs = own.at[0], sib.at[0], own.at[1], sib.at[1]
    rows_of = lambda here: jnp.concatenate([piece[:, here], other[:, here]], axis=0)
    in_flight = weight_copies(facts[0], weights, held, ready)
    factor_products(rows_of, factors, low)
    weight_products(rows_of, in_flight, held, sums)
    pairs, group = own.shape[1:3]
    fresh = [[in_lanes(facts[0], total, index, group // 2) for total in sums] for index in (0, 1)]
    lane = facts[0]
    ahead = [jnp.where(lane == 0, b, a) for a, b in zip(*fresh)]
    behind = [jnp.where(lane == 0, a, b) for a, b in zip(*fresh)]
    for pair in range(pairs):
        step, back = pair + 1, pairs - pair
        near, away = 2 * step - 1 - lane, 2 * back - 2 + lane
        near = ahead if step == pairs else (base[near], base_sib[near])
        away = behind if back == pairs else (base[away], base_sib[away])
        share(facts[2 + step], near, away, outs, pair)
    for which, fresh_low in enumerate(compacted(choices[...], low[...])):
        compact[which] = compact_in[which] + fresh_low


def low_kernel(facts, piece, factors, choices, compact_in, kept, sent, low):
    half = kept.shape[1]
    factor_products(lambda here: piece[:, here], factors, low)
    for which, fresh_low in enumerate(compacted(choices[...], low[...])):
        total = compact_in[which] + fresh_low
        kept[which] = jnp.where(facts[1] == 0, total[:half], total[half:])
        sent[which] = jnp.where(facts[1] == 0, total[half:], total[:half])


def last_kernel(facts, piece, *refs):
    weights, (base, base_sib), refs = refs[:2], refs[2:4], refs[4:]
    outs, sums, (held, ready) = refs[:4], refs[4:6], refs[6:]
    in_flight = weight_copies(facts[0], weights, held, ready)
    weight_products(lambda here: piece[:, here], in_flight, held, sums)
    away = [in_lanes(facts[0], total, 0, piece.shape[0] // 2) for total in sums]
    share(facts[2], (base[0], base_sib[0]), away, outs, 0)


def kernel_call(kernel, facts, rows, total, weights, factors, others, shapes):
    in_vmem, in_hbm = pl.BlockSpec(memory_space=pltpu.VMEM), pl.BlockSpec(memory_space=pl.ANY)
    depth = rows[0].shape[1]
    tile = tile_of(depth)
    scratch, columns = [], 0
    if weights:
        width = weights[0].shape[1]
        columns += 2 * width
        scratch += [pltpu.VMEM((total, width), jnp.float32)] * 2
        scratch += [pltpu.VMEM((2, depth // tile, tile, width), jnp.bfloat16)]
        scratch += [pltpu.SemaphoreType.DMA((2 * depth // tile,))]
    if factors:
        columns += factors[0].shape[0]
        scratch += [pltpu.VMEM((total, factors[0].shape[0]), jnp.float32)]
    return pl.pallas_call(
        kernel,
        in_specs=[pl.BlockSpec(memory_space=pltpu.SMEM)]
        + [in_vmem] * len(rows)
        + [in_hbm] * len(weights)
        + [in_vmem] * (len(factors) + len(others)),
        out_specs=[in_vmem] * len(shapes),
        out_shape=[jax.ShapeDtypeStruct(shape, kind) for shape, kind in shapes],
        scratch_shapes=scratch,
        compiler_params=pltpu.CompilerParams(vmem_limit_bytes=(40 if weights else 8) * 2**20),
        cost_estimate=pl.CostEstimate(
            flops=total * depth * columns // 32,
            bytes_accessed=depth * columns // 16,
            transcendentals=0,
        ),
    )(facts, *rows, *weights, *factors, *others)


def hidden_of(gate, up):
    return (jax.nn.silu(gate.astype(jnp.float32)) * up.astype(jnp.float32)).astype(jnp.bfloat16)


def slots_of(row_adapter_index, adapter_storage_slot):
    names = jnp.arange(adapter_storage_slot.shape[0], dtype=jnp.int32)
    same = row_adapter_index == names[None, :]
    return jnp.sum(jnp.where(same, adapter_storage_slot[None, :], 0), axis=1)


def gathered(
    gate_activation,
    up_activation,
    down_base_weight,
    first_factor_table,
    second_factor_table,
    row_adapter_index,
    adapter_storage_slot,
):
    hidden = hidden_of(gate_activation, up_activation)
    row_count = hidden.shape[0]
    owners = lax.axis_size("wide")
    local_adapter = first_factor_table.shape[0]
    slots = local_adapter * owners
    rank_portion = second_factor_table.shape[1]
    home = lax.axis_index("wide")
    slot_all = slots_of(row_adapter_index, adapter_storage_slot)
    blocks = slot_all.reshape(owners, row_count)
    order = jnp.arange(row_count, dtype=jnp.int32)
    earlier = (blocks[:, :, None] == blocks[:, None, :]) & (order[None, :] < order[:, None])
    position = jnp.sum(earlier.astype(jnp.int32), axis=2)
    rows = lax.all_gather(hidden, "wide", axis=0, tiled=True)
    base = jnp.dot(rows, down_base_weight, preferred_element_type=jnp.float32)
    low = jnp.einsum("re,nqe->nrq", rows, first_factor_table, preferred_element_type=jnp.float32)
    low = low.reshape(local_adapter, owners, row_count, low.shape[2])
    own = home * local_adapter + jnp.arange(local_adapter, dtype=jnp.int32)
    kept = []
    for item in range(MOST):
        mask = (blocks[None] == own[:, None, None]) & (position == item)[None]
        kept.append(jnp.sum(jnp.where(mask[..., None], low, 0), axis=2))
    low = lax.psum_scatter(jnp.stack(kept, axis=2), INNER, scatter_dimension=3, tiled=True)
    low = lax.all_gather(low.astype(jnp.bfloat16), "wide", axis=0, tiled=True)
    spread = 0
    for item in range(MOST):
        mask = (blocks[None] == jnp.arange(slots, dtype=jnp.int32)[:, None, None]) & (position == item)
        spread += jnp.where(mask[..., None], low[:, :, item][:, :, None], 0)
    spread = spread.reshape(slots, owners * row_count, rank_portion)
    delta = jnp.einsum("srq,sqw->rw", spread, second_factor_table, preferred_element_type=jnp.float32)
    total = base + delta
    return lax.psum_scatter(total, INNER, scatter_dimension=0, tiled=True).astype(jnp.bfloat16)


def ring_order(nodes):
    return list(range(0, nodes, 2)) + list(range(nodes - 1, 0, -2))


def ringed(
    gate_activation,
    up_activation,
    down_base_weight,
    first_factor_table,
    second_factor_table,
    row_adapter_index,
    adapter_storage_slot,
):
    f32, bf16 = jnp.float32, jnp.bfloat16
    row_count, width_part = gate_activation.shape
    owners = lax.axis_size("wide")
    nodes = owners // 2
    far = nodes // 2
    steps = far - 1
    own_nodes = nodes // 2
    own_blocks = owners // 2
    group_rows = 2 * row_count
    order = ring_order(nodes)
    depth = width_part // 2
    width = down_base_weight.shape[1]
    rank = first_factor_table.shape[1]

    table = []
    for w in range(owners):
        p = order.index(w // 2)
        at = lambda shift: order[(p + shift) % nodes]
        ways = (-1, 1) if w % 2 == 0 else (1, -1)
        arrivals = [at(0)] + [at(s * k) for k in range(1, far) for s in ways] + [at(far)]
        row = [2 * node + (w % 2 ^ side) for node in arrivals for side in (0, 1)]
        for half in (0, 1):
            here = [(at(s) < own_nodes) == (half == 0) for s in range(far)]
            row += [int(h) for h in here]
            row += [at(s if h else s + far) % own_nodes for s, h in enumerate(here)]
        table.append(row)
    home = lax.axis_index("wide")
    part = lax.axis_index(INNER)
    side = jnp.bitwise_and(home, 1)

    def moved(shift, cross=0):
        return [
            (order[p] * 2 + c, order[(p + shift) % nodes] * 2 + (c ^ cross))
            for p in range(nodes)
            for c in (0, 1)
        ]

    def send(value, shift, cross=0):
        return lax.ppermute(value, "wide", moved(shift, cross))

    def turn(value, way):
        to_right, to_left = moved(way), moved(-way)
        pairs = [pair for pair in to_right if pair[0] % 2 == 0]
        pairs += [pair for pair in to_left if pair[0] % 2 == 1]
        return lax.ppermute(value, "wide", pairs)

    def half_of(value, which, axis):
        return lax.dynamic_slice_in_dim(value, which * depth, depth, axis)

    crossed = [(2 * w + m, 2 * (w ^ 1) + (1 - m)) for w in range(owners) for m in (0, 1)]

    def to_three(to_sib, to_mp, to_both):
        return (
            send(to_sib, 0, 1),
            lax.ppermute(to_mp, INNER, SWAP),
            lax.ppermute(to_both, ("wide",) + INNER, crossed),
        )

    keep = hidden_of(half_of(gate_activation, side, 1), half_of(up_activation, side, 1))
    give = hidden_of(half_of(gate_activation, 1 - side, 1), half_of(up_activation, 1 - side, 1))
    block = jnp.concatenate([keep, send(give, 0, 1)], axis=0)
    one_way, other_way = turn(block, 1), turn(block, -1)

    weight, first, second_factor_table, block = lax.optimization_barrier(
        (down_base_weight, first_factor_table[0], second_factor_table, block)
    )
    other_second = lax.ppermute(second_factor_table, INNER, SWAP)
    weights = (weight, send(weight, 0, 1))
    factors = (
        jnp.concatenate([half_of(first, side, 1), half_of(send(first, 0, 1), side, 1)], axis=0),
    )
    home_late, row_adapter_index, weights = lax.optimization_barrier(
        (home, row_adapter_index, weights)
    )

    pieces = [block, one_way, other_way]
    for step in range(2, steps + 1):
        one_way, other_way = turn(one_way, 1), turn(other_way, -1)
        if step < steps:
            one_way, other_way = lax.optimization_barrier((one_way, other_way))
            pieces += [one_way, other_way]

    row = lax.dynamic_index_in_dim(
        jnp.asarray(np.array(table, np.int32)), home_late, 0, keepdims=False
    )
    edges = np.cumsum([0, 2 * nodes, far, far, far, far])
    arrived, *rest = [row[a:b] for a, b in zip(edges[:-1], edges[1:])]
    flags = jnp.where(part == 0, rest[0], rest[2])
    facts = jnp.concatenate([side[None], part[None].astype(jnp.int32), flags])
    target = jnp.where(part == 0, rest[1], rest[3])
    places = target[:, None] == jnp.arange(own_nodes, dtype=jnp.int32)[None, :]
    slot_all = slots_of(row_adapter_index, adapter_storage_slot).reshape(owners, row_count)
    ranks = jnp.arange(row_count, dtype=jnp.int32)
    earlier = (slot_all[:, :, None] == slot_all[:, None, :]) & (ranks[None, :] < ranks[:, None])
    position = jnp.sum(earlier.astype(jnp.int32), axis=2)
    blocks = jnp.arange(owners, dtype=jnp.int32)

    items = jnp.arange(owners * MOST, dtype=jnp.int32)
    came = arrived[:, None] == blocks[None, :]
    slot_came = jnp.sum(jnp.where(came[:, :, None], slot_all[None], 0), axis=1).reshape(1, -1)
    place_came = jnp.sum(
        jnp.where(came[:, :, None], position[None] + MOST * blocks[None, :, None], 0), axis=1
    ).reshape(1, -1)
    chosen = jnp.concatenate(
        [
            ((place_came == items[:, None]) & (slot_came == slot)).astype(bf16)
            for slot in (home_late, jnp.bitwise_xor(home_late, 1))
        ],
        axis=0,
    )
    early_rows = len(pieces) * group_rows
    middle_rows = early_rows + 2 * group_rows
    choices = [
        chosen[:, :early_rows],
        chosen[:, early_rows:middle_rows],
        chosen[:, middle_rows:],
    ]

    half = own_blocks * MOST
    here = own_blocks * row_count
    slot_here = lax.dynamic_slice_in_dim(slot_all, part * own_blocks, own_blocks).reshape(here, 1)
    position_here = lax.dynamic_slice_in_dim(position, part * own_blocks, own_blocks)
    block_here = jnp.arange(here, dtype=jnp.int32)[:, None] // row_count
    spot = (
        jnp.bitwise_xor(slot_here, home_late) * half
        + block_here * MOST
        + position_here.reshape(here, 1)
    )
    spots = (spot == jnp.arange(owners * half, dtype=jnp.int32)[None, :]).astype(bf16)
    piece = rank // 2
    column = jnp.arange(owners * rank, dtype=jnp.int32)[None, :]
    own_rank = jnp.bitwise_xor(part, column // (owners * piece)) * piece + column % piece
    mask = (slot_here == column // piece % owners).astype(bf16)
    copies = (jnp.arange(rank, dtype=jnp.int32)[:, None] == own_rank).astype(bf16)

    second = jnp.concatenate(
        [values.reshape(owners * piece, width) for values in (second_factor_table, other_second)],
        axis=0,
    )

    compact_shape = ((2, owners * MOST, rank), f32)
    early = kernel_call(
        functools.partial(early_kernel, len(pieces)),
        facts,
        pieces,
        early_rows,
        weights,
        factors,
        (choices[0],),
        [((1, group_rows, width), f32)] * 2
        + [((len(pieces) - 1, group_rows, width), f32)] * 2
        + [compact_shape],
    )
    ready = (facts, spots, mask, copies, choices, places, second)
    one_way, other_way, early, ready = lax.optimization_barrier(
        (one_way, other_way, early, ready)
    )
    facts, spots, mask, copies, choices, places, second = ready

    last = turn(one_way, 1)

    def shares(pairs):
        shape = (pairs, group_rows, width)
        return [(shape, f32)] * 2 + [(shape, bf16)] * 2

    own_more, sib_more, compact = kernel_call(
        middle_kernel,
        facts,
        (one_way, other_way),
        2 * group_rows,
        weights,
        factors,
        (choices[1], early[4], early[2], early[3]),
        [((2, far - 1, group_rows, width), f32)] * 2 + [compact_shape],
    )
    last, compact = lax.optimization_barrier((last, compact))

    kept, sent = kernel_call(
        low_kernel,
        facts,
        (last,),
        group_rows,
        (),
        factors,
        (choices[2], compact),
        [((2, half, rank), f32)] * 2,
    )
    got = to_three(kept, sent, sent)
    low = (kept + got[1] + (got[0] + got[2])[::-1]).astype(bf16)

    kept_more, out_more = [
        a + b for a, b in zip(own_more, send(sib_more, 0, 1))
    ]
    out_more = out_more.astype(bf16)

    def from_node(value, gap):
        return lax.ppermute(value, "wide", [(w, w ^ (2 * gap)) for w in range(owners)])

    def gather(value, gap, reach):
        parts = [from_node(value, gap * k) for k in range(1, reach)]
        return jnp.concatenate([value] + parts, axis=0)

    low, out_more, last = lax.optimization_barrier((low, out_more, last))
    got_more = lax.ppermute(out_more, INNER, SWAP)
    reach = min(4, nodes)
    low = gather(low, 1, reach)

    kept_one, *one = kernel_call(
        last_kernel, facts, (last,), group_rows, weights, (), (early[0], early[1]), shares(1)
    )
    low, one, got_more = lax.optimization_barrier((low, one, got_more))
    gap = reach
    while gap < nodes:
        low = gather(low, gap, 2)
        gap *= 2
    got_one = to_three(*one)
    low, got_more = lax.optimization_barrier((low, got_more))

    more = kept_more + got_more.astype(f32)
    rows = 0
    for pair in range(1, far):
        rows = rows + jnp.where(places[pair][:, None, None], more[pair - 1 : pair], 0)
    own_low = jnp.dot(spots, low.reshape(owners * half, rank), preferred_element_type=f32)
    spread = jnp.dot(own_low.astype(bf16), copies, preferred_element_type=f32).astype(bf16) * mask
    delta = jnp.dot(spread, second, preferred_element_type=f32)
    one = kept_one + got_one[0] + got_one[1].astype(f32) + got_one[2].astype(f32)
    rows = rows + jnp.where(places[0][:, None, None], one, 0)
    return (delta + rows.reshape(-1, width)).astype(bf16)


def solution(mesh):
    shape = dict(mesh.shape)
    wide, inner = shape["wide"], shape["mp"] * shape["sub"]
    paired = shape["sub"] == 1 and inner == 2 and wide % 8 == 0 and wide & (wide - 1) == 0
    if paired:
        nodes = wide // 2
        order = ring_order(nodes)
        paired = all(
            (order[p] < nodes // 2) != (order[(p + nodes // 2) % nodes] < nodes // 2)
            for p in range(nodes)
        )
    return jax.shard_map(
        ringed if paired else gathered,
        mesh=mesh,
        in_specs=(
            P(("groups", "wide"), ("mp", "sub")),
            P(("groups", "wide"), ("mp", "sub")),
            P(("mp", "sub"), "wide"),
            P("wide", None, ("mp", "sub")),
            P(None, ("mp", "sub"), "wide"),
            P("groups", None),
            P(),
        ),
        out_specs=P(("groups", "mp", "sub"), "wide"),
        check_vma=False,
    )
```

```python
import functools

import jax
import jax.numpy as jnp
import numpy as np
from jax import lax
from jax.experimental import pallas as pl
from jax.experimental.pallas import tpu as pltpu
from jax.sharding import PartitionSpec as P

MOST = 2
INNER = ("mp", "sub")
SWAP = [(0, 1), (1, 0)]


def tile_of(depth, most=1024):
    parts = 1
    while depth % parts or (depth // parts) % 128 or depth // parts > most:
        parts += 1
    return depth // parts


def started(sources, places, ready):
    copies = []
    for index, (source, place) in enumerate(zip(sources, places)):
        copies.append(pltpu.make_async_copy(source, place, ready.at[index]))
        copies[-1].start()
    return copies


def weight_copies(lane, weights, held, ready):
    tiles, tile = held.shape[1:3]
    first = pl.multiple_of(lane * tiles * tile, 128)
    sources = [w.at[pl.ds(first + i * tile, tile)] for i in range(tiles) for w in weights]
    places = [held.at[which, i] for i in range(tiles) for which in (0, 1)]
    return started(sources, places, ready)


def weight_products(rows_of, held, sums, copies=None):
    tiles, tile = held.shape[1:3]
    for total in sums:
        total[...] = jnp.zeros_like(total)
    for index in range(tiles):
        rows = rows_of(slice(index * tile, (index + 1) * tile))
        for which, total in enumerate(sums):
            if copies:
                copies[2 * index + which].wait()
            total[...] += jnp.dot(rows, held[which, index], preferred_element_type=jnp.float32)


def factor_products(rows_of, table, low):
    depth = table.shape[1]
    tile = tile_of(depth)
    low[...] = jnp.zeros_like(low)

    def step(index, carry):
        here = pl.ds(pl.multiple_of(index * tile, 128), tile)
        low[...] += lax.dot_general(
            rows_of(here), table[:, here], (((1,), (1,)), ((), ())), preferred_element_type=jnp.float32
        )
        return carry

    lax.fori_loop(0, depth // tile, step, 0)


def in_lanes(lane, total, index, height):
    first = total[2 * index * height : (2 * index + 1) * height]
    other = total[(2 * index + 1) * height : (2 * index + 2) * height]
    whole = jnp.concatenate([first, other], axis=0)
    turned = jnp.concatenate([other, first], axis=0)
    return jnp.where(lane == 0, whole, turned)


def compacted(choice, low):
    high = low.astype(jnp.bfloat16)
    rest = low - high.astype(jnp.float32)
    middle = rest.astype(jnp.bfloat16)
    tail = (rest - middle.astype(jnp.float32)).astype(jnp.bfloat16)
    picked = jnp.dot(
        choice,
        jnp.concatenate([high, middle, tail], axis=1),
        preferred_element_type=jnp.float32,
    )
    size = low.shape[1]
    total = picked[:, :size] + (picked[:, size : 2 * size] + picked[:, 2 * size :])
    count, rank = choice.shape[0] // 2, size // 2
    return total[:count, :rank], total[count:, rank:]


def early_kernel(count, facts, *refs):
    pieces, refs = refs[:count], refs[count:]
    (factors, choices), weights, refs = refs[:2], refs[2:4], refs[4:]
    owns, rests, (compact, held), refs = refs[:2], refs[2:4], refs[4:6], refs[6:]
    sums, (low, ready) = refs[:2], refs[2:]
    rows_of = lambda here: jnp.concatenate([piece[:, here] for piece in pieces], axis=0)
    in_flight = weight_copies(facts[0], weights, held, ready)
    factor_products(rows_of, factors, low)
    weight_products(rows_of, held, sums, in_flight)
    height = owns[0].shape[1] // 2
    for own, rest, total in zip(owns, rests, sums):
        own[0] = in_lanes(facts[0], total, 0, height)
        for index in range(1, count):
            rest[index - 1] = in_lanes(facts[0], total, index, height)
    compact[0], compact[1] = compacted(choices[...], low[...])


def share(flag, near, away, outs, pair):
    (near_own, near_sib), (away_own, away_sib) = near, away
    kept, to_sib, to_mp, to_both = outs
    kept[pair] = jnp.where(flag == 1, near_own, away_own)
    to_sib[pair] = jnp.where(flag == 1, near_sib, away_sib)
    to_mp[pair] = jnp.where(flag == 1, away_own, near_own).astype(to_mp.dtype)
    to_both[pair] = jnp.where(flag == 1, away_sib, near_sib).astype(to_both.dtype)


def middle_kernel(facts, piece, other, *refs):
    (held, factors, choices, compact_in, base, base_sib), refs = refs[:6], refs[6:]
    (own, sib, compact), sums, low = refs[:3], refs[3:5], refs[5]
    outs = own.at[0], sib.at[0], own.at[1], sib.at[1]
    rows_of = lambda here: jnp.concatenate([piece[:, here], other[:, here]], axis=0)
    factor_products(rows_of, factors, low)
    weight_products(rows_of, held, sums)
    pairs, group = own.shape[1:3]
    fresh = [[in_lanes(facts[0], total, index, group // 2) for total in sums] for index in (0, 1)]
    lane = facts[0]
    ahead = [jnp.where(lane == 0, b, a) for a, b in zip(*fresh)]
    behind = [jnp.where(lane == 0, a, b) for a, b in zip(*fresh)]
    for pair in range(pairs):
        step, back = pair + 1, pairs - pair
        near, away = 2 * step - 1 - lane, 2 * back - 2 + lane
        near = ahead if step == pairs else (base[near], base_sib[near])
        away = behind if back == pairs else (base[away], base_sib[away])
        share(facts[2 + step], near, away, outs, pair)
    for which, fresh_low in enumerate(compacted(choices[...], low[...])):
        compact[which] = compact_in[which] + fresh_low


def low_kernel(facts, piece, factors, choices, compact_in, kept, sent, low):
    half = kept.shape[1]
    factor_products(lambda here: piece[:, here], factors, low)
    for which, fresh_low in enumerate(compacted(choices[...], low[...])):
        total = compact_in[which] + fresh_low
        kept[which] = jnp.where(facts[1] == 0, total[:half], total[half:])
        sent[which] = jnp.where(facts[1] == 0, total[half:], total[:half])


def last_kernel(facts, piece, held, base, base_sib, *refs):
    outs, sums = refs[:4], refs[4:]
    weight_products(lambda here: piece[:, here], held, sums)
    away = [in_lanes(facts[0], total, 0, piece.shape[0] // 2) for total in sums]
    share(facts[2], (base[0], base_sib[0]), away, outs, 0)


def kernel_call(kernel, facts, arrays, shapes, scratch, flops, weights=(), grant=12):
    in_vmem = pl.BlockSpec(memory_space=pltpu.VMEM)
    if weights:
        scratch = scratch + [pltpu.SemaphoreType.DMA((len(weights) * shapes[-1][0][1],))]
    return pl.pallas_call(
        kernel,
        in_specs=[pl.BlockSpec(memory_space=pltpu.SMEM)]
        + [in_vmem] * len(arrays)
        + [pl.BlockSpec(memory_space=pl.ANY)] * len(weights),
        out_specs=[in_vmem] * len(shapes),
        out_shape=[jax.ShapeDtypeStruct(shape, kind) for shape, kind in shapes],
        scratch_shapes=scratch,
        compiler_params=pltpu.CompilerParams(vmem_limit_bytes=grant * 2**20),
        cost_estimate=pl.CostEstimate(
            flops=flops // 32, bytes_accessed=flops // 1024, transcendentals=0
        ),
    )(facts, *arrays, *weights)


def hidden_of(gate, up):
    return (jax.nn.silu(gate.astype(jnp.float32)) * up.astype(jnp.float32)).astype(jnp.bfloat16)


def slots_of(row_adapter_index, adapter_storage_slot):
    names = jnp.arange(adapter_storage_slot.shape[0], dtype=jnp.int32)
    same = row_adapter_index == names[None, :]
    return jnp.sum(jnp.where(same, adapter_storage_slot[None, :], 0), axis=1)


def gathered(
    gate_activation,
    up_activation,
    down_base_weight,
    first_factor_table,
    second_factor_table,
    row_adapter_index,
    adapter_storage_slot,
):
    hidden = hidden_of(gate_activation, up_activation)
    row_count = hidden.shape[0]
    owners = lax.axis_size("wide")
    local_adapter = first_factor_table.shape[0]
    slots = local_adapter * owners
    rank_portion = second_factor_table.shape[1]
    home = lax.axis_index("wide")
    slot_all = slots_of(row_adapter_index, adapter_storage_slot)
    blocks = slot_all.reshape(owners, row_count)
    order = jnp.arange(row_count, dtype=jnp.int32)
    earlier = (blocks[:, :, None] == blocks[:, None, :]) & (order[None, :] < order[:, None])
    position = jnp.sum(earlier.astype(jnp.int32), axis=2)
    rows = lax.all_gather(hidden, "wide", axis=0, tiled=True)
    base = jnp.dot(rows, down_base_weight, preferred_element_type=jnp.float32)
    low = jnp.einsum("re,nqe->nrq", rows, first_factor_table, preferred_element_type=jnp.float32)
    low = low.reshape(local_adapter, owners, row_count, low.shape[2])
    own = home * local_adapter + jnp.arange(local_adapter, dtype=jnp.int32)
    kept = []
    for item in range(MOST):
        mask = (blocks[None] == own[:, None, None]) & (position == item)[None]
        kept.append(jnp.sum(jnp.where(mask[..., None], low, 0), axis=2))
    low = lax.psum_scatter(jnp.stack(kept, axis=2), INNER, scatter_dimension=3, tiled=True)
    low = lax.all_gather(low.astype(jnp.bfloat16), "wide", axis=0, tiled=True)
    spread = 0
    for item in range(MOST):
        mask = (blocks[None] == jnp.arange(slots, dtype=jnp.int32)[:, None, None]) & (position == item)
        spread += jnp.where(mask[..., None], low[:, :, item][:, :, None], 0)
    spread = spread.reshape(slots, owners * row_count, rank_portion)
    delta = jnp.einsum("srq,sqw->rw", spread, second_factor_table, preferred_element_type=jnp.float32)
    total = base + delta
    return lax.psum_scatter(total, INNER, scatter_dimension=0, tiled=True).astype(jnp.bfloat16)


def ring_order(nodes):
    return list(range(0, nodes, 2)) + list(range(nodes - 1, 0, -2))


def ringed(
    gate_activation,
    up_activation,
    down_base_weight,
    first_factor_table,
    second_factor_table,
    row_adapter_index,
    adapter_storage_slot,
):
    f32, bf16 = jnp.float32, jnp.bfloat16
    row_count, width_part = gate_activation.shape
    owners = lax.axis_size("wide")
    nodes = owners // 2
    far = nodes // 2
    steps = far - 1
    own_nodes = nodes // 2
    own_blocks = owners // 2
    group_rows = 2 * row_count
    order = ring_order(nodes)
    depth = width_part // 2
    width = down_base_weight.shape[1]
    rank = first_factor_table.shape[1]

    table = []
    for w in range(owners):
        p = order.index(w // 2)
        at = lambda shift: order[(p + shift) % nodes]
        ways = (-1, 1) if w % 2 == 0 else (1, -1)
        arrivals = [at(0)] + [at(s * k) for k in range(1, far) for s in ways] + [at(far)]
        row = [2 * node + (w % 2 ^ side) for node in arrivals for side in (0, 1)]
        for half in (0, 1):
            here = [(at(s) < own_nodes) == (half == 0) for s in range(far)]
            row += [int(h) for h in here]
            row += [at(s if h else s + far) % own_nodes for s, h in enumerate(here)]
        table.append(row)
    home = lax.axis_index("wide")
    part = lax.axis_index(INNER)
    side = jnp.bitwise_and(home, 1)

    def moved(shift, cross=0):
        return [
            (order[p] * 2 + c, order[(p + shift) % nodes] * 2 + (c ^ cross))
            for p in range(nodes)
            for c in (0, 1)
        ]

    def send(value, shift, cross=0):
        return lax.ppermute(value, "wide", moved(shift, cross))

    def turn(value, way):
        to_right, to_left = moved(way), moved(-way)
        pairs = [pair for pair in to_right if pair[0] % 2 == 0]
        pairs += [pair for pair in to_left if pair[0] % 2 == 1]
        return lax.ppermute(value, "wide", pairs)

    def half_of(value, which, axis):
        return lax.dynamic_slice_in_dim(value, which * depth, depth, axis)

    crossed = [(2 * w + m, 2 * (w ^ 1) + (1 - m)) for w in range(owners) for m in (0, 1)]

    def to_three(to_sib, to_mp, to_both):
        return (
            send(to_sib, 0, 1),
            lax.ppermute(to_mp, INNER, SWAP),
            lax.ppermute(to_both, ("wide",) + INNER, crossed),
        )

    give = hidden_of(half_of(gate_activation, 1 - side, 1), half_of(up_activation, 1 - side, 1))
    keep_side, give = lax.optimization_barrier((side, give))
    keep = hidden_of(half_of(gate_activation, keep_side, 1), half_of(up_activation, keep_side, 1))
    block = jnp.concatenate([keep, send(give, 0, 1)], axis=0)
    one_way, other_way = turn(block, 1), turn(block, -1)

    weight, first, second_factor_table, block = lax.optimization_barrier(
        (down_base_weight, first_factor_table[0], second_factor_table, block)
    )
    other_second = lax.ppermute(second_factor_table, INNER, SWAP)
    weights = (weight, send(weight, 0, 1))
    factors = jnp.concatenate(
        [half_of(first, side, 1), half_of(send(first, 0, 1), side, 1)], axis=0
    )
    home_late, row_adapter_index, weights = lax.optimization_barrier(
        (home, row_adapter_index, weights)
    )

    pieces = [block, one_way, other_way]
    for step in range(2, steps + 1):
        one_way, other_way = turn(one_way, 1), turn(other_way, -1)
        if step < steps:
            one_way, other_way = lax.optimization_barrier((one_way, other_way))
            pieces += [one_way, other_way]

    row = lax.dynamic_index_in_dim(
        jnp.asarray(np.array(table, np.int32)), home_late, 0, keepdims=False
    )
    edges = np.cumsum([0, 2 * nodes, far, far, far, far])
    arrived, *rest = [row[a:b] for a, b in zip(edges[:-1], edges[1:])]
    flags = jnp.where(part == 0, rest[0], rest[2])
    facts = jnp.concatenate([side[None], part[None].astype(jnp.int32), flags])
    target = jnp.where(part == 0, rest[1], rest[3])
    places = target[:, None] == jnp.arange(own_nodes, dtype=jnp.int32)[None, :]
    slot_all = slots_of(row_adapter_index, adapter_storage_slot).reshape(owners, row_count)
    ranks = jnp.arange(row_count, dtype=jnp.int32)
    earlier = (slot_all[:, :, None] == slot_all[:, None, :]) & (ranks[None, :] < ranks[:, None])
    position = jnp.sum(earlier.astype(jnp.int32), axis=2)
    blocks = jnp.arange(owners, dtype=jnp.int32)

    items = jnp.arange(owners * MOST, dtype=jnp.int32)
    came = arrived[:, None] == blocks[None, :]
    slot_came = jnp.sum(jnp.where(came[:, :, None], slot_all[None], 0), axis=1).reshape(1, -1)
    place_came = jnp.sum(
        jnp.where(came[:, :, None], position[None] + MOST * blocks[None, :, None], 0), axis=1
    ).reshape(1, -1)
    chosen = jnp.concatenate(
        [
            ((place_came == items[:, None]) & (slot_came == slot)).astype(bf16)
            for slot in (home_late, jnp.bitwise_xor(home_late, 1))
        ],
        axis=0,
    )
    early_rows = len(pieces) * group_rows
    middle_rows = early_rows + 2 * group_rows
    choices = [
        chosen[:, :early_rows],
        chosen[:, early_rows:middle_rows],
        chosen[:, middle_rows:],
    ]

    half = own_blocks * MOST
    here = own_blocks * row_count
    slot_here = lax.dynamic_slice_in_dim(slot_all, part * own_blocks, own_blocks).reshape(here, 1)
    position_here = lax.dynamic_slice_in_dim(position, part * own_blocks, own_blocks)
    block_here = jnp.arange(here, dtype=jnp.int32)[:, None] // row_count
    spot = (
        jnp.bitwise_xor(slot_here, home_late) * half
        + block_here * MOST
        + position_here.reshape(here, 1)
    )
    spots = (spot == jnp.arange(owners * half, dtype=jnp.int32)[None, :]).astype(bf16)
    piece = rank // 2
    column = jnp.arange(owners * rank, dtype=jnp.int32)[None, :]
    own_rank = jnp.bitwise_xor(part, column // (owners * piece)) * piece + column % piece
    mask = (slot_here == column // piece % owners).astype(bf16)
    copies = (jnp.arange(rank, dtype=jnp.int32)[:, None] == own_rank).astype(bf16)

    second = jnp.concatenate(
        [values.reshape(owners * piece, width) for values in (second_factor_table, other_second)],
        axis=0,
    )

    compact_shape = ((2, owners * MOST, rank), f32)
    tile = tile_of(depth)

    def sums(rows, with_low=True):
        columns = [width, width] + [2 * rank] * with_low
        return [pltpu.VMEM((rows, size), f32) for size in columns]

    def flops(rows, columns):
        return 2 * rows * depth * columns

    *early, held = kernel_call(
        functools.partial(early_kernel, len(pieces)),
        facts,
        (*pieces, factors, choices[0]),
        [((1, group_rows, width), f32)] * 2
        + [((len(pieces) - 1, group_rows, width), f32)] * 2
        + [compact_shape, ((2, depth // tile, tile, width), bf16)],
        sums(early_rows),
        flops(early_rows, 2 * (width + rank)),
        weights,
        32,
    )
    ready = (facts, spots, mask, copies, choices, places, second)
    one_way, other_way, early, held, ready = lax.optimization_barrier(
        (one_way, other_way, early, held, ready)
    )
    facts, spots, mask, copies, choices, places, second = ready

    last = turn(one_way, 1)

    def shares(pairs):
        shape = (pairs, group_rows, width)
        return [(shape, f32)] * 2 + [(shape, bf16)] * 2

    own_more, sib_more, compact = kernel_call(
        middle_kernel,
        facts,
        (one_way, other_way, held, factors, choices[1], early[4], early[2], early[3]),
        [((2, far - 1, group_rows, width), f32)] * 2 + [compact_shape],
        sums(2 * group_rows),
        flops(2 * group_rows, 2 * (width + rank)),
    )

    kept_more, out_more = [a + b for a, b in zip(own_more, send(sib_more, 0, 1))]
    out_more = out_more.astype(bf16)
    last, compact = lax.optimization_barrier((last, compact))

    kept, sent = kernel_call(
        low_kernel,
        facts,
        (last, factors, choices[2], compact),
        [((2, half, rank), f32)] * 2,
        [pltpu.VMEM((group_rows, 2 * rank), f32)],
        flops(group_rows, 2 * rank),
    )
    got = to_three(kept, sent, sent)
    low = (kept + got[1] + (got[0] + got[2])[::-1]).astype(bf16)

    def from_node(value, gap):
        return lax.ppermute(value, "wide", [(w, w ^ (2 * gap)) for w in range(owners)])

    def gather(value, gap, reach):
        parts = [from_node(value, gap * k) for k in range(1, reach)]
        return jnp.concatenate([value] + parts, axis=0)

    low, out_more, last = lax.optimization_barrier((low, out_more, last))
    got_more = lax.ppermute(out_more, INNER, SWAP)
    reach = min(4, nodes)
    low = gather(low, 1, reach)

    kept_one, *one = kernel_call(
        last_kernel,
        facts,
        (last, held, early[0], early[1]),
        shares(1),
        sums(group_rows, False),
        flops(group_rows, 2 * width),
    )
    low, one, got_more = lax.optimization_barrier((low, one, got_more))
    gap = reach
    while gap < nodes:
        low = gather(low, gap, 2)
        gap *= 2
    got_one = to_three(*one)
    low, got_more = lax.optimization_barrier((low, got_more))

    more = kept_more + got_more.astype(f32)
    rows = 0
    for pair in range(1, far):
        rows = rows + jnp.where(places[pair][:, None, None], more[pair - 1 : pair], 0)
    own_low = jnp.dot(spots, low.reshape(owners * half, rank), preferred_element_type=f32)
    spread = jnp.dot(own_low.astype(bf16), copies, preferred_element_type=f32).astype(bf16) * mask
    delta = jnp.dot(spread, second, preferred_element_type=f32)
    one = kept_one + got_one[0] + got_one[1].astype(f32) + got_one[2].astype(f32)
    rows = rows + jnp.where(places[0][:, None, None], one, 0)
    return (delta + rows.reshape(-1, width)).astype(bf16)


def solution(mesh):
    shape = dict(mesh.shape)
    wide, inner = shape["wide"], shape["mp"] * shape["sub"]
    paired = shape["sub"] == 1 and inner == 2 and wide % 8 == 0 and wide & (wide - 1) == 0
    if paired:
        nodes = wide // 2
        order = ring_order(nodes)
        paired = all(
            (order[p] < nodes // 2) != (order[(p + nodes // 2) % nodes] < nodes // 2)
            for p in range(nodes)
        )
    return jax.shard_map(
        ringed if paired else gathered,
        mesh=mesh,
        in_specs=(
            P(("groups", "wide"), ("mp", "sub")),
            P(("groups", "wide"), ("mp", "sub")),
            P(("mp", "sub"), "wide"),
            P("wide", None, ("mp", "sub")),
            P(None, ("mp", "sub"), "wide"),
            P("groups", None),
            P(),
        ),
        out_specs=P(("groups", "mp", "sub"), "wide"),
        check_vma=False,
    )
```

```python
import functools

import jax
import jax.numpy as jnp
import numpy as np
from jax import lax
from jax.experimental import pallas as pl
from jax.experimental.pallas import tpu as pltpu
from jax.sharding import PartitionSpec as P

MOST = 2
INNER = ("mp", "sub")
SWAP = [(0, 1), (1, 0)]


def tile_of(depth, most=1024):
    parts = 1
    while depth % parts or (depth // parts) % 128 or depth // parts > most:
        parts += 1
    return depth // parts


def started(sources, places, ready):
    copies = []
    for index, (source, place) in enumerate(zip(sources, places)):
        copies.append(pltpu.make_async_copy(source, place, ready.at[index]))
        copies[-1].start()
    return copies


def weight_copies(lane, weights, held, ready):
    tiles, tile = held.shape[1:3]
    first = pl.multiple_of(lane * tiles * tile, 128)
    sources = [w.at[pl.ds(first + i * tile, tile)] for i in range(tiles) for w in weights]
    places = [held.at[which, i] for i in range(tiles) for which in (0, 1)]
    return started(sources, places, ready)


def weight_products(rows_of, held, sums, copies=None):
    tiles, tile = held.shape[1:3]
    for total in sums:
        total[...] = jnp.zeros_like(total)
    for index in range(tiles):
        rows = rows_of(slice(index * tile, (index + 1) * tile))
        for which, total in enumerate(sums):
            if copies:
                copies[2 * index + which].wait()
            total[...] += jnp.dot(rows, held[which, index], preferred_element_type=jnp.float32)


def factor_products(rows_of, table, low):
    depth = table.shape[1]
    tile = tile_of(depth)
    low[...] = jnp.zeros_like(low)

    def step(index, carry):
        here = pl.ds(pl.multiple_of(index * tile, 128), tile)
        low[...] += lax.dot_general(
            rows_of(here), table[:, here], (((1,), (1,)), ((), ())), preferred_element_type=jnp.float32
        )
        return carry

    lax.fori_loop(0, depth // tile, step, 0)


def in_lanes(lane, total, index, height):
    first = total[2 * index * height : (2 * index + 1) * height]
    other = total[(2 * index + 1) * height : (2 * index + 2) * height]
    whole = jnp.concatenate([first, other], axis=0)
    turned = jnp.concatenate([other, first], axis=0)
    return jnp.where(lane == 0, whole, turned)


def compacted(choice, low):
    high = low.astype(jnp.bfloat16)
    rest = low - high.astype(jnp.float32)
    middle = rest.astype(jnp.bfloat16)
    tail = (rest - middle.astype(jnp.float32)).astype(jnp.bfloat16)
    picked = jnp.dot(
        choice,
        jnp.concatenate([high, middle, tail], axis=1),
        preferred_element_type=jnp.float32,
    )
    size = low.shape[1]
    total = picked[:, :size] + (picked[:, size : 2 * size] + picked[:, 2 * size :])
    count, rank = choice.shape[0] // 2, size // 2
    return total[:count, :rank], total[count:, rank:]


def early_kernel(count, facts, *refs):
    pieces, refs = refs[:count], refs[count:]
    (factors, choices), weights, refs = refs[:2], refs[2:4], refs[4:]
    owns, rests, (compact, held), refs = refs[:2], refs[2:4], refs[4:6], refs[6:]
    sums, (low, ready) = refs[:2], refs[2:]
    rows_of = lambda here: jnp.concatenate([piece[:, here] for piece in pieces], axis=0)
    in_flight = weight_copies(facts[0], weights, held, ready)
    factor_products(rows_of, factors, low)
    weight_products(rows_of, held, sums, in_flight)
    height = owns[0].shape[1] // 2
    for own, rest, total in zip(owns, rests, sums):
        own[0] = in_lanes(facts[0], total, 0, height)
        for index in range(1, count):
            rest[index - 1] = in_lanes(facts[0], total, index, height)
    compact[0], compact[1] = compacted(choices[...], low[...])


def share(flag, near, away, outs, pair):
    (near_own, near_sib), (away_own, away_sib) = near, away
    kept, to_sib, to_mp, to_both = outs
    kept[pair] = jnp.where(flag == 1, near_own, away_own)
    to_sib[pair] = jnp.where(flag == 1, near_sib, away_sib)
    to_mp[pair] = jnp.where(flag == 1, away_own, near_own).astype(to_mp.dtype)
    to_both[pair] = jnp.where(flag == 1, away_sib, near_sib).astype(to_both.dtype)


def middle_kernel(facts, piece, other, *refs):
    (held, factors, choices, compact_in, base, base_sib), refs = refs[:6], refs[6:]
    (own, sib, compact), sums, low = refs[:3], refs[3:5], refs[5]
    outs = own.at[0], sib.at[0], own.at[1], sib.at[1]
    rows_of = lambda here: jnp.concatenate([piece[:, here], other[:, here]], axis=0)
    factor_products(rows_of, factors, low)
    weight_products(rows_of, held, sums)
    pairs, group = own.shape[1:3]
    fresh = [[in_lanes(facts[0], total, index, group // 2) for total in sums] for index in (0, 1)]
    lane = facts[0]
    ahead = [jnp.where(lane == 0, b, a) for a, b in zip(*fresh)]
    behind = [jnp.where(lane == 0, a, b) for a, b in zip(*fresh)]
    for pair in range(pairs):
        step, back = pair + 1, pairs - pair
        near, away = 2 * step - 1 - lane, 2 * back - 2 + lane
        near = ahead if step == pairs else (base[near], base_sib[near])
        away = behind if back == pairs else (base[away], base_sib[away])
        share(facts[2 + step], near, away, outs, pair)
    for which, fresh_low in enumerate(compacted(choices[...], low[...])):
        compact[which] = compact_in[which] + fresh_low


def low_kernel(facts, piece, factors, choices, compact_in, kept, sent, low):
    half = kept.shape[1]
    factor_products(lambda here: piece[:, here], factors, low)
    for which, fresh_low in enumerate(compacted(choices[...], low[...])):
        total = compact_in[which] + fresh_low
        kept[which] = jnp.where(facts[1] == 0, total[:half], total[half:])
        sent[which] = jnp.where(facts[1] == 0, total[half:], total[:half])


def last_kernel(facts, piece, held, base, base_sib, *refs):
    outs, sums = refs[:4], refs[4:]
    weight_products(lambda here: piece[:, here], held, sums)
    away = [in_lanes(facts[0], total, 0, piece.shape[0] // 2) for total in sums]
    share(facts[2], (base[0], base_sib[0]), away, outs, 0)


def final_kernel(pairs, facts, low, spots, mask, copies, second, *refs):
    kept_more, got_more, kept_one, got_sib, got_mp, got_both, out, delta = refs
    f32 = jnp.float32
    own = jnp.dot(spots[...], low[...], preferred_element_type=f32).astype(jnp.bfloat16)
    spread = jnp.dot(own, copies[...], preferred_element_type=f32).astype(jnp.bfloat16) * mask[...]
    delta[...] = jnp.dot(spread, second[...], preferred_element_type=f32).reshape(delta.shape)
    for pair in range(pairs):
        place = facts[2 + pairs + pair]
        if pair:
            value = kept_more[pair - 1] + got_more[pair - 1].astype(f32)
        else:
            value = kept_one[0] + got_sib[0] + (got_mp[0].astype(f32) + got_both[0].astype(f32))
        out[place] = (value + delta[place]).astype(out.dtype)


def kernel_call(kernel, facts, arrays, shapes, scratch, flops, weights=(), grant=12):
    in_vmem = pl.BlockSpec(memory_space=pltpu.VMEM)
    if weights:
        scratch = scratch + [pltpu.SemaphoreType.DMA((len(weights) * shapes[-1][0][1],))]
    return pl.pallas_call(
        kernel,
        in_specs=[pl.BlockSpec(memory_space=pltpu.SMEM)]
        + [in_vmem] * len(arrays)
        + [pl.BlockSpec(memory_space=pl.ANY)] * len(weights),
        out_specs=[in_vmem] * len(shapes),
        out_shape=[jax.ShapeDtypeStruct(shape, kind) for shape, kind in shapes],
        scratch_shapes=scratch,
        compiler_params=pltpu.CompilerParams(vmem_limit_bytes=grant * 2**20),
        cost_estimate=pl.CostEstimate(
            flops=flops // 32, bytes_accessed=flops // 1024, transcendentals=0
        ),
    )(facts, *arrays, *weights)


def hidden_of(gate, up):
    return (jax.nn.silu(gate.astype(jnp.float32)) * up.astype(jnp.float32)).astype(jnp.bfloat16)


def slots_of(row_adapter_index, adapter_storage_slot):
    names = jnp.arange(adapter_storage_slot.shape[0], dtype=jnp.int32)
    same = row_adapter_index == names[None, :]
    return jnp.sum(jnp.where(same, adapter_storage_slot[None, :], 0), axis=1)


def gathered(
    gate_activation,
    up_activation,
    down_base_weight,
    first_factor_table,
    second_factor_table,
    row_adapter_index,
    adapter_storage_slot,
):
    hidden = hidden_of(gate_activation, up_activation)
    row_count = hidden.shape[0]
    owners = lax.axis_size("wide")
    local_adapter = first_factor_table.shape[0]
    slots = local_adapter * owners
    rank_portion = second_factor_table.shape[1]
    home = lax.axis_index("wide")
    slot_all = slots_of(row_adapter_index, adapter_storage_slot)
    blocks = slot_all.reshape(owners, row_count)
    order = jnp.arange(row_count, dtype=jnp.int32)
    earlier = (blocks[:, :, None] == blocks[:, None, :]) & (order[None, :] < order[:, None])
    position = jnp.sum(earlier.astype(jnp.int32), axis=2)
    rows = lax.all_gather(hidden, "wide", axis=0, tiled=True)
    base = jnp.dot(rows, down_base_weight, preferred_element_type=jnp.float32)
    low = jnp.einsum("re,nqe->nrq", rows, first_factor_table, preferred_element_type=jnp.float32)
    low = low.reshape(local_adapter, owners, row_count, low.shape[2])
    own = home * local_adapter + jnp.arange(local_adapter, dtype=jnp.int32)
    kept = []
    for item in range(MOST):
        mask = (blocks[None] == own[:, None, None]) & (position == item)[None]
        kept.append(jnp.sum(jnp.where(mask[..., None], low, 0), axis=2))
    low = lax.psum_scatter(jnp.stack(kept, axis=2), INNER, scatter_dimension=3, tiled=True)
    low = lax.all_gather(low.astype(jnp.bfloat16), "wide", axis=0, tiled=True)
    spread = 0
    for item in range(MOST):
        mask = (blocks[None] == jnp.arange(slots, dtype=jnp.int32)[:, None, None]) & (position == item)
        spread += jnp.where(mask[..., None], low[:, :, item][:, :, None], 0)
    spread = spread.reshape(slots, owners * row_count, rank_portion)
    delta = jnp.einsum("srq,sqw->rw", spread, second_factor_table, preferred_element_type=jnp.float32)
    total = base + delta
    return lax.psum_scatter(total, INNER, scatter_dimension=0, tiled=True).astype(jnp.bfloat16)


def ring_order(nodes):
    return list(range(0, nodes, 2)) + list(range(nodes - 1, 0, -2))


def ringed(
    gate_activation,
    up_activation,
    down_base_weight,
    first_factor_table,
    second_factor_table,
    row_adapter_index,
    adapter_storage_slot,
):
    f32, bf16 = jnp.float32, jnp.bfloat16
    row_count, width_part = gate_activation.shape
    owners = lax.axis_size("wide")
    nodes = owners // 2
    far = nodes // 2
    steps = far - 1
    own_nodes = nodes // 2
    own_blocks = owners // 2
    group_rows = 2 * row_count
    order = ring_order(nodes)
    depth = width_part // 2
    width = down_base_weight.shape[1]
    rank = first_factor_table.shape[1]

    table = []
    for w in range(owners):
        p = order.index(w // 2)
        at = lambda shift: order[(p + shift) % nodes]
        ways = (-1, 1) if w % 2 == 0 else (1, -1)
        arrivals = [at(0)] + [at(s * k) for k in range(1, far) for s in ways] + [at(far)]
        row = [2 * node + (w % 2 ^ side) for node in arrivals for side in (0, 1)]
        for half in (0, 1):
            here = [(at(s) < own_nodes) == (half == 0) for s in range(far)]
            row += [int(h) for h in here]
            row += [at(s if h else s + far) % own_nodes for s, h in enumerate(here)]
        table.append(row)
    home = lax.axis_index("wide")
    part = lax.axis_index(INNER)
    side = jnp.bitwise_and(home, 1)

    def moved(shift, cross=0):
        return [
            (order[p] * 2 + c, order[(p + shift) % nodes] * 2 + (c ^ cross))
            for p in range(nodes)
            for c in (0, 1)
        ]

    def send(value, shift, cross=0):
        return lax.ppermute(value, "wide", moved(shift, cross))

    def turn(value, way):
        to_right, to_left = moved(way), moved(-way)
        pairs = [pair for pair in to_right if pair[0] % 2 == 0]
        pairs += [pair for pair in to_left if pair[0] % 2 == 1]
        return lax.ppermute(value, "wide", pairs)

    def half_of(value, which, axis):
        return lax.dynamic_slice_in_dim(value, which * depth, depth, axis)

    crossed = [(2 * w + m, 2 * (w ^ 1) + (1 - m)) for w in range(owners) for m in (0, 1)]

    def to_three(to_sib, to_mp, to_both):
        return (
            send(to_sib, 0, 1),
            lax.ppermute(to_mp, INNER, SWAP),
            lax.ppermute(to_both, ("wide",) + INNER, crossed),
        )

    give = hidden_of(half_of(gate_activation, 1 - side, 1), half_of(up_activation, 1 - side, 1))
    keep_side, give = lax.optimization_barrier((side, give))
    keep = hidden_of(half_of(gate_activation, keep_side, 1), half_of(up_activation, keep_side, 1))
    block = jnp.concatenate([keep, send(give, 0, 1)], axis=0)
    one_way, other_way = turn(block, 1), turn(block, -1)

    weight, first, second_factor_table, block = lax.optimization_barrier(
        (down_base_weight, first_factor_table[0], second_factor_table, block)
    )
    other_second = lax.ppermute(second_factor_table, INNER, SWAP)
    weights = (weight, send(weight, 0, 1))
    factors = jnp.concatenate(
        [half_of(first, side, 1), half_of(send(first, 0, 1), side, 1)], axis=0
    )
    home_late, row_adapter_index, weights = lax.optimization_barrier(
        (home, row_adapter_index, weights)
    )

    pieces = [block, one_way, other_way]
    for step in range(2, steps + 1):
        one_way, other_way = turn(one_way, 1), turn(other_way, -1)
        if step < steps:
            one_way, other_way = lax.optimization_barrier((one_way, other_way))
            pieces += [one_way, other_way]

    row = lax.dynamic_index_in_dim(
        jnp.asarray(np.array(table, np.int32)), home_late, 0, keepdims=False
    )
    edges = np.cumsum([0, 2 * nodes, far, far, far, far])
    arrived, *rest = [row[a:b] for a, b in zip(edges[:-1], edges[1:])]
    facts = jnp.concatenate(
        [side[None], part[None].astype(jnp.int32)]
        + [jnp.where(part == 0, a, b) for a, b in zip(rest[:2], rest[2:])]
    )
    slot_all = slots_of(row_adapter_index, adapter_storage_slot).reshape(owners, row_count)
    ranks = jnp.arange(row_count, dtype=jnp.int32)
    earlier = (slot_all[:, :, None] == slot_all[:, None, :]) & (ranks[None, :] < ranks[:, None])
    position = jnp.sum(earlier.astype(jnp.int32), axis=2)
    blocks = jnp.arange(owners, dtype=jnp.int32)

    items = jnp.arange(owners * MOST, dtype=jnp.int32)
    came = arrived[:, None] == blocks[None, :]
    slot_came = jnp.sum(jnp.where(came[:, :, None], slot_all[None], 0), axis=1).reshape(1, -1)
    place_came = jnp.sum(
        jnp.where(came[:, :, None], position[None] + MOST * blocks[None, :, None], 0), axis=1
    ).reshape(1, -1)
    chosen = jnp.concatenate(
        [
            ((place_came == items[:, None]) & (slot_came == slot)).astype(bf16)
            for slot in (home_late, jnp.bitwise_xor(home_late, 1))
        ],
        axis=0,
    )
    early_rows = len(pieces) * group_rows
    middle_rows = early_rows + 2 * group_rows
    choices = [
        chosen[:, :early_rows],
        chosen[:, early_rows:middle_rows],
        chosen[:, middle_rows:],
    ]

    half = own_blocks * MOST
    here = own_blocks * row_count
    slot_here = lax.dynamic_slice_in_dim(slot_all, part * own_blocks, own_blocks).reshape(here, 1)
    position_here = lax.dynamic_slice_in_dim(position, part * own_blocks, own_blocks)
    block_here = jnp.arange(here, dtype=jnp.int32)[:, None] // row_count
    spot = (
        jnp.bitwise_xor(slot_here, home_late) * half
        + block_here * MOST
        + position_here.reshape(here, 1)
    )
    spots = (spot == jnp.arange(owners * half, dtype=jnp.int32)[None, :]).astype(bf16)
    piece = rank // 2
    column = jnp.arange(owners * rank, dtype=jnp.int32)[None, :]
    own_rank = jnp.bitwise_xor(part, column // (owners * piece)) * piece + column % piece
    mask = (slot_here == column // piece % owners).astype(bf16)
    copies = (jnp.arange(rank, dtype=jnp.int32)[:, None] == own_rank).astype(bf16)

    second = jnp.concatenate(
        [values.reshape(owners * piece, width) for values in (second_factor_table, other_second)],
        axis=0,
    )

    compact_shape = ((2, owners * MOST, rank), f32)
    tile = tile_of(depth)

    def sums(rows, with_low=True):
        columns = [width, width] + [2 * rank] * with_low
        return [pltpu.VMEM((rows, size), f32) for size in columns]

    def flops(rows, columns):
        return 2 * rows * depth * columns

    facts, spots, mask, copies, choices, second = lax.optimization_barrier(
        (facts, spots, mask, copies, choices, second)
    )
    *early, held = kernel_call(
        functools.partial(early_kernel, len(pieces)),
        facts,
        (*pieces, factors, choices[0]),
        [((1, group_rows, width), f32)] * 2
        + [((len(pieces) - 1, group_rows, width), f32)] * 2
        + [compact_shape, ((2, depth // tile, tile, width), bf16)],
        sums(early_rows),
        flops(early_rows, 2 * (width + rank)),
        weights,
        32,
    )
    one_way, other_way, early, held = lax.optimization_barrier((one_way, other_way, early, held))

    last = turn(one_way, 1)

    def shares(pairs):
        shape = (pairs, group_rows, width)
        return [(shape, f32)] * 2 + [(shape, bf16)] * 2

    own_more, sib_more, compact = kernel_call(
        middle_kernel,
        facts,
        (one_way, other_way, held, factors, choices[1], early[4], early[2], early[3]),
        [((2, far - 1, group_rows, width), f32)] * 2 + [compact_shape],
        sums(2 * group_rows),
        flops(2 * group_rows, 2 * (width + rank)),
    )

    kept_more, out_more = [a + b for a, b in zip(own_more, send(sib_more, 0, 1))]
    out_more = out_more.astype(bf16)
    last, compact = lax.optimization_barrier((last, compact))

    kept, sent = kernel_call(
        low_kernel,
        facts,
        (last, factors, choices[2], compact),
        [((2, half, rank), f32)] * 2,
        [pltpu.VMEM((group_rows, 2 * rank), f32)],
        flops(group_rows, 2 * rank),
    )
    got = to_three(kept, sent, sent)
    low = (kept + got[1] + (got[0] + got[2])[::-1]).astype(bf16)

    def from_node(value, gap):
        return lax.ppermute(value, "wide", [(w, w ^ (2 * gap)) for w in range(owners)])

    def gather(value, gap, reach):
        parts = [from_node(value, gap * k) for k in range(1, reach)]
        return jnp.concatenate([value] + parts, axis=0)

    low, out_more, last = lax.optimization_barrier((low, out_more, last))
    got_more = lax.ppermute(out_more, INNER, SWAP)
    reach = min(4, nodes)
    low = gather(low, 1, reach)

    kept_one, *one = kernel_call(
        last_kernel,
        facts,
        (last, held, early[0], early[1]),
        shares(1),
        sums(group_rows, False),
        flops(group_rows, 2 * width),
    )
    low, one, got_more = lax.optimization_barrier((low, one, got_more))
    gap = reach
    while gap < nodes:
        low = gather(low, gap, 2)
        gap *= 2
    got_one = to_three(*one)

    out = kernel_call(
        functools.partial(final_kernel, far),
        facts,
        (
            low.reshape(owners * half, rank),
            spots,
            mask,
            copies,
            second,
            kept_more,
            got_more,
            kept_one,
            *got_one,
        ),
        [((own_nodes, group_rows, width), bf16)],
        [pltpu.VMEM((own_nodes, group_rows, width), f32)],
        2 * here * owners * rank * width,
    )[0]
    return out.reshape(-1, width)


def solution(mesh):
    shape = dict(mesh.shape)
    wide, inner = shape["wide"], shape["mp"] * shape["sub"]
    paired = shape["sub"] == 1 and inner == 2 and wide % 8 == 0 and wide & (wide - 1) == 0
    if paired:
        nodes = wide // 2
        order = ring_order(nodes)
        paired = all(
            (order[p] < nodes // 2) != (order[(p + nodes // 2) % nodes] < nodes // 2)
            for p in range(nodes)
        )
    return jax.shard_map(
        ringed if paired else gathered,
        mesh=mesh,
        in_specs=(
            P(("groups", "wide"), ("mp", "sub")),
            P(("groups", "wide"), ("mp", "sub")),
            P(("mp", "sub"), "wide"),
            P("wide", None, ("mp", "sub")),
            P(None, ("mp", "sub"), "wide"),
            P("groups", None),
            P(),
        ),
        out_specs=P(("groups", "mp", "sub"), "wide"),
        check_vma=False,
    )
```

```python
import functools

import jax
import jax.numpy as jnp
import numpy as np
from jax import lax
from jax.experimental import pallas as pl
from jax.experimental.pallas import tpu as pltpu
from jax.sharding import PartitionSpec as P

MOST = 2
INNER = ("mp", "sub")
SWAP = [(0, 1), (1, 0)]


def tile_of(depth, most=1024):
    parts = 1
    while depth % parts or (depth // parts) % 128 or depth // parts > most:
        parts += 1
    return depth // parts


def started(sources, places, ready):
    copies = []
    for index, (source, place) in enumerate(zip(sources, places)):
        copies.append(pltpu.make_async_copy(source, place, ready.at[index]))
        copies[-1].start()
    return copies


def weight_copies(lane, weights, held, ready):
    tiles, tile = held.shape[1:3]
    first = pl.multiple_of(lane * tiles * tile, 128)
    sources = [w.at[pl.ds(first + i * tile, tile)] for i in range(tiles) for w in weights]
    places = [held.at[which, i] for i in range(tiles) for which in (0, 1)]
    return started(sources, places, ready)


def weight_products(rows_of, held, sums, copies=None):
    tiles, tile = held.shape[1:3]
    for total in sums:
        total[...] = jnp.zeros_like(total)
    for index in range(tiles):
        rows = rows_of(slice(index * tile, (index + 1) * tile))
        for which, total in enumerate(sums):
            if copies:
                copies[2 * index + which].wait()
            total[...] += jnp.dot(rows, held[which, index], preferred_element_type=jnp.float32)


def factor_products(rows_of, table, low):
    depth = table.shape[1]
    tile = tile_of(depth)
    total = jnp.zeros(low.shape, jnp.float32)
    for index in range(depth // tile):
        here = slice(index * tile, (index + 1) * tile)
        total += lax.dot_general(
            rows_of(here), table[:, here], (((1,), (1,)), ((), ())), preferred_element_type=jnp.float32
        )
    low[...] = total


def in_lanes(lane, total, index, height):
    first = total[2 * index * height : (2 * index + 1) * height]
    other = total[(2 * index + 1) * height : (2 * index + 2) * height]
    whole = jnp.concatenate([first, other], axis=0)
    turned = jnp.concatenate([other, first], axis=0)
    return jnp.where(lane == 0, whole, turned)


def compacted(choice, low):
    high = low.astype(jnp.bfloat16)
    rest = low - high.astype(jnp.float32)
    middle = rest.astype(jnp.bfloat16)
    tail = (rest - middle.astype(jnp.float32)).astype(jnp.bfloat16)
    picked = jnp.dot(
        choice,
        jnp.concatenate([high, middle, tail], axis=1),
        preferred_element_type=jnp.float32,
    )
    size = low.shape[1]
    total = picked[:, :size] + (picked[:, size : 2 * size] + picked[:, 2 * size :])
    count, rank = choice.shape[0] // 2, size // 2
    return total[:count, :rank], total[count:, rank:]


def early_kernel(count, facts, *refs):
    pieces, refs = refs[:count], refs[count:]
    (factors, choices), weights, refs = refs[:2], refs[2:4], refs[4:]
    owns, rests, (compact, held), refs = refs[:2], refs[2:4], refs[4:6], refs[6:]
    sums, (low, ready) = refs[:2], refs[2:]
    rows_of = lambda here: jnp.concatenate([piece[:, here] for piece in pieces], axis=0)
    in_flight = weight_copies(facts[0], weights, held, ready)
    factor_products(rows_of, factors, low)
    weight_products(rows_of, held, sums, in_flight)
    height = owns[0].shape[1] // 2
    for own, rest, total in zip(owns, rests, sums):
        own[0] = in_lanes(facts[0], total, 0, height)
        for index in range(1, count):
            rest[index - 1] = in_lanes(facts[0], total, index, height)
    compact[0], compact[1] = compacted(choices[...], low[...])


def share(flag, near, away, outs, pair):
    (near_own, near_sib), (away_own, away_sib) = near, away
    kept, to_sib, to_mp, to_both = outs
    kept[pair] = jnp.where(flag == 1, near_own, away_own)
    to_sib[pair] = jnp.where(flag == 1, near_sib, away_sib)
    to_mp[pair] = jnp.where(flag == 1, away_own, near_own).astype(to_mp.dtype)
    to_both[pair] = jnp.where(flag == 1, away_sib, near_sib).astype(to_both.dtype)


def middle_kernel(facts, piece, other, *refs):
    (held, factors, choices, compact_in, base, base_sib), refs = refs[:6], refs[6:]
    (own, sib, compact), sums, low = refs[:3], refs[3:5], refs[5]
    outs = own.at[0], sib.at[0], own.at[1], sib.at[1]
    rows_of = lambda here: jnp.concatenate([piece[:, here], other[:, here]], axis=0)
    factor_products(rows_of, factors, low)
    weight_products(rows_of, held, sums)
    pairs, group = own.shape[1:3]
    fresh = [[in_lanes(facts[0], total, index, group // 2) for total in sums] for index in (0, 1)]
    lane = facts[0]
    ahead = [jnp.where(lane == 0, b, a) for a, b in zip(*fresh)]
    behind = [jnp.where(lane == 0, a, b) for a, b in zip(*fresh)]
    for pair in range(pairs):
        step, back = pair + 1, pairs - pair
        near, away = 2 * step - 1 - lane, 2 * back - 2 + lane
        near = ahead if step == pairs else (base[near], base_sib[near])
        away = behind if back == pairs else (base[away], base_sib[away])
        share(facts[2 + step], near, away, outs, pair)
    for which, fresh_low in enumerate(compacted(choices[...], low[...])):
        compact[which] = compact_in[which] + fresh_low


def low_kernel(facts, piece, factors, choices, compact_in, kept, sent, low):
    half = kept.shape[1]
    factor_products(lambda here: piece[:, here], factors, low)
    for which, fresh_low in enumerate(compacted(choices[...], low[...])):
        total = compact_in[which] + fresh_low
        kept[which] = jnp.where(facts[1] == 0, total[:half], total[half:])
        sent[which] = jnp.where(facts[1] == 0, total[half:], total[:half])


def last_kernel(facts, piece, held, base, base_sib, *refs):
    outs, sums = refs[:4], refs[4:]
    weight_products(lambda here: piece[:, here], held, sums)
    away = [in_lanes(facts[0], total, 0, piece.shape[0] // 2) for total in sums]
    share(facts[2], (base[0], base_sib[0]), away, outs, 0)


def delta_kernel(pairs, facts, low, spots, mask, copies, second, kept, got, out):
    f32 = jnp.float32
    own = jnp.dot(spots[...], low[...], preferred_element_type=f32).astype(jnp.bfloat16)
    spread = jnp.dot(own, copies[...], preferred_element_type=f32).astype(jnp.bfloat16) * mask[...]
    out[...] = jnp.dot(spread, second[...], preferred_element_type=f32).reshape(out.shape)
    for pair in range(1, pairs):
        place = facts[2 + pairs + pair]
        out[place] = out[place] + (kept[pair - 1] + got[pair - 1].astype(f32))


def final_kernel(pairs, facts, rest, kept, got_sib, got_mp, got_both, out):
    f32 = jnp.float32
    value = kept[0] + got_sib[0] + (got_mp[0].astype(f32) + got_both[0].astype(f32))
    for place in range(out.shape[0]):
        there = jnp.where(facts[2 + pairs] == place, value, 0)
        out[place] = (rest[place] + there).astype(out.dtype)


def kernel_call(kernel, facts, arrays, shapes, scratch, flops, weights=(), grant=12):
    in_vmem = pl.BlockSpec(memory_space=pltpu.VMEM)
    if weights:
        scratch = scratch + [pltpu.SemaphoreType.DMA((len(weights) * shapes[-1][0][1],))]
    return pl.pallas_call(
        kernel,
        in_specs=[pl.BlockSpec(memory_space=pltpu.SMEM)]
        + [in_vmem] * len(arrays)
        + [pl.BlockSpec(memory_space=pl.ANY)] * len(weights),
        out_specs=[in_vmem] * len(shapes),
        out_shape=[jax.ShapeDtypeStruct(shape, kind) for shape, kind in shapes],
        scratch_shapes=scratch,
        compiler_params=pltpu.CompilerParams(vmem_limit_bytes=grant * 2**20),
        cost_estimate=pl.CostEstimate(
            flops=flops // 32, bytes_accessed=flops // 1024, transcendentals=0
        ),
    )(facts, *arrays, *weights)


def hidden_of(gate, up):
    return (jax.nn.silu(gate.astype(jnp.float32)) * up.astype(jnp.float32)).astype(jnp.bfloat16)


def slots_of(row_adapter_index, adapter_storage_slot):
    names = jnp.arange(adapter_storage_slot.shape[0], dtype=jnp.int32)
    same = row_adapter_index == names[None, :]
    return jnp.sum(jnp.where(same, adapter_storage_slot[None, :], 0), axis=1)


def gathered(
    gate_activation,
    up_activation,
    down_base_weight,
    first_factor_table,
    second_factor_table,
    row_adapter_index,
    adapter_storage_slot,
):
    hidden = hidden_of(gate_activation, up_activation)
    row_count = hidden.shape[0]
    owners = lax.axis_size("wide")
    local_adapter = first_factor_table.shape[0]
    slots = local_adapter * owners
    rank_portion = second_factor_table.shape[1]
    home = lax.axis_index("wide")
    slot_all = slots_of(row_adapter_index, adapter_storage_slot)
    blocks = slot_all.reshape(owners, row_count)
    order = jnp.arange(row_count, dtype=jnp.int32)
    earlier = (blocks[:, :, None] == blocks[:, None, :]) & (order[None, :] < order[:, None])
    position = jnp.sum(earlier.astype(jnp.int32), axis=2)
    rows = lax.all_gather(hidden, "wide", axis=0, tiled=True)
    base = jnp.dot(rows, down_base_weight, preferred_element_type=jnp.float32)
    low = jnp.einsum("re,nqe->nrq", rows, first_factor_table, preferred_element_type=jnp.float32)
    low = low.reshape(local_adapter, owners, row_count, low.shape[2])
    own = home * local_adapter + jnp.arange(local_adapter, dtype=jnp.int32)
    kept = []
    for item in range(MOST):
        mask = (blocks[None] == own[:, None, None]) & (position == item)[None]
        kept.append(jnp.sum(jnp.where(mask[..., None], low, 0), axis=2))
    low = lax.psum_scatter(jnp.stack(kept, axis=2), INNER, scatter_dimension=3, tiled=True)
    low = lax.all_gather(low.astype(jnp.bfloat16), "wide", axis=0, tiled=True)
    spread = 0
    for item in range(MOST):
        mask = (blocks[None] == jnp.arange(slots, dtype=jnp.int32)[:, None, None]) & (position == item)
        spread += jnp.where(mask[..., None], low[:, :, item][:, :, None], 0)
    spread = spread.reshape(slots, owners * row_count, rank_portion)
    delta = jnp.einsum("srq,sqw->rw", spread, second_factor_table, preferred_element_type=jnp.float32)
    total = base + delta
    return lax.psum_scatter(total, INNER, scatter_dimension=0, tiled=True).astype(jnp.bfloat16)


def ring_order(nodes):
    return list(range(0, nodes, 2)) + list(range(nodes - 1, 0, -2))


def ringed(
    gate_activation,
    up_activation,
    down_base_weight,
    first_factor_table,
    second_factor_table,
    row_adapter_index,
    adapter_storage_slot,
):
    f32, bf16 = jnp.float32, jnp.bfloat16
    row_count, width_part = gate_activation.shape
    owners = lax.axis_size("wide")
    nodes = owners // 2
    far = nodes // 2
    steps = far - 1
    own_nodes = nodes // 2
    own_blocks = owners // 2
    group_rows = 2 * row_count
    order = ring_order(nodes)
    depth = width_part // 2
    width = down_base_weight.shape[1]
    rank = first_factor_table.shape[1]

    table = []
    for w in range(owners):
        p = order.index(w // 2)
        at = lambda shift: order[(p + shift) % nodes]
        ways = (-1, 1) if w % 2 == 0 else (1, -1)
        arrivals = [at(0)] + [at(s * k) for k in range(1, far) for s in ways] + [at(far)]
        row = [2 * node + (w % 2 ^ side) for node in arrivals for side in (0, 1)]
        for half in (0, 1):
            here = [(at(s) < own_nodes) == (half == 0) for s in range(far)]
            row += [int(h) for h in here]
            row += [at(s if h else s + far) % own_nodes for s, h in enumerate(here)]
        table.append(row)
    home = lax.axis_index("wide")
    part = lax.axis_index(INNER)
    side = jnp.bitwise_and(home, 1)

    def moved(shift, cross=0):
        return [
            (order[p] * 2 + c, order[(p + shift) % nodes] * 2 + (c ^ cross))
            for p in range(nodes)
            for c in (0, 1)
        ]

    def send(value, shift, cross=0):
        return lax.ppermute(value, "wide", moved(shift, cross))

    def turn(value, way):
        to_right, to_left = moved(way), moved(-way)
        pairs = [pair for pair in to_right if pair[0] % 2 == 0]
        pairs += [pair for pair in to_left if pair[0] % 2 == 1]
        return lax.ppermute(value, "wide", pairs)

    def half_of(value, which, axis):
        return lax.dynamic_slice_in_dim(value, which * depth, depth, axis)

    crossed = [(2 * w + m, 2 * (w ^ 1) + (1 - m)) for w in range(owners) for m in (0, 1)]

    def to_three(to_sib, to_mp, to_both):
        return (
            send(to_sib, 0, 1),
            lax.ppermute(to_mp, INNER, SWAP),
            lax.ppermute(to_both, ("wide",) + INNER, crossed),
        )

    give = hidden_of(half_of(gate_activation, 1 - side, 1), half_of(up_activation, 1 - side, 1))
    keep_side, give = lax.optimization_barrier((side, give))
    keep = hidden_of(half_of(gate_activation, keep_side, 1), half_of(up_activation, keep_side, 1))
    block = jnp.concatenate([keep, send(give, 0, 1)], axis=0)
    one_way, other_way = turn(block, 1), turn(block, -1)

    weight, first, second_factor_table, block = lax.optimization_barrier(
        (down_base_weight, first_factor_table[0], second_factor_table, block)
    )
    other_second = lax.ppermute(second_factor_table, INNER, SWAP)
    weights = (weight, send(weight, 0, 1))
    factors = jnp.concatenate(
        [half_of(first, side, 1), half_of(send(first, 0, 1), side, 1)], axis=0
    )
    home_late, row_adapter_index, weights = lax.optimization_barrier(
        (home, row_adapter_index, weights)
    )

    pieces = [block, one_way, other_way]
    for step in range(2, steps + 1):
        one_way, other_way = turn(one_way, 1), turn(other_way, -1)
        if step < steps:
            one_way, other_way = lax.optimization_barrier((one_way, other_way))
            pieces += [one_way, other_way]

    row = lax.dynamic_index_in_dim(
        jnp.asarray(np.array(table, np.int32)), home_late, 0, keepdims=False
    )
    edges = np.cumsum([0, 2 * nodes, far, far, far, far])
    arrived, *rest = [row[a:b] for a, b in zip(edges[:-1], edges[1:])]
    facts = jnp.concatenate(
        [side[None], part[None].astype(jnp.int32)]
        + [jnp.where(part == 0, a, b) for a, b in zip(rest[:2], rest[2:])]
    )
    slot_all = slots_of(row_adapter_index, adapter_storage_slot).reshape(owners, row_count)
    ranks = jnp.arange(row_count, dtype=jnp.int32)
    earlier = (slot_all[:, :, None] == slot_all[:, None, :]) & (ranks[None, :] < ranks[:, None])
    position = jnp.sum(earlier.astype(jnp.int32), axis=2)
    blocks = jnp.arange(owners, dtype=jnp.int32)

    items = jnp.arange(owners * MOST, dtype=jnp.int32)
    came = arrived[:, None] == blocks[None, :]
    slot_came = jnp.sum(jnp.where(came[:, :, None], slot_all[None], 0), axis=1).reshape(1, -1)
    place_came = jnp.sum(
        jnp.where(came[:, :, None], position[None] + MOST * blocks[None, :, None], 0), axis=1
    ).reshape(1, -1)
    chosen = jnp.concatenate(
        [
            ((place_came == items[:, None]) & (slot_came == slot)).astype(bf16)
            for slot in (home_late, jnp.bitwise_xor(home_late, 1))
        ],
        axis=0,
    )
    early_rows = len(pieces) * group_rows
    middle_rows = early_rows + 2 * group_rows
    choices = [
        chosen[:, :early_rows],
        chosen[:, early_rows:middle_rows],
        chosen[:, middle_rows:],
    ]

    half = own_blocks * MOST
    here = own_blocks * row_count
    slot_here = lax.dynamic_slice_in_dim(slot_all, part * own_blocks, own_blocks).reshape(here, 1)
    position_here = lax.dynamic_slice_in_dim(position, part * own_blocks, own_blocks)
    block_here = jnp.arange(here, dtype=jnp.int32)[:, None] // row_count
    spot = (
        jnp.bitwise_xor(slot_here, home_late) * half
        + block_here * MOST
        + position_here.reshape(here, 1)
    )
    spots = (spot == jnp.arange(owners * half, dtype=jnp.int32)[None, :]).astype(bf16)
    piece = rank // 2
    column = jnp.arange(owners * rank, dtype=jnp.int32)[None, :]
    own_rank = jnp.bitwise_xor(part, column // (owners * piece)) * piece + column % piece
    mask = (slot_here == column // piece % owners).astype(bf16)
    copies = (jnp.arange(rank, dtype=jnp.int32)[:, None] == own_rank).astype(bf16)

    second = jnp.concatenate(
        [values.reshape(owners * piece, width) for values in (second_factor_table, other_second)],
        axis=0,
    )

    compact_shape = ((2, owners * MOST, rank), f32)
    tile = tile_of(depth)

    def sums(rows, with_low=True):
        columns = [width, width] + [2 * rank] * with_low
        return [pltpu.VMEM((rows, size), f32) for size in columns]

    def flops(rows, columns):
        return 2 * rows * depth * columns

    facts, spots, mask, copies, choices, second = lax.optimization_barrier(
        (facts, spots, mask, copies, choices, second)
    )
    *early, held = kernel_call(
        functools.partial(early_kernel, len(pieces)),
        facts,
        (*pieces, factors, choices[0]),
        [((1, group_rows, width), f32)] * 2
        + [((len(pieces) - 1, group_rows, width), f32)] * 2
        + [compact_shape, ((2, depth // tile, tile, width), bf16)],
        sums(early_rows),
        flops(early_rows, 2 * (width + rank)),
        weights,
        32,
    )
    one_way, other_way, early, held = lax.optimization_barrier((one_way, other_way, early, held))

    last = turn(one_way, 1)

    def shares(pairs):
        shape = (pairs, group_rows, width)
        return [(shape, f32)] * 2 + [(shape, bf16)] * 2

    own_more, sib_more, compact = kernel_call(
        middle_kernel,
        facts,
        (one_way, other_way, held, factors, choices[1], early[4], early[2], early[3]),
        [((2, far - 1, group_rows, width), f32)] * 2 + [compact_shape],
        sums(2 * group_rows),
        flops(2 * group_rows, 2 * (width + rank)),
    )

    kept_more, out_more = [a + b for a, b in zip(own_more, send(sib_more, 0, 1))]
    out_more = out_more.astype(bf16)
    last, compact = lax.optimization_barrier((last, compact))

    kept, sent = kernel_call(
        low_kernel,
        facts,
        (last, factors, choices[2], compact),
        [((2, half, rank), f32)] * 2,
        [pltpu.VMEM((group_rows, 2 * rank), f32)],
        flops(group_rows, 2 * rank),
    )
    got = to_three(kept, sent, sent)
    low = (kept + got[1] + (got[0] + got[2])[::-1]).astype(bf16)

    def from_node(value, gap):
        return lax.ppermute(value, "wide", [(w, w ^ (2 * gap)) for w in range(owners)])

    def gather(value, gap, reach):
        parts = [from_node(value, gap * k) for k in range(1, reach)]
        return jnp.concatenate([value] + parts, axis=0)

    low, out_more, last = lax.optimization_barrier((low, out_more, last))
    got_more = lax.ppermute(out_more, INNER, SWAP)
    reach = min(4, nodes)
    low = gather(low, 1, reach)

    kept_one, *one = kernel_call(
        last_kernel,
        facts,
        (last, held, early[0], early[1]),
        shares(1),
        sums(group_rows, False),
        flops(group_rows, 2 * width),
    )
    low, one, got_more = lax.optimization_barrier((low, one, got_more))
    gap = reach
    while gap < nodes:
        low = gather(low, gap, 2)
        gap *= 2
    got_one = to_three(*one)

    shape = (own_nodes, group_rows, width)
    rest = kernel_call(
        functools.partial(delta_kernel, far),
        facts,
        (low.reshape(owners * half, rank), spots, mask, copies, second, kept_more, got_more),
        [(shape, f32)],
        [],
        2 * here * owners * rank * width,
    )[0]
    out = kernel_call(
        functools.partial(final_kernel, far),
        facts,
        (rest, kept_one, *got_one),
        [(shape, bf16)],
        [],
        here * width,
    )[0]
    return out.reshape(-1, width)


def solution(mesh):
    shape = dict(mesh.shape)
    wide, inner = shape["wide"], shape["mp"] * shape["sub"]
    paired = shape["sub"] == 1 and inner == 2 and wide % 8 == 0 and wide & (wide - 1) == 0
    if paired:
        nodes = wide // 2
        order = ring_order(nodes)
        paired = all(
            (order[p] < nodes // 2) != (order[(p + nodes // 2) % nodes] < nodes // 2)
            for p in range(nodes)
        )
    return jax.shard_map(
        ringed if paired else gathered,
        mesh=mesh,
        in_specs=(
            P(("groups", "wide"), ("mp", "sub")),
            P(("groups", "wide"), ("mp", "sub")),
            P(("mp", "sub"), "wide"),
            P("wide", None, ("mp", "sub")),
            P(None, ("mp", "sub"), "wide"),
            P("groups", None),
            P(),
        ),
        out_specs=P(("groups", "mp", "sub"), "wide"),
        check_vma=False,
    )
```

```python
import functools

import jax
import jax.numpy as jnp
import numpy as np
from jax import lax
from jax.experimental import pallas as pl
from jax.experimental.pallas import tpu as pltpu
from jax.sharding import PartitionSpec as P

MOST = 2
INNER = ("mp", "sub")
SWAP = [(0, 1), (1, 0)]


def tile_of(depth, most=1024):
    parts = 1
    while depth % parts or (depth // parts) % 128 or depth // parts > most:
        parts += 1
    return depth // parts


def started(sources, places, ready):
    copies = []
    for index, (source, place) in enumerate(zip(sources, places)):
        copies.append(pltpu.make_async_copy(source, place, ready.at[index]))
        copies[-1].start()
    return copies


def weight_copies(lane, weights, held, ready):
    tiles, tile = held.shape[1:3]
    first = pl.multiple_of(lane * tiles * tile, 128)
    sources = [w.at[pl.ds(first + i * tile, tile)] for i in range(tiles) for w in weights]
    places = [held.at[which, i] for i in range(tiles) for which in (0, 1)]
    return started(sources, places, ready)


def weight_products(rows_of, held, sums, copies=None):
    tiles, tile = held.shape[1:3]
    for total in sums:
        total[...] = jnp.zeros_like(total)
    for index in range(tiles):
        rows = rows_of(slice(index * tile, (index + 1) * tile))
        for which, total in enumerate(sums):
            if copies:
                copies[2 * index + which].wait()
            total[...] += jnp.dot(rows, held[which, index], preferred_element_type=jnp.float32)


def factor_products(rows_of, table, low):
    depth = table.shape[1]
    tile = tile_of(depth)

    def product(here):
        return lax.dot_general(
            rows_of(here), table[:, here], (((1,), (1,)), ((), ())), preferred_element_type=jnp.float32
        )

    if low.shape[0] <= 128:
        total = jnp.zeros(low.shape, jnp.float32)
        for index in range(depth // tile):
            total += product(slice(index * tile, (index + 1) * tile))
        low[...] = total
        return
    low[...] = jnp.zeros_like(low)

    def step(index, carry):
        low[...] += product(pl.ds(pl.multiple_of(index * tile, 128), tile))
        return carry

    lax.fori_loop(0, depth // tile, step, 0)


def in_lanes(lane, total, index, height):
    first = total[2 * index * height : (2 * index + 1) * height]
    other = total[(2 * index + 1) * height : (2 * index + 2) * height]
    whole = jnp.concatenate([first, other], axis=0)
    turned = jnp.concatenate([other, first], axis=0)
    return jnp.where(lane == 0, whole, turned)


def compacted(choice, low):
    high = low.astype(jnp.bfloat16)
    rest = low - high.astype(jnp.float32)
    middle = rest.astype(jnp.bfloat16)
    tail = (rest - middle.astype(jnp.float32)).astype(jnp.bfloat16)
    picked = jnp.dot(
        choice,
        jnp.concatenate([high, middle, tail], axis=1),
        preferred_element_type=jnp.float32,
    )
    size = low.shape[1]
    total = picked[:, :size] + (picked[:, size : 2 * size] + picked[:, 2 * size :])
    count, rank = choice.shape[0] // 2, size // 2
    return total[:count, :rank], total[count:, rank:]


def early_kernel(count, facts, *refs):
    pieces, refs = refs[:count], refs[count:]
    (factors, choices), weights, refs = refs[:2], refs[2:4], refs[4:]
    owns, rests, (compact, held), refs = refs[:2], refs[2:4], refs[4:6], refs[6:]
    sums, (low, ready) = refs[:2], refs[2:]
    rows_of = lambda here: jnp.concatenate([piece[:, here] for piece in pieces], axis=0)
    in_flight = weight_copies(facts[0], weights, held, ready)
    factor_products(rows_of, factors, low)
    weight_products(rows_of, held, sums, in_flight)
    height = owns[0].shape[1] // 2
    for own, rest, total in zip(owns, rests, sums):
        own[0] = in_lanes(facts[0], total, 0, height)
        for index in range(1, count):
            rest[index - 1] = in_lanes(facts[0], total, index, height)
    compact[0], compact[1] = compacted(choices[...], low[...])


def share(flag, near, away, outs, pair):
    (near_own, near_sib), (away_own, away_sib) = near, away
    kept, to_sib, to_mp, to_both = outs
    kept[pair] = jnp.where(flag == 1, near_own, away_own)
    to_sib[pair] = jnp.where(flag == 1, near_sib, away_sib)
    to_mp[pair] = jnp.where(flag == 1, away_own, near_own).astype(to_mp.dtype)
    to_both[pair] = jnp.where(flag == 1, away_sib, near_sib).astype(to_both.dtype)


def middle_kernel(facts, piece, other, held, base, base_sib, own, sib, *sums):
    outs = own.at[0], sib.at[0], own.at[1], sib.at[1]
    rows_of = lambda here: jnp.concatenate([piece[:, here], other[:, here]], axis=0)
    weight_products(rows_of, held, sums)
    pairs, group = own.shape[1:3]
    fresh = [[in_lanes(facts[0], total, index, group // 2) for total in sums] for index in (0, 1)]
    lane = facts[0]
    ahead = [jnp.where(lane == 0, b, a) for a, b in zip(*fresh)]
    behind = [jnp.where(lane == 0, a, b) for a, b in zip(*fresh)]
    for pair in range(pairs):
        step, back = pair + 1, pairs - pair
        near, away = 2 * step - 1 - lane, 2 * back - 2 + lane
        near = ahead if step == pairs else (base[near], base_sib[near])
        away = behind if back == pairs else (base[away], base_sib[away])
        share(facts[2 + step], near, away, outs, pair)


def low_kernel(facts, piece, other, far_rows, factors, choices, compact_in, kept, sent, low, low_far):
    half = kept.shape[1]
    rows_of = lambda here: jnp.concatenate([piece[:, here], other[:, here]], axis=0)
    factor_products(rows_of, factors, low)
    factor_products(lambda here: far_rows[:, here], factors, low_far)
    both = jnp.concatenate([low[...], low_far[...]], axis=0)
    for which, fresh_low in enumerate(compacted(choices[...], both)):
        total = compact_in[which] + fresh_low
        kept[which] = jnp.where(facts[1] == 0, total[:half], total[half:])
        sent[which] = jnp.where(facts[1] == 0, total[half:], total[:half])


def last_kernel(facts, piece, held, base, base_sib, *refs):
    outs, sums = refs[:4], refs[4:]
    weight_products(lambda here: piece[:, here], held, sums)
    away = [in_lanes(facts[0], total, 0, piece.shape[0] // 2) for total in sums]
    share(facts[2], (base[0], base_sib[0]), away, outs, 0)


def delta_kernel(pairs, facts, low, spots, mask, copies, second, kept, got, out):
    f32 = jnp.float32
    own = jnp.dot(spots[...], low[...], preferred_element_type=f32).astype(jnp.bfloat16)
    spread = jnp.dot(own, copies[...], preferred_element_type=f32).astype(jnp.bfloat16) * mask[...]
    out[...] = jnp.dot(spread, second[...], preferred_element_type=f32).reshape(out.shape)
    for pair in range(1, pairs):
        place = facts[2 + pairs + pair]
        out[place] = out[place] + (kept[pair - 1] + got[pair - 1].astype(f32))


def final_kernel(pairs, facts, rest, kept, got_sib, got_mp, got_both, out):
    f32 = jnp.float32
    value = kept[0] + got_sib[0] + (got_mp[0].astype(f32) + got_both[0].astype(f32))
    for place in range(out.shape[0]):
        there = jnp.where(facts[2 + pairs] == place, value, 0)
        out[place] = (rest[place] + there).astype(out.dtype)


def kernel_call(kernel, facts, arrays, shapes, scratch, flops, weights=(), grant=12):
    in_vmem = pl.BlockSpec(memory_space=pltpu.VMEM)
    if weights:
        scratch = scratch + [pltpu.SemaphoreType.DMA((len(weights) * shapes[-1][0][1],))]
    return pl.pallas_call(
        kernel,
        in_specs=[pl.BlockSpec(memory_space=pltpu.SMEM)]
        + [in_vmem] * len(arrays)
        + [pl.BlockSpec(memory_space=pl.ANY)] * len(weights),
        out_specs=[in_vmem] * len(shapes),
        out_shape=[jax.ShapeDtypeStruct(shape, kind) for shape, kind in shapes],
        scratch_shapes=scratch,
        compiler_params=pltpu.CompilerParams(vmem_limit_bytes=grant * 2**20),
        cost_estimate=pl.CostEstimate(
            flops=flops // 32, bytes_accessed=flops // 1024, transcendentals=0
        ),
    )(facts, *arrays, *weights)


def hidden_of(gate, up):
    return (jax.nn.silu(gate.astype(jnp.float32)) * up.astype(jnp.float32)).astype(jnp.bfloat16)


def slots_of(row_adapter_index, adapter_storage_slot):
    names = jnp.arange(adapter_storage_slot.shape[0], dtype=jnp.int32)
    same = row_adapter_index == names[None, :]
    return jnp.sum(jnp.where(same, adapter_storage_slot[None, :], 0), axis=1)


def gathered(
    gate_activation,
    up_activation,
    down_base_weight,
    first_factor_table,
    second_factor_table,
    row_adapter_index,
    adapter_storage_slot,
):
    hidden = hidden_of(gate_activation, up_activation)
    row_count = hidden.shape[0]
    owners = lax.axis_size("wide")
    local_adapter = first_factor_table.shape[0]
    slots = local_adapter * owners
    rank_portion = second_factor_table.shape[1]
    home = lax.axis_index("wide")
    slot_all = slots_of(row_adapter_index, adapter_storage_slot)
    blocks = slot_all.reshape(owners, row_count)
    order = jnp.arange(row_count, dtype=jnp.int32)
    earlier = (blocks[:, :, None] == blocks[:, None, :]) & (order[None, :] < order[:, None])
    position = jnp.sum(earlier.astype(jnp.int32), axis=2)
    rows = lax.all_gather(hidden, "wide", axis=0, tiled=True)
    base = jnp.dot(rows, down_base_weight, preferred_element_type=jnp.float32)
    low = jnp.einsum("re,nqe->nrq", rows, first_factor_table, preferred_element_type=jnp.float32)
    low = low.reshape(local_adapter, owners, row_count, low.shape[2])
    own = home * local_adapter + jnp.arange(local_adapter, dtype=jnp.int32)
    kept = []
    for item in range(MOST):
        mask = (blocks[None] == own[:, None, None]) & (position == item)[None]
        kept.append(jnp.sum(jnp.where(mask[..., None], low, 0), axis=2))
    low = lax.psum_scatter(jnp.stack(kept, axis=2), INNER, scatter_dimension=3, tiled=True)
    low = lax.all_gather(low.astype(jnp.bfloat16), "wide", axis=0, tiled=True)
    spread = 0
    for item in range(MOST):
        mask = (blocks[None] == jnp.arange(slots, dtype=jnp.int32)[:, None, None]) & (position == item)
        spread += jnp.where(mask[..., None], low[:, :, item][:, :, None], 0)
    spread = spread.reshape(slots, owners * row_count, rank_portion)
    delta = jnp.einsum("srq,sqw->rw", spread, second_factor_table, preferred_element_type=jnp.float32)
    total = base + delta
    return lax.psum_scatter(total, INNER, scatter_dimension=0, tiled=True).astype(jnp.bfloat16)


def ring_order(nodes):
    return list(range(0, nodes, 2)) + list(range(nodes - 1, 0, -2))


def ringed(
    gate_activation,
    up_activation,
    down_base_weight,
    first_factor_table,
    second_factor_table,
    row_adapter_index,
    adapter_storage_slot,
):
    f32, bf16 = jnp.float32, jnp.bfloat16
    row_count, width_part = gate_activation.shape
    owners = lax.axis_size("wide")
    nodes = owners // 2
    far = nodes // 2
    steps = far - 1
    own_nodes = nodes // 2
    own_blocks = owners // 2
    group_rows = 2 * row_count
    order = ring_order(nodes)
    depth = width_part // 2
    width = down_base_weight.shape[1]
    rank = first_factor_table.shape[1]

    table = []
    for w in range(owners):
        p = order.index(w // 2)
        at = lambda shift: order[(p + shift) % nodes]
        ways = (-1, 1) if w % 2 == 0 else (1, -1)
        arrivals = [at(0)] + [at(s * k) for k in range(1, far) for s in ways] + [at(far)]
        row = [2 * node + (w % 2 ^ side) for node in arrivals for side in (0, 1)]
        for half in (0, 1):
            here = [(at(s) < own_nodes) == (half == 0) for s in range(far)]
            row += [int(h) for h in here]
            row += [at(s if h else s + far) % own_nodes for s, h in enumerate(here)]
        table.append(row)
    home = lax.axis_index("wide")
    part = lax.axis_index(INNER)
    side = jnp.bitwise_and(home, 1)

    def moved(shift, cross=0):
        return [
            (order[p] * 2 + c, order[(p + shift) % nodes] * 2 + (c ^ cross))
            for p in range(nodes)
            for c in (0, 1)
        ]

    def send(value, shift, cross=0):
        return lax.ppermute(value, "wide", moved(shift, cross))

    def turn(value, way):
        to_right, to_left = moved(way), moved(-way)
        pairs = [pair for pair in to_right if pair[0] % 2 == 0]
        pairs += [pair for pair in to_left if pair[0] % 2 == 1]
        return lax.ppermute(value, "wide", pairs)

    def half_of(value, which, axis):
        return lax.dynamic_slice_in_dim(value, which * depth, depth, axis)

    crossed = [(2 * w + m, 2 * (w ^ 1) + (1 - m)) for w in range(owners) for m in (0, 1)]

    def to_three(to_sib, to_mp, to_both):
        return (
            send(to_sib, 0, 1),
            lax.ppermute(to_mp, INNER, SWAP),
            lax.ppermute(to_both, ("wide",) + INNER, crossed),
        )

    give = hidden_of(half_of(gate_activation, 1 - side, 1), half_of(up_activation, 1 - side, 1))
    keep_side, give = lax.optimization_barrier((side, give))
    keep = hidden_of(half_of(gate_activation, keep_side, 1), half_of(up_activation, keep_side, 1))
    block = jnp.concatenate([keep, send(give, 0, 1)], axis=0)
    one_way, other_way = turn(block, 1), turn(block, -1)

    weight, first, second_factor_table, block = lax.optimization_barrier(
        (down_base_weight, first_factor_table[0], second_factor_table, block)
    )
    other_second = lax.ppermute(second_factor_table, INNER, SWAP)
    weights = (weight, send(weight, 0, 1))
    factors = jnp.concatenate(
        [half_of(first, side, 1), half_of(send(first, 0, 1), side, 1)], axis=0
    )
    home_late, part_late, row_adapter_index, other_second = lax.optimization_barrier(
        (home, part, row_adapter_index, other_second)
    )

    pieces = [block, one_way, other_way]
    for step in range(2, steps + 1):
        one_way, other_way = turn(one_way, 1), turn(other_way, -1)
        if step < steps:
            one_way, other_way = lax.optimization_barrier((one_way, other_way))
            pieces += [one_way, other_way]

    row = lax.dynamic_index_in_dim(
        jnp.asarray(np.array(table, np.int32)), home_late, 0, keepdims=False
    )
    edges = np.cumsum([0, 2 * nodes, far, far, far, far])
    arrived, *rest = [row[a:b] for a, b in zip(edges[:-1], edges[1:])]
    facts = jnp.concatenate(
        [side[None], part_late[None].astype(jnp.int32)]
        + [jnp.where(part_late == 0, a, b) for a, b in zip(rest[:2], rest[2:])]
    )
    slot_all = slots_of(row_adapter_index, adapter_storage_slot).reshape(owners, row_count)
    ranks = jnp.arange(row_count, dtype=jnp.int32)
    earlier = (slot_all[:, :, None] == slot_all[:, None, :]) & (ranks[None, :] < ranks[:, None])
    position = jnp.sum(earlier.astype(jnp.int32), axis=2)
    blocks = jnp.arange(owners, dtype=jnp.int32)

    items = jnp.arange(owners * MOST, dtype=jnp.int32)
    came = arrived[:, None] == blocks[None, :]
    slot_came = jnp.sum(jnp.where(came[:, :, None], slot_all[None], 0), axis=1).reshape(1, -1)
    place_came = jnp.sum(
        jnp.where(came[:, :, None], position[None] + MOST * blocks[None, :, None], 0), axis=1
    ).reshape(1, -1)
    chosen = jnp.concatenate(
        [
            ((place_came == items[:, None]) & (slot_came == slot)).astype(bf16)
            for slot in (home_late, jnp.bitwise_xor(home_late, 1))
        ],
        axis=0,
    )
    early_rows = len(pieces) * group_rows
    sides, places = jnp.arange(2, dtype=jnp.int32), jnp.arange(MOST, dtype=jnp.int32)
    far_wide = arrived[-2:]
    far_choice = (
        (sides[:, None, None, None, None, None] == sides[:, None, None])
        & (blocks[:, None, None, None, None] == far_wide[:, None])
        & (places[:, None, None, None] == places)
    )
    far_choice = far_choice.reshape(2 * owners * MOST, 4 * MOST).astype(bf16)
    choices = [
        chosen[:, :early_rows],
        jnp.concatenate([chosen[:, early_rows : early_rows + 2 * group_rows], far_choice], axis=1),
    ]

    own_is = jnp.bitwise_xor(home_late, sides)[:, None, None] == blocks[None, :, None]
    own_slot = jnp.sum(jnp.where(own_is, slot_all[None], 0), axis=1)
    own_position = jnp.sum(jnp.where(own_is, position[None], 0), axis=1)
    pick = (
        (sides[:, None, None, None] == sides[:, None])
        & (own_slot[:, None, None, :] == far_wide[:, None, None, None, None])
        & (own_position[:, None, None, :] == places[:, None, None])
    )
    pick = pick.reshape(4 * MOST, group_rows).astype(bf16)
    picked = jnp.dot(pick, block, preferred_element_type=f32).astype(bf16)
    far_rows = send(picked, far)

    half = own_blocks * MOST
    here = own_blocks * row_count
    slot_here = lax.dynamic_slice_in_dim(slot_all, part_late * own_blocks, own_blocks).reshape(here, 1)
    position_here = lax.dynamic_slice_in_dim(position, part_late * own_blocks, own_blocks)
    block_here = jnp.arange(here, dtype=jnp.int32)[:, None] // row_count
    spot = (
        jnp.bitwise_xor(slot_here, home_late) * half
        + block_here * MOST
        + position_here.reshape(here, 1)
    )
    spots = (spot == jnp.arange(owners * half, dtype=jnp.int32)[None, :]).astype(bf16)
    piece = rank // 2
    column = jnp.arange(owners * rank, dtype=jnp.int32)[None, :]
    own_rank = jnp.bitwise_xor(part_late, column // (owners * piece)) * piece + column % piece
    mask = (slot_here == column // piece % owners).astype(bf16)
    copies = (jnp.arange(rank, dtype=jnp.int32)[:, None] == own_rank).astype(bf16)

    other_second, far_rows = lax.optimization_barrier((other_second, far_rows))
    second = jnp.concatenate(
        [values.reshape(owners * piece, width) for values in (second_factor_table, other_second)],
        axis=0,
    )

    compact_shape = ((2, owners * MOST, rank), f32)
    tile = tile_of(depth)

    def sums(rows, with_low=True):
        columns = [width, width] + [2 * rank] * with_low
        return [pltpu.VMEM((rows, size), f32) for size in columns]

    def flops(rows, columns):
        return 2 * rows * depth * columns

    facts, spots, mask, copies, choices, second = lax.optimization_barrier(
        (facts, spots, mask, copies, choices, second)
    )
    *early, held = kernel_call(
        functools.partial(early_kernel, len(pieces)),
        facts,
        (*pieces, factors, choices[0]),
        [((1, group_rows, width), f32)] * 2
        + [((len(pieces) - 1, group_rows, width), f32)] * 2
        + [compact_shape, ((2, depth // tile, tile, width), bf16)],
        sums(early_rows),
        flops(early_rows, 2 * (width + rank)),
        weights,
        32,
    )
    one_way, other_way, early, held = lax.optimization_barrier((one_way, other_way, early, held))

    last = turn(one_way, 1)

    def shares(pairs):
        shape = (pairs, group_rows, width)
        return [(shape, f32)] * 2 + [(shape, bf16)] * 2

    kept, sent = kernel_call(
        low_kernel,
        facts,
        (one_way, other_way, far_rows, factors, choices[1], early[4]),
        [((2, half, rank), f32)] * 2,
        [pltpu.VMEM((rows, 2 * rank), f32) for rows in (2 * group_rows, 4 * MOST)],
        flops(2 * group_rows, 2 * rank),
    )
    kept, sent, one_way, other_way = lax.optimization_barrier((kept, sent, one_way, other_way))

    got = to_three(kept, sent, sent)

    own_more, sib_more = kernel_call(
        middle_kernel,
        facts,
        (one_way, other_way, held, early[2], early[3]),
        [((2, far - 1, group_rows, width), f32)] * 2,
        sums(2 * group_rows, False),
        flops(2 * group_rows, 2 * width),
    )
    kept_more, out_more = [a + b for a, b in zip(own_more, send(sib_more, 0, 1))]
    out_more = out_more.astype(bf16)

    kept_one, *one = kernel_call(
        last_kernel,
        facts,
        (last, held, early[0], early[1]),
        shares(1),
        sums(group_rows, False),
        1024 * flops(group_rows, 2 * width),
    )

    def from_node(value, gap):
        return lax.ppermute(value, "wide", [(w, w ^ (2 * gap)) for w in range(owners)])

    def gather(value, gap, reach):
        parts = [from_node(value, gap * k) for k in range(1, reach)]
        return jnp.concatenate([value] + parts, axis=0)

    got, one = lax.optimization_barrier((got, one))
    low = (kept + got[1] + (got[0] + got[2])[::-1]).astype(bf16)
    gap = 1
    while gap < nodes:
        reach = min(4, nodes // gap)
        low = gather(low, gap, reach)
        gap *= reach
    got_more = lax.ppermute(out_more, INNER, SWAP)
    got_one = to_three(*one)

    shape = (own_nodes, group_rows, width)
    rest = kernel_call(
        functools.partial(delta_kernel, far),
        facts,
        (low.reshape(owners * half, rank), spots, mask, copies, second, kept_more, got_more),
        [(shape, f32)],
        [],
        2 * here * owners * rank * width,
    )[0]
    out = kernel_call(
        functools.partial(final_kernel, far),
        facts,
        (rest, kept_one, *got_one),
        [(shape, bf16)],
        [],
        here * width,
    )[0]
    return out.reshape(-1, width)


def solution(mesh):
    shape = dict(mesh.shape)
    wide, inner = shape["wide"], shape["mp"] * shape["sub"]
    paired = shape["sub"] == 1 and inner == 2 and wide % 8 == 0 and wide & (wide - 1) == 0
    if paired:
        nodes = wide // 2
        order = ring_order(nodes)
        paired = all(
            (order[p] < nodes // 2) != (order[(p + nodes // 2) % nodes] < nodes // 2)
            for p in range(nodes)
        )
    return jax.shard_map(
        ringed if paired else gathered,
        mesh=mesh,
        in_specs=(
            P(("groups", "wide"), ("mp", "sub")),
            P(("groups", "wide"), ("mp", "sub")),
            P(("mp", "sub"), "wide"),
            P("wide", None, ("mp", "sub")),
            P(None, ("mp", "sub"), "wide"),
            P("groups", None),
            P(),
        ),
        out_specs=P(("groups", "mp", "sub"), "wide"),
        check_vma=False,
    )
```

```python
import functools

import jax
import jax.numpy as jnp
import numpy as np
from jax import lax
from jax.experimental import pallas as pl
from jax.experimental.pallas import tpu as pltpu
from jax.sharding import PartitionSpec as P

MOST = 2
INNER = ("mp", "sub")
SWAP = [(0, 1), (1, 0)]


def tile_of(depth, most=1024):
    parts = 1
    while depth % parts or (depth // parts) % 128 or depth // parts > most:
        parts += 1
    return depth // parts


def started(sources, places, ready):
    copies = []
    for index, (source, place) in enumerate(zip(sources, places)):
        copies.append(pltpu.make_async_copy(source, place, ready.at[index]))
        copies[-1].start()
    return copies


def weight_copies(lane, weights, held, ready):
    tiles, tile = held.shape[1:3]
    first = pl.multiple_of(lane * tiles * tile, 128)
    sources = [w.at[pl.ds(first + i * tile, tile)] for i in range(tiles) for w in weights]
    places = [held.at[which, i] for i in range(tiles) for which in (0, 1)]
    return started(sources, places, ready)


def weight_products(rows_of, held, sums, copies=None):
    tiles, tile = held.shape[1:3]
    for total in sums:
        total[...] = jnp.zeros_like(total)
    for index in range(tiles):
        rows = rows_of(slice(index * tile, (index + 1) * tile))
        for which, total in enumerate(sums):
            if copies:
                copies[2 * index + which].wait()
            total[...] += jnp.dot(rows, held[which, index], preferred_element_type=jnp.float32)


def factor_products(rows_of, table, low):
    depth = table.shape[1]
    tile = tile_of(depth)

    def product(here):
        return lax.dot_general(
            rows_of(here), table[:, here], (((1,), (1,)), ((), ())), preferred_element_type=jnp.float32
        )

    if low.shape[0] <= 128:
        total = jnp.zeros(low.shape, jnp.float32)
        for index in range(depth // tile):
            total += product(slice(index * tile, (index + 1) * tile))
        low[...] = total
        return
    low[...] = jnp.zeros_like(low)

    def step(index, carry):
        low[...] += product(pl.ds(pl.multiple_of(index * tile, 128), tile))
        return carry

    lax.fori_loop(0, depth // tile, step, 0)


def in_lanes(lane, total, index, height):
    first = total[2 * index * height : (2 * index + 1) * height]
    other = total[(2 * index + 1) * height : (2 * index + 2) * height]
    whole = jnp.concatenate([first, other], axis=0)
    turned = jnp.concatenate([other, first], axis=0)
    return jnp.where(lane == 0, whole, turned)


def compacted(choice, low):
    high = low.astype(jnp.bfloat16)
    rest = low - high.astype(jnp.float32)
    middle = rest.astype(jnp.bfloat16)
    tail = (rest - middle.astype(jnp.float32)).astype(jnp.bfloat16)
    picked = jnp.dot(
        choice,
        jnp.concatenate([high, middle, tail], axis=1),
        preferred_element_type=jnp.float32,
    )
    size = low.shape[1]
    total = picked[:, :size] + (picked[:, size : 2 * size] + picked[:, 2 * size :])
    count, rank = choice.shape[0] // 2, size // 2
    return total[:count, :rank], total[count:, rank:]


def early_kernel(count, facts, *refs):
    pieces, refs = refs[:count], refs[count:]
    (factors, choices), weights, refs = refs[:2], refs[2:4], refs[4:]
    owns, rests, (compact, held), refs = refs[:2], refs[2:4], refs[4:6], refs[6:]
    sums, (low, ready) = refs[:2], refs[2:]
    rows_of = lambda here: jnp.concatenate([piece[:, here] for piece in pieces], axis=0)
    in_flight = weight_copies(facts[0], weights, held, ready)
    factor_products(rows_of, factors, low)
    weight_products(rows_of, held, sums, in_flight)
    height = owns[0].shape[1] // 2
    for own, rest, total in zip(owns, rests, sums):
        own[0] = in_lanes(facts[0], total, 0, height)
        for index in range(1, count):
            rest[index - 1] = in_lanes(facts[0], total, index, height)
    compact[0], compact[1] = compacted(choices[...], low[...])


def share(flag, near, away, outs, pair):
    (near_own, near_sib), (away_own, away_sib) = near, away
    kept, to_sib, to_mp, to_both = outs
    kept[pair] = jnp.where(flag == 1, near_own, away_own)
    to_sib[pair] = jnp.where(flag == 1, near_sib, away_sib)
    to_mp[pair] = jnp.where(flag == 1, away_own, near_own).astype(to_mp.dtype)
    to_both[pair] = jnp.where(flag == 1, away_sib, near_sib).astype(to_both.dtype)


def middle_kernel(facts, piece, other, held, base, base_sib, own, sib, *sums):
    outs = own.at[0], sib.at[0], own.at[1], sib.at[1]
    rows_of = lambda here: jnp.concatenate([piece[:, here], other[:, here]], axis=0)
    weight_products(rows_of, held, sums)
    pairs, group = own.shape[1:3]
    fresh = [[in_lanes(facts[0], total, index, group // 2) for total in sums] for index in (0, 1)]
    lane = facts[0]
    ahead = [jnp.where(lane == 0, b, a) for a, b in zip(*fresh)]
    behind = [jnp.where(lane == 0, a, b) for a, b in zip(*fresh)]
    for pair in range(pairs):
        step, back = pair + 1, pairs - pair
        near, away = 2 * step - 1 - lane, 2 * back - 2 + lane
        near = ahead if step == pairs else (base[near], base_sib[near])
        away = behind if back == pairs else (base[away], base_sib[away])
        share(facts[2 + step], near, away, outs, pair)


def low_kernel(facts, piece, other, far_rows, factors, choices, compact_in, kept, sent, low, low_far):
    half = kept.shape[1]
    rows_of = lambda here: jnp.concatenate([piece[:, here], other[:, here]], axis=0)
    factor_products(rows_of, factors, low)
    factor_products(lambda here: far_rows[:, here], factors, low_far)
    both = jnp.concatenate([low[...], low_far[...]], axis=0)
    for which, fresh_low in enumerate(compacted(choices[...], both)):
        total = compact_in[which] + fresh_low
        kept[which] = jnp.where(facts[1] == 0, total[:half], total[half:])
        sent[which] = jnp.where(facts[1] == 0, total[half:], total[:half])


def last_kernel(facts, piece, held, base, base_sib, *refs):
    outs, sums = refs[:4], refs[4:]
    weight_products(lambda here: piece[:, here], held, sums)
    away = [in_lanes(facts[0], total, 0, piece.shape[0] // 2) for total in sums]
    share(facts[2], (base[0], base_sib[0]), away, outs, 0)


def delta_kernel(pairs, facts, low, spots, mask, copies, second, kept, got, out):
    f32 = jnp.float32
    own = jnp.dot(spots[...], low[...], preferred_element_type=f32).astype(jnp.bfloat16)
    spread = jnp.dot(own, copies[...], preferred_element_type=f32).astype(jnp.bfloat16) * mask[...]
    out[...] = jnp.dot(spread, second[...], preferred_element_type=f32).reshape(out.shape)
    for pair in range(1, pairs):
        place = facts[2 + pairs + pair]
        out[place] = out[place] + (kept[pair - 1] + got[pair - 1].astype(f32))


def final_kernel(pairs, facts, rest, kept, got_sib, got_mp, got_both, out):
    f32 = jnp.float32
    value = kept[0] + got_sib[0] + (got_mp[0].astype(f32) + got_both[0].astype(f32))
    for place in range(out.shape[0]):
        there = jnp.where(facts[2 + pairs] == place, value, 0)
        out[place] = (rest[place] + there).astype(out.dtype)


def kernel_call(kernel, facts, arrays, shapes, scratch, flops, weights=(), grant=12):
    in_vmem = pl.BlockSpec(memory_space=pltpu.VMEM)
    if weights:
        scratch = scratch + [pltpu.SemaphoreType.DMA((len(weights) * shapes[-1][0][1],))]
    return pl.pallas_call(
        kernel,
        in_specs=[pl.BlockSpec(memory_space=pltpu.SMEM)]
        + [in_vmem] * len(arrays)
        + [pl.BlockSpec(memory_space=pl.ANY)] * len(weights),
        out_specs=[in_vmem] * len(shapes),
        out_shape=[jax.ShapeDtypeStruct(shape, kind) for shape, kind in shapes],
        scratch_shapes=scratch,
        compiler_params=pltpu.CompilerParams(vmem_limit_bytes=grant * 2**20),
        cost_estimate=pl.CostEstimate(
            flops=flops // 32, bytes_accessed=flops // 1024, transcendentals=0
        ),
    )(facts, *arrays, *weights)


def hidden_of(gate, up):
    return (jax.nn.silu(gate.astype(jnp.float32)) * up.astype(jnp.float32)).astype(jnp.bfloat16)


def slots_of(row_adapter_index, adapter_storage_slot):
    names = jnp.arange(adapter_storage_slot.shape[0], dtype=jnp.int32)
    same = row_adapter_index == names[None, :]
    return jnp.sum(jnp.where(same, adapter_storage_slot[None, :], 0), axis=1)


def gathered(
    gate_activation,
    up_activation,
    down_base_weight,
    first_factor_table,
    second_factor_table,
    row_adapter_index,
    adapter_storage_slot,
):
    hidden = hidden_of(gate_activation, up_activation)
    row_count = hidden.shape[0]
    owners = lax.axis_size("wide")
    local_adapter = first_factor_table.shape[0]
    slots = local_adapter * owners
    rank_portion = second_factor_table.shape[1]
    home = lax.axis_index("wide")
    slot_all = slots_of(row_adapter_index, adapter_storage_slot)
    blocks = slot_all.reshape(owners, row_count)
    order = jnp.arange(row_count, dtype=jnp.int32)
    earlier = (blocks[:, :, None] == blocks[:, None, :]) & (order[None, :] < order[:, None])
    position = jnp.sum(earlier.astype(jnp.int32), axis=2)
    rows = lax.all_gather(hidden, "wide", axis=0, tiled=True)
    base = jnp.dot(rows, down_base_weight, preferred_element_type=jnp.float32)
    low = jnp.einsum("re,nqe->nrq", rows, first_factor_table, preferred_element_type=jnp.float32)
    low = low.reshape(local_adapter, owners, row_count, low.shape[2])
    own = home * local_adapter + jnp.arange(local_adapter, dtype=jnp.int32)
    kept = []
    for item in range(MOST):
        mask = (blocks[None] == own[:, None, None]) & (position == item)[None]
        kept.append(jnp.sum(jnp.where(mask[..., None], low, 0), axis=2))
    low = lax.psum_scatter(jnp.stack(kept, axis=2), INNER, scatter_dimension=3, tiled=True)
    low = lax.all_gather(low.astype(jnp.bfloat16), "wide", axis=0, tiled=True)
    spread = 0
    for item in range(MOST):
        mask = (blocks[None] == jnp.arange(slots, dtype=jnp.int32)[:, None, None]) & (position == item)
        spread += jnp.where(mask[..., None], low[:, :, item][:, :, None], 0)
    spread = spread.reshape(slots, owners * row_count, rank_portion)
    delta = jnp.einsum("srq,sqw->rw", spread, second_factor_table, preferred_element_type=jnp.float32)
    total = base + delta
    return lax.psum_scatter(total, INNER, scatter_dimension=0, tiled=True).astype(jnp.bfloat16)


def ring_order(nodes):
    return list(range(0, nodes, 2)) + list(range(nodes - 1, 0, -2))


def ringed(
    gate_activation,
    up_activation,
    down_base_weight,
    first_factor_table,
    second_factor_table,
    row_adapter_index,
    adapter_storage_slot,
):
    f32, bf16 = jnp.float32, jnp.bfloat16
    row_count, width_part = gate_activation.shape
    owners = lax.axis_size("wide")
    nodes = owners // 2
    far = nodes // 2
    steps = far - 1
    own_nodes = nodes // 2
    own_blocks = owners // 2
    group_rows = 2 * row_count
    order = ring_order(nodes)
    depth = width_part // 2
    width = down_base_weight.shape[1]
    rank = first_factor_table.shape[1]

    table = []
    for w in range(owners):
        p = order.index(w // 2)
        at = lambda shift: order[(p + shift) % nodes]
        ways = (-1, 1) if w % 2 == 0 else (1, -1)
        arrivals = [at(0)] + [at(s * k) for k in range(1, far) for s in ways] + [at(far)]
        row = [2 * node + (w % 2 ^ side) for node in arrivals for side in (0, 1)]
        for half in (0, 1):
            here = [(at(s) < own_nodes) == (half == 0) for s in range(far)]
            row += [int(h) for h in here]
            row += [at(s if h else s + far) % own_nodes for s, h in enumerate(here)]
        table.append(row)
    home = lax.axis_index("wide")
    part = lax.axis_index(INNER)
    side = jnp.bitwise_and(home, 1)

    def moved(shift, cross=0):
        return [
            (order[p] * 2 + c, order[(p + shift) % nodes] * 2 + (c ^ cross))
            for p in range(nodes)
            for c in (0, 1)
        ]

    def send(value, shift, cross=0):
        return lax.ppermute(value, "wide", moved(shift, cross))

    def turn(value, way):
        to_right, to_left = moved(way), moved(-way)
        pairs = [pair for pair in to_right if pair[0] % 2 == 0]
        pairs += [pair for pair in to_left if pair[0] % 2 == 1]
        return lax.ppermute(value, "wide", pairs)

    def half_of(value, which, axis):
        return lax.dynamic_slice_in_dim(value, which * depth, depth, axis)

    crossed = [(2 * w + m, 2 * (w ^ 1) + (1 - m)) for w in range(owners) for m in (0, 1)]

    def to_three(to_sib, to_mp, to_both):
        return (
            send(to_sib, 0, 1),
            lax.ppermute(to_mp, INNER, SWAP),
            lax.ppermute(to_both, ("wide",) + INNER, crossed),
        )

    give = hidden_of(half_of(gate_activation, 1 - side, 1), half_of(up_activation, 1 - side, 1))
    keep_side, give = lax.optimization_barrier((side, give))
    keep = hidden_of(half_of(gate_activation, keep_side, 1), half_of(up_activation, keep_side, 1))
    block = jnp.concatenate([keep, send(give, 0, 1)], axis=0)
    one_way, other_way = turn(block, 1), turn(block, -1)

    weight, first, second_factor_table, block = lax.optimization_barrier(
        (down_base_weight, first_factor_table[0], second_factor_table, block)
    )
    other_second = lax.ppermute(second_factor_table, INNER, SWAP)
    weights = (weight, send(weight, 0, 1))
    factors = jnp.concatenate(
        [half_of(first, side, 1), half_of(send(first, 0, 1), side, 1)], axis=0
    )
    home_late, part_late, row_adapter_index, other_second = lax.optimization_barrier(
        (home, part, row_adapter_index, other_second)
    )

    pieces = [block, one_way, other_way]
    for step in range(2, steps + 1):
        one_way, other_way = turn(one_way, 1), turn(other_way, -1)
        if step < steps:
            one_way, other_way = lax.optimization_barrier((one_way, other_way))
            pieces += [one_way, other_way]

    row = lax.dynamic_index_in_dim(
        jnp.asarray(np.array(table, np.int32)), home_late, 0, keepdims=False
    )
    edges = np.cumsum([0, 2 * nodes, far, far, far, far])
    arrived, *rest = [row[a:b] for a, b in zip(edges[:-1], edges[1:])]
    facts = jnp.concatenate(
        [side[None], part_late[None].astype(jnp.int32)]
        + [jnp.where(part_late == 0, a, b) for a, b in zip(rest[:2], rest[2:])]
    )
    slot_all = slots_of(row_adapter_index, adapter_storage_slot).reshape(owners, row_count)
    ranks = jnp.arange(row_count, dtype=jnp.int32)
    earlier = (slot_all[:, :, None] == slot_all[:, None, :]) & (ranks[None, :] < ranks[:, None])
    position = jnp.sum(earlier.astype(jnp.int32), axis=2)
    blocks = jnp.arange(owners, dtype=jnp.int32)

    items = jnp.arange(owners * MOST, dtype=jnp.int32)
    came = arrived[:, None] == blocks[None, :]
    slot_came = jnp.sum(jnp.where(came[:, :, None], slot_all[None], 0), axis=1).reshape(1, -1)
    place_came = jnp.sum(
        jnp.where(came[:, :, None], position[None] + MOST * blocks[None, :, None], 0), axis=1
    ).reshape(1, -1)
    chosen = jnp.concatenate(
        [
            ((place_came == items[:, None]) & (slot_came == slot)).astype(bf16)
            for slot in (home_late, jnp.bitwise_xor(home_late, 1))
        ],
        axis=0,
    )
    early_rows = len(pieces) * group_rows
    sides, places = jnp.arange(2, dtype=jnp.int32), jnp.arange(MOST, dtype=jnp.int32)
    far_wide = arrived[-2:]
    far_choice = (
        (sides[:, None, None, None, None, None] == sides[:, None, None])
        & (blocks[:, None, None, None, None] == far_wide[:, None])
        & (places[:, None, None, None] == places)
    )
    far_choice = far_choice.reshape(2 * owners * MOST, 4 * MOST).astype(bf16)
    choices = [
        chosen[:, :early_rows],
        jnp.concatenate([chosen[:, early_rows : early_rows + 2 * group_rows], far_choice], axis=1),
    ]

    own_is = jnp.bitwise_xor(home_late, sides)[:, None, None] == blocks[None, :, None]
    own_slot = jnp.sum(jnp.where(own_is, slot_all[None], 0), axis=1)
    own_position = jnp.sum(jnp.where(own_is, position[None], 0), axis=1)
    pick = (
        (sides[:, None, None, None] == sides[:, None])
        & (own_slot[:, None, None, :] == far_wide[:, None, None, None, None])
        & (own_position[:, None, None, :] == places[:, None, None])
    )
    pick = pick.reshape(4 * MOST, group_rows).astype(bf16)
    picked = jnp.dot(pick, block, preferred_element_type=f32).astype(bf16)
    far_rows = send(picked, far)

    half = own_blocks * MOST
    here = own_blocks * row_count
    slot_here = lax.dynamic_slice_in_dim(slot_all, part_late * own_blocks, own_blocks).reshape(here, 1)
    position_here = lax.dynamic_slice_in_dim(position, part_late * own_blocks, own_blocks)
    block_here = jnp.arange(here, dtype=jnp.int32)[:, None] // row_count
    spot = (
        jnp.bitwise_xor(slot_here, home_late) * half
        + block_here * MOST
        + position_here.reshape(here, 1)
    )
    spots = (spot == jnp.arange(owners * half, dtype=jnp.int32)[None, :]).astype(bf16)
    piece = rank // 2
    column = jnp.arange(owners * rank, dtype=jnp.int32)[None, :]
    own_rank = jnp.bitwise_xor(part_late, column // (owners * piece)) * piece + column % piece
    mask = (slot_here == column // piece % owners).astype(bf16)
    copies = (jnp.arange(rank, dtype=jnp.int32)[:, None] == own_rank).astype(bf16)

    other_second, far_rows = lax.optimization_barrier((other_second, far_rows))
    second = jnp.concatenate(
        [values.reshape(owners * piece, width) for values in (second_factor_table, other_second)],
        axis=0,
    )

    compact_shape = ((2, owners * MOST, rank), f32)
    tile = tile_of(depth)

    def sums(rows, with_low=True):
        columns = [width, width] + [2 * rank] * with_low
        return [pltpu.VMEM((rows, size), f32) for size in columns]

    def flops(rows, columns):
        return 2 * rows * depth * columns

    facts, spots, mask, copies, choices, second = lax.optimization_barrier(
        (facts, spots, mask, copies, choices, second)
    )
    *early, held = kernel_call(
        functools.partial(early_kernel, len(pieces)),
        facts,
        (*pieces, factors, choices[0]),
        [((1, group_rows, width), f32)] * 2
        + [((len(pieces) - 1, group_rows, width), f32)] * 2
        + [compact_shape, ((2, depth // tile, tile, width), bf16)],
        sums(early_rows),
        flops(early_rows, 2 * (width + rank)),
        weights,
        32,
    )
    one_way, other_way, early, held = lax.optimization_barrier((one_way, other_way, early, held))

    last = turn(one_way, 1)

    def shares(pairs):
        shape = (pairs, group_rows, width)
        return [(shape, f32)] * 2 + [(shape, bf16)] * 2

    kept, sent = kernel_call(
        low_kernel,
        facts,
        (one_way, other_way, far_rows, factors, choices[1], early[4]),
        [((2, half, rank), f32)] * 2,
        [pltpu.VMEM((rows, 2 * rank), f32) for rows in (2 * group_rows, 4 * MOST)],
        flops(2 * group_rows, 2 * rank),
    )
    kept, sent, one_way, other_way = lax.optimization_barrier((kept, sent, one_way, other_way))

    got = to_three(kept, sent, sent)

    own_more, sib_more = kernel_call(
        middle_kernel,
        facts,
        (one_way, other_way, held, early[2], early[3]),
        [((2, far - 1, group_rows, width), f32)] * 2,
        sums(2 * group_rows, False),
        flops(2 * group_rows, 2 * width),
    )
    kept_more, out_more = [a + b for a, b in zip(own_more, send(sib_more, 0, 1))]
    out_more = out_more.astype(bf16)

    kept_one, *one = kernel_call(
        last_kernel,
        facts,
        (last, held, early[0], early[1]),
        shares(1),
        sums(group_rows, False),
        1024 * flops(group_rows, 2 * width),
    )

    def from_node(value, gap):
        return lax.ppermute(value, "wide", [(w, w ^ (2 * gap)) for w in range(owners)])

    def gather(value, gap, reach):
        parts = [from_node(value, gap * k) for k in range(1, reach)]
        return jnp.concatenate([value] + parts, axis=0)

    got, one = lax.optimization_barrier((got, one))
    low = (kept + got[1] + (got[0] + got[2])[::-1]).astype(bf16)
    reach = min(4, nodes)
    low = gather(low, 1, reach)
    low, one[0] = lax.optimization_barrier((low, one[0]))
    while reach < nodes:
        low = gather(low, reach, 2)
        reach *= 2
    got_more = lax.ppermute(out_more, INNER, SWAP)
    got_one = to_three(*one)

    shape = (own_nodes, group_rows, width)
    rest = kernel_call(
        functools.partial(delta_kernel, far),
        facts,
        (low.reshape(owners * half, rank), spots, mask, copies, second, kept_more, got_more),
        [(shape, f32)],
        [],
        2 * here * owners * rank * width,
    )[0]
    out = kernel_call(
        functools.partial(final_kernel, far),
        facts,
        (rest, kept_one, *got_one),
        [(shape, bf16)],
        [],
        here * width,
    )[0]
    return out.reshape(-1, width)


def solution(mesh):
    shape = dict(mesh.shape)
    wide, inner = shape["wide"], shape["mp"] * shape["sub"]
    paired = shape["sub"] == 1 and inner == 2 and wide % 8 == 0 and wide & (wide - 1) == 0
    if paired:
        nodes = wide // 2
        order = ring_order(nodes)
        paired = all(
            (order[p] < nodes // 2) != (order[(p + nodes // 2) % nodes] < nodes // 2)
            for p in range(nodes)
        )
    return jax.shard_map(
        ringed if paired else gathered,
        mesh=mesh,
        in_specs=(
            P(("groups", "wide"), ("mp", "sub")),
            P(("groups", "wide"), ("mp", "sub")),
            P(("mp", "sub"), "wide"),
            P("wide", None, ("mp", "sub")),
            P(None, ("mp", "sub"), "wide"),
            P("groups", None),
            P(),
        ),
        out_specs=P(("groups", "mp", "sub"), "wide"),
        check_vma=False,
    )
```

```python
import functools

import jax
import jax.numpy as jnp
import numpy as np
from jax import lax
from jax.experimental import pallas as pl
from jax.experimental.pallas import tpu as pltpu
from jax.sharding import PartitionSpec as P

MOST = 2
INNER = ("mp", "sub")
SWAP = [(0, 1), (1, 0)]


def tile_of(depth, most=1024):
    parts = 1
    while depth % parts or (depth // parts) % 128 or depth // parts > most:
        parts += 1
    return depth // parts


def started(sources, places, ready):
    copies = []
    for index, (source, place) in enumerate(zip(sources, places)):
        copies.append(pltpu.make_async_copy(source, place, ready.at[index]))
        copies[-1].start()
    return copies


def weight_copies(lane, weights, held, ready):
    tiles, tile = held.shape[1:3]
    first = pl.multiple_of(lane * tiles * tile, 128)
    sources = [w.at[pl.ds(first + i * tile, tile)] for i in range(tiles) for w in weights]
    places = [held.at[which, i] for i in range(tiles) for which in (0, 1)]
    return started(sources, places, ready)


def weight_products(rows_of, held, sums, copies=None, first=0):
    tiles, tile = held.shape[1:3]
    for total in sums:
        total[...] = jnp.zeros_like(total)
    for index in range(tiles):
        rows = rows_of(slice(index * tile, (index + 1) * tile))
        for which, total in enumerate(sums):
            if copies:
                copies[2 * index + which].wait()
            total[...] += jnp.dot(rows, held[first + which, index], preferred_element_type=jnp.float32)


def factor_products(rows_of, table, low):
    depth = table.shape[1]
    tile = tile_of(depth)

    def product(here):
        return lax.dot_general(
            rows_of(here), table[:, here], (((1,), (1,)), ((), ())), preferred_element_type=jnp.float32
        )

    if low.shape[0] <= 128:
        total = jnp.zeros(low.shape, jnp.float32)
        for index in range(depth // tile):
            total += product(slice(index * tile, (index + 1) * tile))
        low[...] = total
        return
    low[...] = jnp.zeros_like(low)

    def step(index, carry):
        low[...] += product(pl.ds(pl.multiple_of(index * tile, 128), tile))
        return carry

    lax.fori_loop(0, depth // tile, step, 0)


def in_lanes(lane, total, index, height):
    first = total[2 * index * height : (2 * index + 1) * height]
    other = total[(2 * index + 1) * height : (2 * index + 2) * height]
    whole = jnp.concatenate([first, other], axis=0)
    turned = jnp.concatenate([other, first], axis=0)
    return jnp.where(lane == 0, whole, turned)


def compacted(choice, low):
    high = low.astype(jnp.bfloat16)
    rest = low - high.astype(jnp.float32)
    middle = rest.astype(jnp.bfloat16)
    tail = (rest - middle.astype(jnp.float32)).astype(jnp.bfloat16)
    picked = jnp.dot(
        choice,
        jnp.concatenate([high, middle, tail], axis=1),
        preferred_element_type=jnp.float32,
    )
    size = low.shape[1]
    total = picked[:, :size] + (picked[:, size : 2 * size] + picked[:, 2 * size :])
    count, rank = choice.shape[0] // 2, size // 2
    return total[:count, :rank], total[count:, rank:]


def early_kernel(count, facts, *refs):
    pieces, refs = refs[:count], refs[count:]
    (factors, choices), weights, refs = refs[:2], refs[2:4], refs[4:]
    owns, rests, (compact, held), refs = refs[:2], refs[2:4], refs[4:6], refs[6:]
    sums, (low, ready) = refs[:2], refs[2:]
    rows_of = lambda here: jnp.concatenate([piece[:, here] for piece in pieces], axis=0)
    in_flight = weight_copies(facts[0], weights, held, ready)
    factor_products(rows_of, factors, low)
    weight_products(rows_of, held, sums, in_flight)
    height = owns[0].shape[1] // 2
    for own, rest, total in zip(owns, rests, sums):
        own[0] = in_lanes(facts[0], total, 0, height)
        for index in range(1, count):
            rest[index - 1] = in_lanes(facts[0], total, index, height)
    compact[0], compact[1] = compacted(choices[...], low[...])


def share(flag, near, away, outs, pair):
    (near_own, near_sib), (away_own, away_sib) = near, away
    kept, to_sib, to_mp, to_both = outs
    kept[pair] = jnp.where(flag == 1, near_own, away_own)
    to_sib[pair] = jnp.where(flag == 1, near_sib, away_sib)
    to_mp[pair] = jnp.where(flag == 1, away_own, near_own).astype(to_mp.dtype)
    to_both[pair] = jnp.where(flag == 1, away_sib, near_sib).astype(to_both.dtype)


def middle_kernel(facts, piece, other, held, base, base_sib, own, sib, *sums):
    outs = own.at[0], sib.at[0], own.at[1], sib.at[1]
    rows_of = lambda here: jnp.concatenate([piece[:, here], other[:, here]], axis=0)
    weight_products(rows_of, held, sums)
    pairs, group = own.shape[1:3]
    fresh = [[in_lanes(facts[0], total, index, group // 2) for total in sums] for index in (0, 1)]
    lane = facts[0]
    ahead = [jnp.where(lane == 0, b, a) for a, b in zip(*fresh)]
    behind = [jnp.where(lane == 0, a, b) for a, b in zip(*fresh)]
    for pair in range(pairs):
        step, back = pair + 1, pairs - pair
        near, away = 2 * step - 1 - lane, 2 * back - 2 + lane
        near = ahead if step == pairs else (base[near], base_sib[near])
        away = behind if back == pairs else (base[away], base_sib[away])
        share(facts[2 + step], near, away, outs, pair)


def low_kernel(facts, piece, other, far_rows, factors, choices, compact_in, kept, sent, low, low_far):
    half = kept.shape[1]
    rows_of = lambda here: jnp.concatenate([piece[:, here], other[:, here]], axis=0)
    factor_products(rows_of, factors, low)
    factor_products(lambda here: far_rows[:, here], factors, low_far)
    both = jnp.concatenate([low[...], low_far[...]], axis=0)
    for which, fresh_low in enumerate(compacted(choices[...], both)):
        total = compact_in[which] + fresh_low
        kept[which] = jnp.where(facts[1] == 0, total[:half], total[half:])
        sent[which] = jnp.where(facts[1] == 0, total[half:], total[:half])


def last_kernel(which, facts, piece, held, base, mine, others, total):
    weight_products(lambda here: piece[:, here], held, [total], first=which)
    away = in_lanes(facts[0], total, 0, piece.shape[0] // 2)
    mine[0] = jnp.where(facts[2] == 1, base[0], away)
    others[0] = jnp.where(facts[2] == 1, away, base[0]).astype(others.dtype)


def delta_kernel(facts, low, spots, mask, copies, second, out):
    f32 = jnp.float32
    own = jnp.dot(spots[...], low[...], preferred_element_type=f32).astype(jnp.bfloat16)
    spread = jnp.dot(own, copies[...], preferred_element_type=f32).astype(jnp.bfloat16) * mask[...]
    out[...] = jnp.dot(spread, second[...], preferred_element_type=f32).reshape(out.shape)


def final_kernel(pairs, facts, delta, kept_more, got_more, kept, got_sib, got_mp, got_both, out):
    f32 = jnp.float32
    for pair in range(pairs):
        if pair:
            value = kept_more[pair - 1] + got_more[pair - 1].astype(f32)
        else:
            value = kept[0] + got_sib[0] + (got_mp[0].astype(f32) + got_both[0].astype(f32))
        place = facts[2 + pairs + pair]
        out[place] = (value + delta[place]).astype(out.dtype)


def kernel_call(kernel, facts, arrays, shapes, scratch, flops, weights=(), grant=12):
    in_vmem = pl.BlockSpec(memory_space=pltpu.VMEM)
    if weights:
        scratch = scratch + [pltpu.SemaphoreType.DMA((len(weights) * shapes[-1][0][1],))]
    return pl.pallas_call(
        kernel,
        in_specs=[pl.BlockSpec(memory_space=pltpu.SMEM)]
        + [in_vmem] * len(arrays)
        + [pl.BlockSpec(memory_space=pl.ANY)] * len(weights),
        out_specs=[in_vmem] * len(shapes),
        out_shape=[jax.ShapeDtypeStruct(shape, kind) for shape, kind in shapes],
        scratch_shapes=scratch,
        compiler_params=pltpu.CompilerParams(vmem_limit_bytes=grant * 2**20),
        cost_estimate=pl.CostEstimate(
            flops=flops // 32, bytes_accessed=flops // 1024, transcendentals=0
        ),
    )(facts, *arrays, *weights)


def hidden_of(gate, up):
    return (jax.nn.silu(gate.astype(jnp.float32)) * up.astype(jnp.float32)).astype(jnp.bfloat16)


def slots_of(row_adapter_index, adapter_storage_slot):
    names = jnp.arange(adapter_storage_slot.shape[0], dtype=jnp.int32)
    same = row_adapter_index == names[None, :]
    return jnp.sum(jnp.where(same, adapter_storage_slot[None, :], 0), axis=1)


def gathered(
    gate_activation,
    up_activation,
    down_base_weight,
    first_factor_table,
    second_factor_table,
    row_adapter_index,
    adapter_storage_slot,
):
    hidden = hidden_of(gate_activation, up_activation)
    row_count = hidden.shape[0]
    owners = lax.axis_size("wide")
    local_adapter = first_factor_table.shape[0]
    slots = local_adapter * owners
    rank_portion = second_factor_table.shape[1]
    home = lax.axis_index("wide")
    slot_all = slots_of(row_adapter_index, adapter_storage_slot)
    blocks = slot_all.reshape(owners, row_count)
    order = jnp.arange(row_count, dtype=jnp.int32)
    earlier = (blocks[:, :, None] == blocks[:, None, :]) & (order[None, :] < order[:, None])
    position = jnp.sum(earlier.astype(jnp.int32), axis=2)
    rows = lax.all_gather(hidden, "wide", axis=0, tiled=True)
    base = jnp.dot(rows, down_base_weight, preferred_element_type=jnp.float32)
    low = jnp.einsum("re,nqe->nrq", rows, first_factor_table, preferred_element_type=jnp.float32)
    low = low.reshape(local_adapter, owners, row_count, low.shape[2])
    own = home * local_adapter + jnp.arange(local_adapter, dtype=jnp.int32)
    kept = []
    for item in range(MOST):
        mask = (blocks[None] == own[:, None, None]) & (position == item)[None]
        kept.append(jnp.sum(jnp.where(mask[..., None], low, 0), axis=2))
    low = lax.psum_scatter(jnp.stack(kept, axis=2), INNER, scatter_dimension=3, tiled=True)
    low = lax.all_gather(low.astype(jnp.bfloat16), "wide", axis=0, tiled=True)
    spread = 0
    for item in range(MOST):
        mask = (blocks[None] == jnp.arange(slots, dtype=jnp.int32)[:, None, None]) & (position == item)
        spread += jnp.where(mask[..., None], low[:, :, item][:, :, None], 0)
    spread = spread.reshape(slots, owners * row_count, rank_portion)
    delta = jnp.einsum("srq,sqw->rw", spread, second_factor_table, preferred_element_type=jnp.float32)
    total = base + delta
    return lax.psum_scatter(total, INNER, scatter_dimension=0, tiled=True).astype(jnp.bfloat16)


def ring_order(nodes):
    return list(range(0, nodes, 2)) + list(range(nodes - 1, 0, -2))


def ringed(
    gate_activation,
    up_activation,
    down_base_weight,
    first_factor_table,
    second_factor_table,
    row_adapter_index,
    adapter_storage_slot,
):
    f32, bf16 = jnp.float32, jnp.bfloat16
    row_count, width_part = gate_activation.shape
    owners = lax.axis_size("wide")
    nodes = owners // 2
    far = nodes // 2
    steps = far - 1
    own_nodes = nodes // 2
    own_blocks = owners // 2
    group_rows = 2 * row_count
    order = ring_order(nodes)
    depth = width_part // 2
    width = down_base_weight.shape[1]
    rank = first_factor_table.shape[1]

    table = []
    for w in range(owners):
        p = order.index(w // 2)
        at = lambda shift: order[(p + shift) % nodes]
        ways = (-1, 1) if w % 2 == 0 else (1, -1)
        arrivals = [at(0)] + [at(s * k) for k in range(1, far) for s in ways] + [at(far)]
        row = [2 * node + (w % 2 ^ side) for node in arrivals for side in (0, 1)]
        for half in (0, 1):
            here = [(at(s) < own_nodes) == (half == 0) for s in range(far)]
            row += [int(h) for h in here]
            row += [at(s if h else s + far) % own_nodes for s, h in enumerate(here)]
        table.append(row)
    home = lax.axis_index("wide")
    part = lax.axis_index(INNER)
    side = jnp.bitwise_and(home, 1)

    def moved(shift, cross=0):
        return [
            (order[p] * 2 + c, order[(p + shift) % nodes] * 2 + (c ^ cross))
            for p in range(nodes)
            for c in (0, 1)
        ]

    def send(value, shift, cross=0):
        return lax.ppermute(value, "wide", moved(shift, cross))

    def turn(value, way):
        to_right, to_left = moved(way), moved(-way)
        pairs = [pair for pair in to_right if pair[0] % 2 == 0]
        pairs += [pair for pair in to_left if pair[0] % 2 == 1]
        return lax.ppermute(value, "wide", pairs)

    def half_of(value, which, axis):
        return lax.dynamic_slice_in_dim(value, which * depth, depth, axis)

    crossed = [(2 * w + m, 2 * (w ^ 1) + (1 - m)) for w in range(owners) for m in (0, 1)]

    def to_three(to_sib, to_mp, to_both):
        return (
            send(to_sib, 0, 1),
            lax.ppermute(to_mp, INNER, SWAP),
            lax.ppermute(to_both, ("wide",) + INNER, crossed),
        )

    give = hidden_of(half_of(gate_activation, 1 - side, 1), half_of(up_activation, 1 - side, 1))
    keep_side, give = lax.optimization_barrier((side, give))
    keep = hidden_of(half_of(gate_activation, keep_side, 1), half_of(up_activation, keep_side, 1))
    block = jnp.concatenate([keep, send(give, 0, 1)], axis=0)
    one_way, other_way = turn(block, 1), turn(block, -1)

    weight, first, second_factor_table, block = lax.optimization_barrier(
        (down_base_weight, first_factor_table[0], second_factor_table, block)
    )
    other_second = lax.ppermute(second_factor_table, INNER, SWAP)
    weights = (weight, send(weight, 0, 1))
    factors = jnp.concatenate(
        [half_of(first, side, 1), half_of(send(first, 0, 1), side, 1)], axis=0
    )
    home_late, part_late, row_adapter_index, other_second = lax.optimization_barrier(
        (home, part, row_adapter_index, other_second)
    )

    pieces = [block, one_way, other_way]
    for step in range(2, steps + 1):
        one_way, other_way = turn(one_way, 1), turn(other_way, -1)
        if step < steps:
            one_way, other_way = lax.optimization_barrier((one_way, other_way))
            pieces += [one_way, other_way]

    row = lax.dynamic_index_in_dim(
        jnp.asarray(np.array(table, np.int32)), home_late, 0, keepdims=False
    )
    edges = np.cumsum([0, 2 * nodes, far, far, far, far])
    arrived, *rest = [row[a:b] for a, b in zip(edges[:-1], edges[1:])]
    facts = jnp.concatenate(
        [side[None], part_late[None].astype(jnp.int32)]
        + [jnp.where(part_late == 0, a, b) for a, b in zip(rest[:2], rest[2:])]
    )
    slot_all = slots_of(row_adapter_index, adapter_storage_slot).reshape(owners, row_count)
    ranks = jnp.arange(row_count, dtype=jnp.int32)
    earlier = (slot_all[:, :, None] == slot_all[:, None, :]) & (ranks[None, :] < ranks[:, None])
    position = jnp.sum(earlier.astype(jnp.int32), axis=2)
    blocks = jnp.arange(owners, dtype=jnp.int32)

    items = jnp.arange(owners * MOST, dtype=jnp.int32)
    came = arrived[:, None] == blocks[None, :]
    slot_came = jnp.sum(jnp.where(came[:, :, None], slot_all[None], 0), axis=1).reshape(1, -1)
    place_came = jnp.sum(
        jnp.where(came[:, :, None], position[None] + MOST * blocks[None, :, None], 0), axis=1
    ).reshape(1, -1)
    chosen = jnp.concatenate(
        [
            ((place_came == items[:, None]) & (slot_came == slot)).astype(bf16)
            for slot in (home_late, jnp.bitwise_xor(home_late, 1))
        ],
        axis=0,
    )
    early_rows = len(pieces) * group_rows
    sides, places = jnp.arange(2, dtype=jnp.int32), jnp.arange(MOST, dtype=jnp.int32)
    far_wide = arrived[-2:]
    far_choice = (
        (sides[:, None, None, None, None, None] == sides[:, None, None])
        & (blocks[:, None, None, None, None] == far_wide[:, None])
        & (places[:, None, None, None] == places)
    )
    far_choice = far_choice.reshape(2 * owners * MOST, 4 * MOST).astype(bf16)
    choices = [
        chosen[:, :early_rows],
        jnp.concatenate([chosen[:, early_rows : early_rows + 2 * group_rows], far_choice], axis=1),
    ]

    own_is = jnp.bitwise_xor(home_late, sides)[:, None, None] == blocks[None, :, None]
    own_slot = jnp.sum(jnp.where(own_is, slot_all[None], 0), axis=1)
    own_position = jnp.sum(jnp.where(own_is, position[None], 0), axis=1)
    pick = (
        (sides[:, None, None, None] == sides[:, None])
        & (own_slot[:, None, None, :] == far_wide[:, None, None, None, None])
        & (own_position[:, None, None, :] == places[:, None, None])
    )
    pick = pick.reshape(4 * MOST, group_rows).astype(bf16)
    picked = jnp.dot(pick, block, preferred_element_type=f32).astype(bf16)
    far_rows = send(picked, far)

    half = own_blocks * MOST
    here = own_blocks * row_count
    slot_here = lax.dynamic_slice_in_dim(slot_all, part_late * own_blocks, own_blocks).reshape(here, 1)
    position_here = lax.dynamic_slice_in_dim(position, part_late * own_blocks, own_blocks)
    block_here = jnp.arange(here, dtype=jnp.int32)[:, None] // row_count
    spot = (
        jnp.bitwise_xor(slot_here, home_late) * half
        + block_here * MOST
        + position_here.reshape(here, 1)
    )
    spots = (spot == jnp.arange(owners * half, dtype=jnp.int32)[None, :]).astype(bf16)
    piece = rank // 2
    column = jnp.arange(owners * rank, dtype=jnp.int32)[None, :]
    own_rank = jnp.bitwise_xor(part_late, column // (owners * piece)) * piece + column % piece
    mask = (slot_here == column // piece % owners).astype(bf16)
    copies = (jnp.arange(rank, dtype=jnp.int32)[:, None] == own_rank).astype(bf16)

    other_second, far_rows = lax.optimization_barrier((other_second, far_rows))
    second = jnp.concatenate(
        [values.reshape(owners * piece, width) for values in (second_factor_table, other_second)],
        axis=0,
    )

    compact_shape = ((2, owners * MOST, rank), f32)
    tile = tile_of(depth)

    def sums(rows, with_low=True):
        columns = [width, width] + [2 * rank] * with_low
        return [pltpu.VMEM((rows, size), f32) for size in columns]

    def flops(rows, columns):
        return 2 * rows * depth * columns

    facts, spots, mask, copies, choices, second = lax.optimization_barrier(
        (facts, spots, mask, copies, choices, second)
    )
    *early, held = kernel_call(
        functools.partial(early_kernel, len(pieces)),
        facts,
        (*pieces, factors, choices[0]),
        [((1, group_rows, width), f32)] * 2
        + [((len(pieces) - 1, group_rows, width), f32)] * 2
        + [compact_shape, ((2, depth // tile, tile, width), bf16)],
        sums(early_rows),
        flops(early_rows, 2 * (width + rank)),
        weights,
        32,
    )
    one_way, other_way, early, held = lax.optimization_barrier((one_way, other_way, early, held))

    last = turn(one_way, 1)

    kept, sent = kernel_call(
        low_kernel,
        facts,
        (one_way, other_way, far_rows, factors, choices[1], early[4]),
        [((2, half, rank), f32)] * 2,
        [pltpu.VMEM((rows, 2 * rank), f32) for rows in (2 * group_rows, 4 * MOST)],
        flops(2 * group_rows, 2 * rank),
    )
    kept, sent, one_way, other_way = lax.optimization_barrier((kept, sent, one_way, other_way))

    got = to_three(kept, sent, sent)

    own_more, sib_more = kernel_call(
        middle_kernel,
        facts,
        (one_way, other_way, held, early[2], early[3]),
        [((2, far - 1, group_rows, width), f32)] * 2,
        sums(2 * group_rows, False),
        flops(2 * group_rows, 2 * width),
    )
    got_sib = send(sib_more, 0, 1)

    def last_rows(which, rows, base, cost):
        shape = (1, group_rows, width)
        return kernel_call(
            functools.partial(last_kernel, which),
            facts,
            (rows, held, base),
            [(shape, f32), (shape, bf16)],
            [pltpu.VMEM((group_rows, width), f32)],
            cost * flops(group_rows, width),
        )

    to_sib, to_both = last_rows(1, last, early[1], 1024)
    got, got_sib, to_sib, to_both = lax.optimization_barrier((got, got_sib, to_sib, to_both))
    kept_more, out_more = [a + b for a, b in zip(own_more, got_sib)]
    low = (kept + got[1] + (got[0] + got[2])[::-1]).astype(bf16)
    low, last = lax.optimization_barrier((low, last))

    def from_node(value, gap):
        return lax.ppermute(value, "wide", [(w, w ^ (2 * gap)) for w in range(owners)])

    gap = 1
    while gap < nodes:
        reach = min(4, nodes // gap)
        parts = [from_node(low, gap * k) for k in range(1, reach)]
        low = jnp.concatenate([low] + parts, axis=0)
        gap *= reach
    got_more = lax.ppermute(out_more.astype(bf16), INNER, SWAP)
    kept_one, to_mp = last_rows(0, last, early[0], 1)
    got_one = to_three(to_sib, to_mp, to_both)

    shape = (own_nodes, group_rows, width)
    delta = kernel_call(
        delta_kernel,
        facts,
        (low.reshape(owners * half, rank), spots, mask, copies, second),
        [(shape, f32)],
        [],
        2 * here * owners * rank * width,
    )[0]
    out = kernel_call(
        functools.partial(final_kernel, far),
        facts,
        (delta, kept_more, got_more, kept_one, *got_one),
        [(shape, bf16)],
        [],
        here * width,
    )[0]
    return out.reshape(-1, width)


def solution(mesh):
    shape = dict(mesh.shape)
    wide, inner = shape["wide"], shape["mp"] * shape["sub"]
    paired = shape["sub"] == 1 and inner == 2 and wide % 8 == 0 and wide & (wide - 1) == 0
    if paired:
        nodes = wide // 2
        order = ring_order(nodes)
        paired = all(
            (order[p] < nodes // 2) != (order[(p + nodes // 2) % nodes] < nodes // 2)
            for p in range(nodes)
        )
    return jax.shard_map(
        ringed if paired else gathered,
        mesh=mesh,
        in_specs=(
            P(("groups", "wide"), ("mp", "sub")),
            P(("groups", "wide"), ("mp", "sub")),
            P(("mp", "sub"), "wide"),
            P("wide", None, ("mp", "sub")),
            P(None, ("mp", "sub"), "wide"),
            P("groups", None),
            P(),
        ),
        out_specs=P(("groups", "mp", "sub"), "wide"),
        check_vma=False,
    )
```

```python
import functools

import jax
import jax.numpy as jnp
import numpy as np
from jax import lax
from jax.experimental import pallas as pl
from jax.experimental.pallas import tpu as pltpu
from jax.sharding import PartitionSpec as P

MOST = 2
INNER = ("mp", "sub")
SWAP = [(0, 1), (1, 0)]


def tile_of(depth, most=1024):
    parts = 1
    while depth % parts or (depth // parts) % 128 or depth // parts > most:
        parts += 1
    return depth // parts


def started(sources, places, ready):
    copies = []
    for index, (source, place) in enumerate(zip(sources, places)):
        copies.append(pltpu.make_async_copy(source, place, ready.at[index]))
        copies[-1].start()
    return copies


def weight_copies(lane, weights, held, ready):
    tiles, tile = held.shape[1:3]
    first = pl.multiple_of(lane * tiles * tile, 128)
    sources = [w.at[pl.ds(first + i * tile, tile)] for i in range(tiles) for w in weights]
    places = [held.at[which, i] for i in range(tiles) for which in (0, 1)]
    return started(sources, places, ready)


def weight_products(rows_of, held, sums, copies=None, first=0):
    tiles, tile = held.shape[1:3]
    for total in sums:
        total[...] = jnp.zeros_like(total)
    for index in range(tiles):
        rows = rows_of(slice(index * tile, (index + 1) * tile))
        for which, total in enumerate(sums):
            if copies:
                copies[2 * index + which].wait()
            total[...] += jnp.dot(rows, held[first + which, index], preferred_element_type=jnp.float32)


def factor_products(rows_of, table, low):
    depth = table.shape[1]
    tile = tile_of(depth)

    def product(here):
        return lax.dot_general(
            rows_of(here), table[:, here], (((1,), (1,)), ((), ())), preferred_element_type=jnp.float32
        )

    if low.shape[0] <= 128:
        total = jnp.zeros(low.shape, jnp.float32)
        for index in range(depth // tile):
            total += product(slice(index * tile, (index + 1) * tile))
        low[...] = total
        return
    low[...] = jnp.zeros_like(low)

    def step(index, carry):
        low[...] += product(pl.ds(pl.multiple_of(index * tile, 128), tile))
        return carry

    lax.fori_loop(0, depth // tile, step, 0)


def in_lanes(lane, total, index, height):
    first = total[2 * index * height : (2 * index + 1) * height]
    other = total[(2 * index + 1) * height : (2 * index + 2) * height]
    whole = jnp.concatenate([first, other], axis=0)
    turned = jnp.concatenate([other, first], axis=0)
    return jnp.where(lane == 0, whole, turned)


def compacted(choice, low):
    high = low.astype(jnp.bfloat16)
    rest = low - high.astype(jnp.float32)
    middle = rest.astype(jnp.bfloat16)
    tail = (rest - middle.astype(jnp.float32)).astype(jnp.bfloat16)
    picked = jnp.dot(
        choice,
        jnp.concatenate([high, middle, tail], axis=1),
        preferred_element_type=jnp.float32,
    )
    size = low.shape[1]
    total = picked[:, :size] + (picked[:, size : 2 * size] + picked[:, 2 * size :])
    count, rank = choice.shape[0] // 2, size // 2
    return total[:count, :rank], total[count:, rank:]


def early_kernel(count, facts, *refs):
    pieces, refs = refs[:count], refs[count:]
    (factors, choices), weights, refs = refs[:2], refs[2:4], refs[4:]
    owns, rests, (compact, held), refs = refs[:2], refs[2:4], refs[4:6], refs[6:]
    sums, (low, ready) = refs[:2], refs[2:]
    rows_of = lambda here: jnp.concatenate([piece[:, here] for piece in pieces], axis=0)
    in_flight = weight_copies(facts[0], weights, held, ready)
    factor_products(rows_of, factors, low)
    weight_products(rows_of, held, sums, in_flight)
    height = owns[0].shape[1] // 2
    for own, rest, total in zip(owns, rests, sums):
        own[0] = in_lanes(facts[0], total, 0, height)
        for index in range(1, count):
            rest[index - 1] = in_lanes(facts[0], total, index, height)
    compact[0], compact[1] = compacted(choices[...], low[...])


def share(flag, near, away, outs, pair):
    (near_own, near_sib), (away_own, away_sib) = near, away
    kept, to_sib, to_mp, to_both = outs
    kept[pair] = jnp.where(flag == 1, near_own, away_own)
    to_sib[pair] = jnp.where(flag == 1, near_sib, away_sib)
    to_mp[pair] = jnp.where(flag == 1, away_own, near_own).astype(to_mp.dtype)
    to_both[pair] = jnp.where(flag == 1, away_sib, near_sib).astype(to_both.dtype)


def middle_kernel(facts, piece, other, held, base, base_sib, own, sib, *sums):
    outs = own.at[0], sib.at[0], own.at[1], sib.at[1]
    rows_of = lambda here: jnp.concatenate([piece[:, here], other[:, here]], axis=0)
    weight_products(rows_of, held, sums)
    pairs, group = own.shape[1:3]
    fresh = [[in_lanes(facts[0], total, index, group // 2) for total in sums] for index in (0, 1)]
    lane = facts[0]
    ahead = [jnp.where(lane == 0, b, a) for a, b in zip(*fresh)]
    behind = [jnp.where(lane == 0, a, b) for a, b in zip(*fresh)]
    for pair in range(pairs):
        step, back = pair + 1, pairs - pair
        near, away = 2 * step - 1 - lane, 2 * back - 2 + lane
        near = ahead if step == pairs else (base[near], base_sib[near])
        away = behind if back == pairs else (base[away], base_sib[away])
        share(facts[2 + step], near, away, outs, pair)


def low_kernel(facts, piece, other, far_rows, factors, choices, compact_in, kept, sent, low, low_far):
    half = kept.shape[1]
    rows_of = lambda here: jnp.concatenate([piece[:, here], other[:, here]], axis=0)
    factor_products(rows_of, factors, low)
    factor_products(lambda here: far_rows[:, here], factors, low_far)
    both = jnp.concatenate([low[...], low_far[...]], axis=0)
    for which, fresh_low in enumerate(compacted(choices[...], both)):
        total = compact_in[which] + fresh_low
        kept[which] = jnp.where(facts[1] == 0, total[:half], total[half:])
        sent[which] = jnp.where(facts[1] == 0, total[half:], total[:half])


def last_kernel(which, facts, piece, held, base, mine, others, total):
    weight_products(lambda here: piece[:, here], held, [total], first=which)
    away = in_lanes(facts[0], total, 0, piece.shape[0] // 2)
    mine[0] = jnp.where(facts[2] == 1, base[0], away)
    others[0] = jnp.where(facts[2] == 1, away, base[0]).astype(others.dtype)


def delta_kernel(facts, low, spots, mask, copies, second, out):
    f32 = jnp.float32
    own = jnp.dot(spots[...], low[...], preferred_element_type=f32).astype(jnp.bfloat16)
    spread = jnp.dot(own, copies[...], preferred_element_type=f32).astype(jnp.bfloat16) * mask[...]
    out[...] = jnp.dot(spread, second[...], preferred_element_type=f32).reshape(out.shape)


def final_kernel(pairs, facts, delta, kept_more, got_more, kept, got_sib, got_mp, got_both, out):
    f32 = jnp.float32
    for pair in range(pairs):
        if pair:
            value = kept_more[pair - 1] + got_more[pair - 1].astype(f32)
        else:
            value = kept[0] + got_sib[0] + (got_mp[0].astype(f32) + got_both[0].astype(f32))
        place = facts[2 + pairs + pair]
        out[place] = (value + delta[place]).astype(out.dtype)


def kernel_call(kernel, facts, arrays, shapes, scratch, flops, weights=(), grant=12):
    in_vmem = pl.BlockSpec(memory_space=pltpu.VMEM)
    if weights:
        scratch = scratch + [pltpu.SemaphoreType.DMA((len(weights) * shapes[-1][0][1],))]
    return pl.pallas_call(
        kernel,
        in_specs=[pl.BlockSpec(memory_space=pltpu.SMEM)]
        + [in_vmem] * len(arrays)
        + [pl.BlockSpec(memory_space=pl.ANY)] * len(weights),
        out_specs=[in_vmem] * len(shapes),
        out_shape=[jax.ShapeDtypeStruct(shape, kind) for shape, kind in shapes],
        scratch_shapes=scratch,
        compiler_params=pltpu.CompilerParams(vmem_limit_bytes=grant * 2**20),
        cost_estimate=pl.CostEstimate(
            flops=flops // 32, bytes_accessed=flops // 1024, transcendentals=0
        ),
    )(facts, *arrays, *weights)


def hidden_of(gate, up):
    return (jax.nn.silu(gate.astype(jnp.float32)) * up.astype(jnp.float32)).astype(jnp.bfloat16)


def slots_of(row_adapter_index, adapter_storage_slot):
    names = jnp.arange(adapter_storage_slot.shape[0], dtype=jnp.int32)
    same = row_adapter_index == names[None, :]
    return jnp.sum(jnp.where(same, adapter_storage_slot[None, :], 0), axis=1)


def gathered(
    gate_activation,
    up_activation,
    down_base_weight,
    first_factor_table,
    second_factor_table,
    row_adapter_index,
    adapter_storage_slot,
):
    hidden = hidden_of(gate_activation, up_activation)
    row_count = hidden.shape[0]
    owners = lax.axis_size("wide")
    local_adapter = first_factor_table.shape[0]
    slots = local_adapter * owners
    rank_portion = second_factor_table.shape[1]
    home = lax.axis_index("wide")
    slot_all = slots_of(row_adapter_index, adapter_storage_slot)
    blocks = slot_all.reshape(owners, row_count)
    order = jnp.arange(row_count, dtype=jnp.int32)
    earlier = (blocks[:, :, None] == blocks[:, None, :]) & (order[None, :] < order[:, None])
    position = jnp.sum(earlier.astype(jnp.int32), axis=2)
    rows = lax.all_gather(hidden, "wide", axis=0, tiled=True)
    base = jnp.dot(rows, down_base_weight, preferred_element_type=jnp.float32)
    low = jnp.einsum("re,nqe->nrq", rows, first_factor_table, preferred_element_type=jnp.float32)
    low = low.reshape(local_adapter, owners, row_count, low.shape[2])
    own = home * local_adapter + jnp.arange(local_adapter, dtype=jnp.int32)
    kept = []
    for item in range(MOST):
        mask = (blocks[None] == own[:, None, None]) & (position == item)[None]
        kept.append(jnp.sum(jnp.where(mask[..., None], low, 0), axis=2))
    low = lax.psum_scatter(jnp.stack(kept, axis=2), INNER, scatter_dimension=3, tiled=True)
    low = lax.all_gather(low.astype(jnp.bfloat16), "wide", axis=0, tiled=True)
    spread = 0
    for item in range(MOST):
        mask = (blocks[None] == jnp.arange(slots, dtype=jnp.int32)[:, None, None]) & (position == item)
        spread += jnp.where(mask[..., None], low[:, :, item][:, :, None], 0)
    spread = spread.reshape(slots, owners * row_count, rank_portion)
    delta = jnp.einsum("srq,sqw->rw", spread, second_factor_table, preferred_element_type=jnp.float32)
    total = base + delta
    return lax.psum_scatter(total, INNER, scatter_dimension=0, tiled=True).astype(jnp.bfloat16)


def ring_order(nodes):
    return list(range(0, nodes, 2)) + list(range(nodes - 1, 0, -2))


def ringed(
    gate_activation,
    up_activation,
    down_base_weight,
    first_factor_table,
    second_factor_table,
    row_adapter_index,
    adapter_storage_slot,
):
    f32, bf16 = jnp.float32, jnp.bfloat16
    row_count, width_part = gate_activation.shape
    owners = lax.axis_size("wide")
    nodes = owners // 2
    far = nodes // 2
    steps = far - 1
    own_nodes = nodes // 2
    own_blocks = owners // 2
    group_rows = 2 * row_count
    order = ring_order(nodes)
    depth = width_part // 2
    width = down_base_weight.shape[1]
    rank = first_factor_table.shape[1]

    table = []
    for w in range(owners):
        p = order.index(w // 2)
        at = lambda shift: order[(p + shift) % nodes]
        ways = (-1, 1) if w % 2 == 0 else (1, -1)
        arrivals = [at(0)] + [at(s * k) for k in range(1, far) for s in ways] + [at(far)]
        row = [2 * node + (w % 2 ^ side) for node in arrivals for side in (0, 1)]
        for half in (0, 1):
            here = [(at(s) < own_nodes) == (half == 0) for s in range(far)]
            row += [int(h) for h in here]
            row += [at(s if h else s + far) % own_nodes for s, h in enumerate(here)]
        table.append(row)
    home = lax.axis_index("wide")
    part = lax.axis_index(INNER)
    side = jnp.bitwise_and(home, 1)

    def moved(shift, cross=0):
        return [
            (order[p] * 2 + c, order[(p + shift) % nodes] * 2 + (c ^ cross))
            for p in range(nodes)
            for c in (0, 1)
        ]

    def send(value, shift, cross=0):
        return lax.ppermute(value, "wide", moved(shift, cross))

    def turn(value, way):
        to_right, to_left = moved(way), moved(-way)
        pairs = [pair for pair in to_right if pair[0] % 2 == 0]
        pairs += [pair for pair in to_left if pair[0] % 2 == 1]
        return lax.ppermute(value, "wide", pairs)

    def half_of(value, which, axis):
        return lax.dynamic_slice_in_dim(value, which * depth, depth, axis)

    crossed = [(2 * w + m, 2 * (w ^ 1) + (1 - m)) for w in range(owners) for m in (0, 1)]

    def to_three(to_sib, to_mp, to_both):
        return (
            send(to_sib, 0, 1),
            lax.ppermute(to_mp, INNER, SWAP),
            lax.ppermute(to_both, ("wide",) + INNER, crossed),
        )

    give = hidden_of(half_of(gate_activation, 1 - side, 1), half_of(up_activation, 1 - side, 1))
    keep_side, give = lax.optimization_barrier((side, give))
    keep = hidden_of(half_of(gate_activation, keep_side, 1), half_of(up_activation, keep_side, 1))
    block = jnp.concatenate([keep, send(give, 0, 1)], axis=0)
    one_way, other_way = turn(block, 1), turn(block, -1)

    weight, first, second_factor_table, block = lax.optimization_barrier(
        (down_base_weight, first_factor_table[0], second_factor_table, block)
    )
    other_second = lax.ppermute(second_factor_table, INNER, SWAP)
    weights = (weight, send(weight, 0, 1))
    factors = jnp.concatenate(
        [half_of(first, side, 1), half_of(send(first, 0, 1), side, 1)], axis=0
    )
    home_late, part_late, row_adapter_index, other_second = lax.optimization_barrier(
        (home, part, row_adapter_index, other_second)
    )

    pieces = [block, one_way, other_way]
    for step in range(2, steps + 1):
        one_way, other_way = turn(one_way, 1), turn(other_way, -1)
        if step < steps:
            one_way, other_way = lax.optimization_barrier((one_way, other_way))
            pieces += [one_way, other_way]

    row = lax.dynamic_index_in_dim(
        jnp.asarray(np.array(table, np.int32)), home_late, 0, keepdims=False
    )
    edges = np.cumsum([0, 2 * nodes, far, far, far, far])
    arrived, *rest = [row[a:b] for a, b in zip(edges[:-1], edges[1:])]
    facts = jnp.concatenate(
        [side[None], part_late[None].astype(jnp.int32)]
        + [jnp.where(part_late == 0, a, b) for a, b in zip(rest[:2], rest[2:])]
    )
    slot_all = slots_of(row_adapter_index, adapter_storage_slot).reshape(owners, row_count)
    ranks = jnp.arange(row_count, dtype=jnp.int32)
    earlier = (slot_all[:, :, None] == slot_all[:, None, :]) & (ranks[None, :] < ranks[:, None])
    position = jnp.sum(earlier.astype(jnp.int32), axis=2)
    blocks = jnp.arange(owners, dtype=jnp.int32)

    items = jnp.arange(owners * MOST, dtype=jnp.int32)
    came = arrived[:, None] == blocks[None, :]
    slot_came = jnp.sum(jnp.where(came[:, :, None], slot_all[None], 0), axis=1).reshape(1, -1)
    place_came = jnp.sum(
        jnp.where(came[:, :, None], position[None] + MOST * blocks[None, :, None], 0), axis=1
    ).reshape(1, -1)
    chosen = jnp.concatenate(
        [
            ((place_came == items[:, None]) & (slot_came == slot)).astype(bf16)
            for slot in (home_late, jnp.bitwise_xor(home_late, 1))
        ],
        axis=0,
    )
    early_rows = len(pieces) * group_rows
    sides, places = jnp.arange(2, dtype=jnp.int32), jnp.arange(MOST, dtype=jnp.int32)
    far_wide = arrived[-2:]
    far_choice = (
        (sides[:, None, None, None, None, None] == sides[:, None, None])
        & (blocks[:, None, None, None, None] == far_wide[:, None])
        & (places[:, None, None, None] == places)
    )
    far_choice = far_choice.reshape(2 * owners * MOST, 4 * MOST).astype(bf16)
    choices = [
        chosen[:, :early_rows],
        jnp.concatenate([chosen[:, early_rows : early_rows + 2 * group_rows], far_choice], axis=1),
    ]

    own_is = jnp.bitwise_xor(home_late, sides)[:, None, None] == blocks[None, :, None]
    own_slot = jnp.sum(jnp.where(own_is, slot_all[None], 0), axis=1)
    own_position = jnp.sum(jnp.where(own_is, position[None], 0), axis=1)
    pick = (
        (sides[:, None, None, None] == sides[:, None])
        & (own_slot[:, None, None, :] == far_wide[:, None, None, None, None])
        & (own_position[:, None, None, :] == places[:, None, None])
    )
    pick = pick.reshape(4 * MOST, group_rows).astype(bf16)
    picked = jnp.dot(pick, block, preferred_element_type=f32).astype(bf16)
    far_rows = send(picked, far)

    half = own_blocks * MOST
    here = own_blocks * row_count
    slot_here = lax.dynamic_slice_in_dim(slot_all, part_late * own_blocks, own_blocks).reshape(here, 1)
    position_here = lax.dynamic_slice_in_dim(position, part_late * own_blocks, own_blocks)
    block_here = jnp.arange(here, dtype=jnp.int32)[:, None] // row_count
    spot = (
        jnp.bitwise_xor(slot_here, home_late) * half
        + block_here * MOST
        + position_here.reshape(here, 1)
    )
    spots = (spot == jnp.arange(owners * half, dtype=jnp.int32)[None, :]).astype(bf16)
    piece = rank // 2
    column = jnp.arange(owners * rank, dtype=jnp.int32)[None, :]
    own_rank = jnp.bitwise_xor(part_late, column // (owners * piece)) * piece + column % piece
    mask = (slot_here == column // piece % owners).astype(bf16)
    copies = (jnp.arange(rank, dtype=jnp.int32)[:, None] == own_rank).astype(bf16)

    other_second, far_rows = lax.optimization_barrier((other_second, far_rows))
    second = jnp.concatenate(
        [values.reshape(owners * piece, width) for values in (second_factor_table, other_second)],
        axis=0,
    )

    compact_shape = ((2, owners * MOST, rank), f32)
    tile = tile_of(depth)

    def sums(rows, with_low=True):
        columns = [width, width] + [2 * rank] * with_low
        return [pltpu.VMEM((rows, size), f32) for size in columns]

    def flops(rows, columns):
        return 2 * rows * depth * columns

    facts, spots, mask, copies, choices, second = lax.optimization_barrier(
        (facts, spots, mask, copies, choices, second)
    )
    *early, held = kernel_call(
        functools.partial(early_kernel, len(pieces)),
        facts,
        (*pieces, factors, choices[0]),
        [((1, group_rows, width), f32)] * 2
        + [((len(pieces) - 1, group_rows, width), f32)] * 2
        + [compact_shape, ((2, depth // tile, tile, width), bf16)],
        sums(early_rows),
        flops(early_rows, 2 * (width + rank)),
        weights,
        32,
    )
    one_way, other_way, early, held = lax.optimization_barrier((one_way, other_way, early, held))

    last = turn(one_way, 1)

    kept, sent = kernel_call(
        low_kernel,
        facts,
        (one_way, other_way, far_rows, factors, choices[1], early[4]),
        [((2, half, rank), f32)] * 2,
        [pltpu.VMEM((rows, 2 * rank), f32) for rows in (2 * group_rows, 4 * MOST)],
        flops(2 * group_rows, 2 * rank),
    )
    kept, sent, one_way, other_way = lax.optimization_barrier((kept, sent, one_way, other_way))

    got = to_three(kept, sent, sent)

    own_more, sib_more = kernel_call(
        middle_kernel,
        facts,
        (one_way, other_way, held, early[2], early[3]),
        [((2, far - 1, group_rows, width), f32)] * 2,
        sums(2 * group_rows, False),
        flops(2 * group_rows, 2 * width),
    )
    got_sib = send(sib_more, 0, 1)

    def last_rows(which, rows, base, cost):
        shape = (1, group_rows, width)
        return kernel_call(
            functools.partial(last_kernel, which),
            facts,
            (rows, held, base),
            [(shape, f32), (shape, bf16)],
            [pltpu.VMEM((group_rows, width), f32)],
            cost * flops(group_rows, width),
        )

    to_sib, to_both = last_rows(1, last, early[1], 1024)
    got, got_sib, to_sib, to_both = lax.optimization_barrier((got, got_sib, to_sib, to_both))
    kept_more, out_more = [a + b for a, b in zip(own_more, got_sib)]
    low = (kept + got[1] + (got[0] + got[2])[::-1]).astype(bf16)
    low, last = lax.optimization_barrier((low, last))

    def from_node(value, gap):
        return lax.ppermute(value, "wide", [(w, w ^ (2 * gap)) for w in range(owners)])

    def gather(value, gap, reach):
        parts = [from_node(value, gap * k) for k in range(1, reach)]
        return jnp.concatenate([value] + parts, axis=0)

    reach = min(4, nodes)
    low, to_sib = lax.optimization_barrier((gather(low, 1, reach), to_sib))
    while reach < nodes:
        low = gather(low, reach, 2)
        reach *= 2
    got_more = lax.ppermute(out_more.astype(bf16), INNER, SWAP)
    kept_one, to_mp = last_rows(0, last, early[0], 1)
    got_one = to_three(to_sib, to_mp, to_both)

    shape = (own_nodes, group_rows, width)
    delta = kernel_call(
        delta_kernel,
        facts,
        (low.reshape(owners * half, rank), spots, mask, copies, second),
        [(shape, f32)],
        [],
        2 * here * owners * rank * width,
    )[0]
    out = kernel_call(
        functools.partial(final_kernel, far),
        facts,
        (delta, kept_more, got_more, kept_one, *got_one),
        [(shape, bf16)],
        [],
        here * width,
    )[0]
    return out.reshape(-1, width)


def solution(mesh):
    shape = dict(mesh.shape)
    wide, inner = shape["wide"], shape["mp"] * shape["sub"]
    paired = shape["sub"] == 1 and inner == 2 and wide % 8 == 0 and wide & (wide - 1) == 0
    if paired:
        nodes = wide // 2
        order = ring_order(nodes)
        paired = all(
            (order[p] < nodes // 2) != (order[(p + nodes // 2) % nodes] < nodes // 2)
            for p in range(nodes)
        )
    return jax.shard_map(
        ringed if paired else gathered,
        mesh=mesh,
        in_specs=(
            P(("groups", "wide"), ("mp", "sub")),
            P(("groups", "wide"), ("mp", "sub")),
            P(("mp", "sub"), "wide"),
            P("wide", None, ("mp", "sub")),
            P(None, ("mp", "sub"), "wide"),
            P("groups", None),
            P(),
        ),
        out_specs=P(("groups", "mp", "sub"), "wide"),
        check_vma=False,
    )
```

```python
import functools

import jax
import jax.numpy as jnp
import numpy as np
from jax import lax
from jax.experimental import pallas as pl
from jax.experimental.pallas import tpu as pltpu
from jax.sharding import PartitionSpec as P

MOST = 2
INNER = ("mp", "sub")
SWAP = [(0, 1), (1, 0)]


def tile_of(depth, most=1024):
    parts = 1
    while depth % parts or (depth // parts) % 128 or depth // parts > most:
        parts += 1
    return depth // parts


def started(sources, places, ready):
    copies = []
    for index, (source, place) in enumerate(zip(sources, places)):
        copies.append(pltpu.make_async_copy(source, place, ready.at[index]))
        copies[-1].start()
    return copies


def weight_copies(lane, weights, held, ready):
    tiles, tile = held.shape[1:3]
    first = pl.multiple_of(lane * tiles * tile, 128)
    sources = [w.at[pl.ds(first + i * tile, tile)] for i in range(tiles) for w in weights]
    places = [held.at[which, i] for i in range(tiles) for which in (0, 1)]
    return started(sources, places, ready)


def weight_products(rows_of, held, sums, copies=None, first=0):
    tiles, tile = held.shape[1:3]
    for total in sums:
        total[...] = jnp.zeros_like(total)
    for index in range(tiles):
        rows = rows_of(slice(index * tile, (index + 1) * tile))
        for which, total in enumerate(sums):
            if copies:
                copies[2 * index + which].wait()
            total[...] += jnp.dot(rows, held[first + which, index], preferred_element_type=jnp.float32)


def factor_products(rows_of, table, low):
    depth = table.shape[1]
    tile = tile_of(depth)

    def product(here):
        return lax.dot_general(
            rows_of(here), table[:, here], (((1,), (1,)), ((), ())), preferred_element_type=jnp.float32
        )

    if low.shape[0] <= 128:
        total = jnp.zeros(low.shape, jnp.float32)
        for index in range(depth // tile):
            total += product(slice(index * tile, (index + 1) * tile))
        low[...] = total
        return
    low[...] = jnp.zeros_like(low)

    def step(index, carry):
        low[...] += product(pl.ds(pl.multiple_of(index * tile, 128), tile))
        return carry

    lax.fori_loop(0, depth // tile, step, 0)


def in_lanes(lane, total, index, height):
    first = total[2 * index * height : (2 * index + 1) * height]
    other = total[(2 * index + 1) * height : (2 * index + 2) * height]
    whole = jnp.concatenate([first, other], axis=0)
    turned = jnp.concatenate([other, first], axis=0)
    return jnp.where(lane == 0, whole, turned)


def compacted(choice, low):
    high = low.astype(jnp.bfloat16)
    rest = low - high.astype(jnp.float32)
    middle = rest.astype(jnp.bfloat16)
    tail = (rest - middle.astype(jnp.float32)).astype(jnp.bfloat16)
    picked = jnp.dot(
        choice,
        jnp.concatenate([high, middle, tail], axis=1),
        preferred_element_type=jnp.float32,
    )
    size = low.shape[1]
    total = picked[:, :size] + (picked[:, size : 2 * size] + picked[:, 2 * size :])
    count, rank = choice.shape[0] // 2, size // 2
    return total[:count, :rank], total[count:, rank:]


def early_kernel(count, facts, *refs):
    pieces, refs = refs[:count], refs[count:]
    (factors, choices), weights, refs = refs[:2], refs[2:4], refs[4:]
    owns, rests, (compact, held), refs = refs[:2], refs[2:4], refs[4:6], refs[6:]
    sums, (low, ready) = refs[:2], refs[2:]
    rows_of = lambda here: jnp.concatenate([piece[:, here] for piece in pieces], axis=0)
    in_flight = weight_copies(facts[0], weights, held, ready)
    factor_products(rows_of, factors, low)
    weight_products(rows_of, held, sums, in_flight)
    height = owns[0].shape[1] // 2
    for own, rest, total in zip(owns, rests, sums):
        own[0] = in_lanes(facts[0], total, 0, height)
        for index in range(1, count):
            rest[index - 1] = in_lanes(facts[0], total, index, height)
    compact[0], compact[1] = compacted(choices[...], low[...])


def share(flag, near, away, outs, pair):
    (near_own, near_sib), (away_own, away_sib) = near, away
    kept, to_sib, to_mp, to_both = outs
    kept[pair] = jnp.where(flag == 1, near_own, away_own)
    to_sib[pair] = jnp.where(flag == 1, near_sib, away_sib)
    to_mp[pair] = jnp.where(flag == 1, away_own, near_own).astype(to_mp.dtype)
    to_both[pair] = jnp.where(flag == 1, away_sib, near_sib).astype(to_both.dtype)


def middle_kernel(facts, piece, other, held, base, base_sib, own, sib, *sums):
    outs = own.at[0], sib.at[0], own.at[1], sib.at[1]
    rows_of = lambda here: jnp.concatenate([piece[:, here], other[:, here]], axis=0)
    weight_products(rows_of, held, sums)
    pairs, group = own.shape[1:3]
    fresh = [[in_lanes(facts[0], total, index, group // 2) for total in sums] for index in (0, 1)]
    lane = facts[0]
    ahead = [jnp.where(lane == 0, b, a) for a, b in zip(*fresh)]
    behind = [jnp.where(lane == 0, a, b) for a, b in zip(*fresh)]
    for pair in range(pairs):
        step, back = pair + 1, pairs - pair
        near, away = 2 * step - 1 - lane, 2 * back - 2 + lane
        near = ahead if step == pairs else (base[near], base_sib[near])
        away = behind if back == pairs else (base[away], base_sib[away])
        share(facts[2 + step], near, away, outs, pair)


def low_kernel(facts, piece, other, far_rows, factors, choices, compact_in, kept, sent, low, low_far):
    half = kept.shape[1]
    rows_of = lambda here: jnp.concatenate([piece[:, here], other[:, here]], axis=0)
    factor_products(rows_of, factors, low)
    factor_products(lambda here: far_rows[:, here], factors, low_far)
    both = jnp.concatenate([low[...], low_far[...]], axis=0)
    for which, fresh_low in enumerate(compacted(choices[...], both)):
        total = compact_in[which] + fresh_low
        kept[which] = jnp.where(facts[1] == 0, total[:half], total[half:])
        sent[which] = jnp.where(facts[1] == 0, total[half:], total[:half])


def last_kernel(which, facts, piece, held, base, mine, others, total):
    weight_products(lambda here: piece[:, here], held, [total], first=which)
    away = in_lanes(facts[0], total, 0, piece.shape[0] // 2)
    mine[0] = jnp.where(facts[2] == 1, base[0], away)
    others[0] = jnp.where(facts[2] == 1, away, base[0]).astype(others.dtype)


def delta_kernel(facts, low, spots, mask, copies, second, out):
    f32 = jnp.float32
    own = jnp.dot(spots[...], low[...], preferred_element_type=f32).astype(jnp.bfloat16)
    spread = jnp.dot(own, copies[...], preferred_element_type=f32).astype(jnp.bfloat16) * mask[...]
    out[...] = jnp.dot(spread, second[...], preferred_element_type=f32).reshape(out.shape)


def final_kernel(pairs, facts, delta, kept_more, got_more, kept, got_sib, got_mp, got_both, out):
    f32 = jnp.float32
    for pair in range(pairs):
        if pair:
            value = kept_more[pair - 1] + got_more[pair - 1].astype(f32)
        else:
            value = kept[0] + got_sib[0] + (got_mp[0].astype(f32) + got_both[0].astype(f32))
        place = facts[2 + pairs + pair]
        out[place] = (value + delta[place]).astype(out.dtype)


def kernel_call(kernel, facts, arrays, shapes, scratch, flops, weights=(), grant=12):
    in_vmem = pl.BlockSpec(memory_space=pltpu.VMEM)
    if weights:
        scratch = scratch + [pltpu.SemaphoreType.DMA((len(weights) * shapes[-1][0][1],))]
    return pl.pallas_call(
        kernel,
        in_specs=[pl.BlockSpec(memory_space=pltpu.SMEM)]
        + [in_vmem] * len(arrays)
        + [pl.BlockSpec(memory_space=pl.ANY)] * len(weights),
        out_specs=[in_vmem] * len(shapes),
        out_shape=[jax.ShapeDtypeStruct(shape, kind) for shape, kind in shapes],
        scratch_shapes=scratch,
        compiler_params=pltpu.CompilerParams(vmem_limit_bytes=grant * 2**20),
        cost_estimate=pl.CostEstimate(
            flops=flops // 32, bytes_accessed=flops // 1024, transcendentals=0
        ),
    )(facts, *arrays, *weights)


def hidden_of(gate, up):
    return (jax.nn.silu(gate.astype(jnp.float32)) * up.astype(jnp.float32)).astype(jnp.bfloat16)


def slots_of(row_adapter_index, adapter_storage_slot):
    names = jnp.arange(adapter_storage_slot.shape[0], dtype=jnp.int32)
    same = row_adapter_index == names[None, :]
    return jnp.sum(jnp.where(same, adapter_storage_slot[None, :], 0), axis=1)


def gathered(
    gate_activation,
    up_activation,
    down_base_weight,
    first_factor_table,
    second_factor_table,
    row_adapter_index,
    adapter_storage_slot,
):
    hidden = hidden_of(gate_activation, up_activation)
    row_count = hidden.shape[0]
    owners = lax.axis_size("wide")
    local_adapter = first_factor_table.shape[0]
    slots = local_adapter * owners
    rank_portion = second_factor_table.shape[1]
    home = lax.axis_index("wide")
    slot_all = slots_of(row_adapter_index, adapter_storage_slot)
    blocks = slot_all.reshape(owners, row_count)
    order = jnp.arange(row_count, dtype=jnp.int32)
    earlier = (blocks[:, :, None] == blocks[:, None, :]) & (order[None, :] < order[:, None])
    position = jnp.sum(earlier.astype(jnp.int32), axis=2)
    rows = lax.all_gather(hidden, "wide", axis=0, tiled=True)
    base = jnp.dot(rows, down_base_weight, preferred_element_type=jnp.float32)
    low = jnp.einsum("re,nqe->nrq", rows, first_factor_table, preferred_element_type=jnp.float32)
    low = low.reshape(local_adapter, owners, row_count, low.shape[2])
    own = home * local_adapter + jnp.arange(local_adapter, dtype=jnp.int32)
    kept = []
    for item in range(MOST):
        mask = (blocks[None] == own[:, None, None]) & (position == item)[None]
        kept.append(jnp.sum(jnp.where(mask[..., None], low, 0), axis=2))
    low = lax.psum_scatter(jnp.stack(kept, axis=2), INNER, scatter_dimension=3, tiled=True)
    low = lax.all_gather(low.astype(jnp.bfloat16), "wide", axis=0, tiled=True)
    spread = 0
    for item in range(MOST):
        mask = (blocks[None] == jnp.arange(slots, dtype=jnp.int32)[:, None, None]) & (position == item)
        spread += jnp.where(mask[..., None], low[:, :, item][:, :, None], 0)
    spread = spread.reshape(slots, owners * row_count, rank_portion)
    delta = jnp.einsum("srq,sqw->rw", spread, second_factor_table, preferred_element_type=jnp.float32)
    total = base + delta
    return lax.psum_scatter(total, INNER, scatter_dimension=0, tiled=True).astype(jnp.bfloat16)


def ring_order(nodes):
    return list(range(0, nodes, 2)) + list(range(nodes - 1, 0, -2))


def ringed(
    gate_activation,
    up_activation,
    down_base_weight,
    first_factor_table,
    second_factor_table,
    row_adapter_index,
    adapter_storage_slot,
):
    f32, bf16 = jnp.float32, jnp.bfloat16
    row_count, width_part = gate_activation.shape
    owners = lax.axis_size("wide")
    nodes = owners // 2
    far = nodes // 2
    steps = far - 1
    own_nodes = nodes // 2
    own_blocks = owners // 2
    group_rows = 2 * row_count
    order = ring_order(nodes)
    depth = width_part // 2
    width = down_base_weight.shape[1]
    rank = first_factor_table.shape[1]

    table = []
    for w in range(owners):
        p = order.index(w // 2)
        at = lambda shift: order[(p + shift) % nodes]
        ways = (-1, 1) if w % 2 == 0 else (1, -1)
        arrivals = [at(0)] + [at(s * k) for k in range(1, far) for s in ways] + [at(far)]
        row = [2 * node + (w % 2 ^ side) for node in arrivals for side in (0, 1)]
        for half in (0, 1):
            here = [(at(s) < own_nodes) == (half == 0) for s in range(far)]
            row += [int(h) for h in here]
            row += [at(s if h else s + far) % own_nodes for s, h in enumerate(here)]
        table.append(row)
    home = lax.axis_index("wide")
    part = lax.axis_index(INNER)
    side = jnp.bitwise_and(home, 1)

    def moved(shift, cross=0):
        return [
            (order[p] * 2 + c, order[(p + shift) % nodes] * 2 + (c ^ cross))
            for p in range(nodes)
            for c in (0, 1)
        ]

    def send(value, shift, cross=0):
        return lax.ppermute(value, "wide", moved(shift, cross))

    def turn(value, way):
        to_right, to_left = moved(way), moved(-way)
        pairs = [pair for pair in to_right if pair[0] % 2 == 0]
        pairs += [pair for pair in to_left if pair[0] % 2 == 1]
        return lax.ppermute(value, "wide", pairs)

    def half_of(value, which, axis):
        return lax.dynamic_slice_in_dim(value, which * depth, depth, axis)

    crossed = [(2 * w + m, 2 * (w ^ 1) + (1 - m)) for w in range(owners) for m in (0, 1)]

    def to_three(to_sib, to_mp, to_both):
        return (
            send(to_sib, 0, 1),
            lax.ppermute(to_mp, INNER, SWAP),
            lax.ppermute(to_both, ("wide",) + INNER, crossed),
        )

    give = hidden_of(half_of(gate_activation, 1 - side, 1), half_of(up_activation, 1 - side, 1))
    keep_side, give = lax.optimization_barrier((side, give))
    keep = hidden_of(half_of(gate_activation, keep_side, 1), half_of(up_activation, keep_side, 1))
    block = jnp.concatenate([keep, send(give, 0, 1)], axis=0)
    one_way, other_way = turn(block, 1), turn(block, -1)

    weight, first, second_factor_table, block = lax.optimization_barrier(
        (down_base_weight, first_factor_table[0], second_factor_table, block)
    )
    other_second = lax.ppermute(second_factor_table, INNER, SWAP)
    weights = (weight, send(weight, 0, 1))
    factors = jnp.concatenate(
        [half_of(first, side, 1), half_of(send(first, 0, 1), side, 1)], axis=0
    )
    home_late, part_late, row_adapter_index, other_second = lax.optimization_barrier(
        (home, part, row_adapter_index, other_second)
    )

    pieces = [block, one_way, other_way]
    for step in range(2, steps + 1):
        one_way, other_way = turn(one_way, 1), turn(other_way, -1)
        if step < steps:
            one_way, other_way = lax.optimization_barrier((one_way, other_way))
            pieces += [one_way, other_way]

    row = lax.dynamic_index_in_dim(
        jnp.asarray(np.array(table, np.int32)), home_late, 0, keepdims=False
    )
    edges = np.cumsum([0, 2 * nodes, far, far, far, far])
    arrived, *rest = [row[a:b] for a, b in zip(edges[:-1], edges[1:])]
    facts = jnp.concatenate(
        [side[None], part_late[None].astype(jnp.int32)]
        + [jnp.where(part_late == 0, a, b) for a, b in zip(rest[:2], rest[2:])]
    )
    slot_all = slots_of(row_adapter_index, adapter_storage_slot).reshape(owners, row_count)
    ranks = jnp.arange(row_count, dtype=jnp.int32)
    earlier = (slot_all[:, :, None] == slot_all[:, None, :]) & (ranks[None, :] < ranks[:, None])
    position = jnp.sum(earlier.astype(jnp.int32), axis=2)
    blocks = jnp.arange(owners, dtype=jnp.int32)

    items = jnp.arange(owners * MOST, dtype=jnp.int32)
    came = arrived[:, None] == blocks[None, :]
    slot_came = jnp.sum(jnp.where(came[:, :, None], slot_all[None], 0), axis=1).reshape(1, -1)
    place_came = jnp.sum(
        jnp.where(came[:, :, None], position[None] + MOST * blocks[None, :, None], 0), axis=1
    ).reshape(1, -1)
    chosen = jnp.concatenate(
        [
            ((place_came == items[:, None]) & (slot_came == slot)).astype(bf16)
            for slot in (home_late, jnp.bitwise_xor(home_late, 1))
        ],
        axis=0,
    )
    early_rows = len(pieces) * group_rows
    sides, places = jnp.arange(2, dtype=jnp.int32), jnp.arange(MOST, dtype=jnp.int32)
    far_wide = arrived[-2:]
    far_choice = (
        (sides[:, None, None, None, None, None] == sides[:, None, None])
        & (blocks[:, None, None, None, None] == far_wide[:, None])
        & (places[:, None, None, None] == places)
    )
    far_choice = far_choice.reshape(2 * owners * MOST, 4 * MOST).astype(bf16)
    choices = [
        chosen[:, :early_rows],
        jnp.concatenate([chosen[:, early_rows : early_rows + 2 * group_rows], far_choice], axis=1),
    ]

    own_is = jnp.bitwise_xor(home_late, sides)[:, None, None] == blocks[None, :, None]
    own_slot = jnp.sum(jnp.where(own_is, slot_all[None], 0), axis=1)
    own_position = jnp.sum(jnp.where(own_is, position[None], 0), axis=1)
    pick = (
        (sides[:, None, None, None] == sides[:, None])
        & (own_slot[:, None, None, :] == far_wide[:, None, None, None, None])
        & (own_position[:, None, None, :] == places[:, None, None])
    )
    pick = pick.reshape(4 * MOST, group_rows).astype(bf16)
    picked = jnp.dot(pick, block, preferred_element_type=f32).astype(bf16)
    far_rows = send(picked, far)

    half = own_blocks * MOST
    here = own_blocks * row_count
    slot_here = lax.dynamic_slice_in_dim(slot_all, part_late * own_blocks, own_blocks).reshape(here, 1)
    position_here = lax.dynamic_slice_in_dim(position, part_late * own_blocks, own_blocks)
    block_here = jnp.arange(here, dtype=jnp.int32)[:, None] // row_count
    spot = (
        jnp.bitwise_xor(slot_here, home_late) * half
        + block_here * MOST
        + position_here.reshape(here, 1)
    )
    spots = (spot == jnp.arange(owners * half, dtype=jnp.int32)[None, :]).astype(bf16)
    piece = rank // 2
    column = jnp.arange(owners * rank, dtype=jnp.int32)[None, :]
    own_rank = jnp.bitwise_xor(part_late, column // (owners * piece)) * piece + column % piece
    mask = (slot_here == column // piece % owners).astype(bf16)
    copies = (jnp.arange(rank, dtype=jnp.int32)[:, None] == own_rank).astype(bf16)

    other_second, far_rows = lax.optimization_barrier((other_second, far_rows))
    second = jnp.concatenate(
        [values.reshape(owners * piece, width) for values in (second_factor_table, other_second)],
        axis=0,
    )

    compact_shape = ((2, owners * MOST, rank), f32)
    tile = tile_of(depth)

    def sums(rows, with_low=True):
        columns = [width, width] + [2 * rank] * with_low
        return [pltpu.VMEM((rows, size), f32) for size in columns]

    def flops(rows, columns):
        return 2 * rows * depth * columns

    facts, spots, mask, copies, choices, second = lax.optimization_barrier(
        (facts, spots, mask, copies, choices, second)
    )
    *early, held = kernel_call(
        functools.partial(early_kernel, len(pieces)),
        facts,
        (*pieces, factors, choices[0]),
        [((1, group_rows, width), f32)] * 2
        + [((len(pieces) - 1, group_rows, width), f32)] * 2
        + [compact_shape, ((2, depth // tile, tile, width), bf16)],
        sums(early_rows),
        flops(early_rows, 2 * (width + rank)),
        weights,
        32,
    )
    one_way, other_way, early, held = lax.optimization_barrier((one_way, other_way, early, held))

    last = turn(one_way, 1)

    kept, sent = kernel_call(
        low_kernel,
        facts,
        (one_way, other_way, far_rows, factors, choices[1], early[4]),
        [((2, half, rank), f32)] * 2,
        [pltpu.VMEM((rows, 2 * rank), f32) for rows in (2 * group_rows, 4 * MOST)],
        flops(2 * group_rows, 2 * rank),
    )
    kept, sent, one_way, other_way = lax.optimization_barrier((kept, sent, one_way, other_way))

    got = to_three(kept, sent, sent)

    own_more, sib_more = kernel_call(
        middle_kernel,
        facts,
        (one_way, other_way, held, early[2], early[3]),
        [((2, far - 1, group_rows, width), f32)] * 2,
        sums(2 * group_rows, False),
        flops(2 * group_rows, 2 * width),
    )
    got_sib = send(sib_more, 0, 1)

    def last_rows(which, rows, base, cost):
        shape = (1, group_rows, width)
        return kernel_call(
            functools.partial(last_kernel, which),
            facts,
            (rows, held, base),
            [(shape, f32), (shape, bf16)],
            [pltpu.VMEM((group_rows, width), f32)],
            cost * flops(group_rows, width),
        )

    to_sib, to_both = last_rows(1, last, early[1], 1024)
    got, got_sib, to_sib, to_both = lax.optimization_barrier((got, got_sib, to_sib, to_both))
    kept_more, out_more = [a + b for a, b in zip(own_more, got_sib)]
    low = (kept + got[1] + (got[0] + got[2])[::-1]).astype(bf16)
    low, last = lax.optimization_barrier((low, last))

    def from_node(value, gap):
        return lax.ppermute(value, "wide", [(w, w ^ (2 * gap)) for w in range(owners)])

    def gather(value, gap, reach):
        parts = [from_node(value, gap * k) for k in range(1, reach)]
        return jnp.concatenate([value] + parts, axis=0)

    reach = min(4, nodes)
    kept_one, to_mp = last_rows(0, last, early[0], 1)
    low, to_sib, to_mp = lax.optimization_barrier((gather(low, 1, reach), to_sib, to_mp))
    while reach < nodes:
        low = gather(low, reach, 2)
        reach *= 2
    got_more = lax.ppermute(out_more.astype(bf16), INNER, SWAP)
    got_one = to_three(to_sib, to_mp, to_both)

    shape = (own_nodes, group_rows, width)
    delta = kernel_call(
        delta_kernel,
        facts,
        (low.reshape(owners * half, rank), spots, mask, copies, second),
        [(shape, f32)],
        [],
        2 * here * owners * rank * width,
    )[0]
    out = kernel_call(
        functools.partial(final_kernel, far),
        facts,
        (delta, kept_more, got_more, kept_one, *got_one),
        [(shape, bf16)],
        [],
        here * width,
    )[0]
    return out.reshape(-1, width)


def solution(mesh):
    shape = dict(mesh.shape)
    wide, inner = shape["wide"], shape["mp"] * shape["sub"]
    paired = shape["sub"] == 1 and inner == 2 and wide % 8 == 0 and wide & (wide - 1) == 0
    if paired:
        nodes = wide // 2
        order = ring_order(nodes)
        paired = all(
            (order[p] < nodes // 2) != (order[(p + nodes // 2) % nodes] < nodes // 2)
            for p in range(nodes)
        )
    return jax.shard_map(
        ringed if paired else gathered,
        mesh=mesh,
        in_specs=(
            P(("groups", "wide"), ("mp", "sub")),
            P(("groups", "wide"), ("mp", "sub")),
            P(("mp", "sub"), "wide"),
            P("wide", None, ("mp", "sub")),
            P(None, ("mp", "sub"), "wide"),
            P("groups", None),
            P(),
        ),
        out_specs=P(("groups", "mp", "sub"), "wide"),
        check_vma=False,
    )
```
